512 devices in a mesh: dp: 16 (over z, core), seq: 32 (over y, x).
Axes of the slice: x: 4, y: 8, z: 8, core: 2. Of those that a mesh axis runs over, the one named last changes fastest.
Arguments:
- bytes_in: bfloat16 [16, 4096, 1024], P('dp', 'seq'), may hold values from -6 to 6
- flags: int32 [16, 4096], P('dp', 'seq'), may hold values from 0 to 1, as said below
- enc_gain: bfloat16 [1024], replicated, may hold values from 0.099609375 to 1.8984375
- conv_weight: bfloat16 [4, 1024], replicated, may hold values from -3 to 3
- widen: bfloat16 [1024], replicated, may hold values from -5 to 5
- main_gain: bfloat16 [2048], replicated, may hold values from 0.099609375 to 1.8984375
- gate_weight: bfloat16 [2048, 4096], P(None, 'seq'), may hold values from -0.125 to 0.125
- up_weight: bfloat16 [2048, 4096], P(None, 'seq'), may hold values from -0.125 to 0.125
- down_weight: bfloat16 [4096, 1024], P('seq'), may hold values from -0.09375 to 0.09375
- out_cot: bfloat16 [16, 4096, 1024], P('dp', 'seq'), may hold values from -6 to 6
Outputs:
- bytes_grad: bfloat16 [16, 4096, 1024], P('dp', 'seq')
- gate_grad: float32 [2048, 4096], P(None, 'seq')
- up_grad: float32 [2048, 4096], P(None, 'seq')
- down_grad: float32 [4096, 1024], P('seq')
The draws below stay inside these ranges and needn't reach their ends.
Inputs may be any that keep to these rules, and one draw needn't show every extreme that they name: `flags`: every sequence has exactly 512 ones; every device's 128 bytes hold 1 to 48 of them, one device of every sequence exactly 48; the first byte of every sequence is 1.
All inputs are finite; a program needn't handle non-finite values.
Results may differ from the reference program's by a relative error of at most 0.023.
Values may be sent and summed in bfloat16 or wider, within the bound.
A program may use at most 64 MiB of HBM per device.

```python
import jax
import jax.numpy as jnp
from jax import lax

E = 1024
D = 2048
FF = 4096
KW = 4
BYTE_DEV = 128
CH_DEV = 16
CAP = 48
BYTES = 4096
GROUPS = 512
SEQS = 16
N_SEQ = 32


def flags_of_sequence(key):
    heavy_key, weight_key, order_key = jax.random.split(key, 3)
    shards = jnp.arange(N_SEQ)
    heavy = jax.random.randint(heavy_key, (), 0, N_SEQ)
    shares = jax.random.randint(weight_key, (N_SEQ,), 2, 5)
    shares = jnp.where(shards == heavy, 0, shares)
    spare = CH_DEV * N_SEQ - CAP - (N_SEQ - 1)
    running = jnp.cumsum(shares).astype(jnp.int32)
    edges = spare * running // running[-1]
    before = jnp.concatenate([jnp.zeros((1,), jnp.int32), edges[:-1]])
    counts = jnp.where(shards == heavy, CAP, 1 + edges - before)
    orders = jax.vmap(lambda part_key: jax.random.permutation(part_key, BYTE_DEV))(jax.random.split(order_key, N_SEQ))
    rotated = (orders[0] - orders[0, 0]) % BYTE_DEV
    orders = orders.at[0].set(rotated)
    return (orders < counts[:, None]).astype(jnp.int32).reshape(BYTE_DEV * N_SEQ)


def draw_flags(key, part):
    key = jax.random.fold_in(key, 11)
    return jax.vmap(flags_of_sequence)(jax.random.split(key, SEQS))


def levels(key, dims, cuts, low, top_value):
    def one(position, blocks):
        heights = jax.random.uniform(jax.random.fold_in(jax.random.fold_in(key, 6), position), (blocks,), jnp.float32, low / len(cuts), top_value / len(cuts))
        return jnp.repeat(jnp.exp(heights), dims[position] // blocks).reshape((-1,) + (1,) * (len(dims) - position - 1))

    level = one(*cuts[0])
    for cut in cuts[1:]:
        level = level * one(*cut)
    return level


def normal_values(key, extent, width, bound, cuts=(), kind=jnp.bfloat16):
    array = jax.random.normal(key, extent, jnp.float32) * width
    if len(cuts) > 0:
        array = levels(key, extent, cuts, -0.22, 0.18) * array
    return jnp.clip(array, min=-bound, max=bound).astype(kind)


def setup_inputs(seed: int = 0) -> dict:
    streams_of = jax.random.split(jax.random.key(seed), 11)
    return {
        "bytes_in": normal_values(streams_of[0], (SEQS, BYTES, E), 1.0, 6.0, ((0, 16), (1, 32))),
        "flags": draw_flags(jax.random.fold_in(streams_of[10], 71), 0),
        "enc_gain": jnp.clip(1.0 + 0.18 * jax.random.normal(streams_of[2], (E,), jnp.float32), 0.099609375, 1.8984375).astype(jnp.bfloat16),
        "conv_weight": normal_values(streams_of[3], (KW, E), 0.5, 3.0),
        "widen": normal_values(streams_of[4], (D - E,), 1.0, 5.0),
        "main_gain": jnp.clip(1.0 + 0.18 * jax.random.normal(streams_of[5], (D,), jnp.float32), 0.099609375, 1.8984375).astype(jnp.bfloat16),
        "gate_weight": normal_values(streams_of[6], (D, FF), D ** -0.5, 0.125, ((1, 32),)),
        "up_weight": normal_values(streams_of[7], (D, FF), D ** -0.5, 0.125, ((1, 32),)),
        "down_weight": normal_values(streams_of[8], (FF, E), FF ** -0.5, 0.09375, ((0, 32),)),
        "out_cot": normal_values(streams_of[9], (SEQS, BYTES, E), 1.0, 6.0, ((0, 16), (1, 32))),
    }


EPS = 1e-05

def rms_scale(value, gain):
    return value * lax.rsqrt(lax.optimization_barrier(jnp.mean(value * value, axis=-1, keepdims=True)) + EPS) * gain.astype(jnp.float32)

def encode(value, enc_gain, conv_weight):
    normed = rms_scale(value, enc_gain)
    length = value.shape[0]
    padded = jnp.concatenate([jnp.zeros((KW - 1, value.shape[1]), jnp.float32), normed], 0)
    mixed = conv_weight[0].astype(jnp.float32) * padded[KW - 1:KW - 1 + length]
    for tap in range(1, KW):
        mixed = mixed + conv_weight[tap].astype(jnp.float32) * padded[KW - 1 - tap:KW - 1 - tap + length]
    return value + jax.nn.silu(mixed)

def main_rows(group_in, group_cot, widen, main_gain, gate_w, up_w, down_w):
    count = group_in.shape[0]
    extra = jnp.broadcast_to(widen.astype(jnp.float32)[None, :], (count, widen.shape[0]))
    widened = jnp.concatenate([group_in.astype(jnp.float32), extra], 1)
    inverse = lax.rsqrt(lax.optimization_barrier(jnp.mean(widened * widened, axis=-1, keepdims=True)) + EPS)
    unit = widened * inverse
    gain32 = main_gain.astype(jnp.float32)
    normed = (unit * gain32).astype(jnp.bfloat16)
    gate = jnp.dot(normed, gate_w, preferred_element_type=jnp.float32)
    upval = jnp.dot(normed, up_w, preferred_element_type=jnp.float32)
    sigma = jax.nn.sigmoid(gate)
    swish = gate * sigma
    act = (swish * upval).astype(jnp.bfloat16)
    act_cot = jnp.dot(group_cot, down_w.T, preferred_element_type=jnp.float32)
    gate_cot = (act_cot * upval * sigma * (1.0 + gate * (1.0 - sigma))).astype(jnp.bfloat16)
    up_cot = (act_cot * swish).astype(jnp.bfloat16)
    normed_cot = jnp.dot(gate_cot, gate_w.T, preferred_element_type=jnp.float32)
    normed_cot = normed_cot + jnp.dot(up_cot, up_w.T, preferred_element_type=jnp.float32)
    scaled = normed_cot * gain32
    inner = lax.optimization_barrier(jnp.mean(scaled * unit, axis=-1, keepdims=True))
    part = ((scaled - unit * inner) * inverse)[:, :group_in.shape[1]]
    return (normed, act, gate_cot, up_cot, part)

def reference(bytes_in, flags, enc_gain, conv_weight, widen, main_gain, gate_weight, up_weight, down_weight, out_cot):
    block_width = FF // N_SEQ
    gate_blocks = gate_weight.reshape(D, N_SEQ, block_width).transpose(1, 0, 2)
    up_blocks = up_weight.reshape(D, N_SEQ, block_width).transpose(1, 0, 2)
    down_blocks = down_weight.reshape(N_SEQ, block_width, E)

    def one_sequence(carry, inputs):
        sequence, marks, cotangent = inputs
        value = sequence.astype(jnp.float32)
        full, pullback = jax.vjp(lambda entry: encode(entry, enc_gain, conv_weight), value)
        enc_out = full.astype(jnp.bfloat16)
        group_of = (jnp.cumsum(marks) - 1).astype(jnp.int32)
        mark32 = marks.astype(jnp.float32)[:, None]
        group_in = jax.ops.segment_sum(enc_out.astype(jnp.float32) * mark32, group_of, num_segments=GROUPS).astype(jnp.bfloat16)
        group_cot = jax.ops.segment_sum(cotangent.astype(jnp.float32), group_of, num_segments=GROUPS).astype(jnp.bfloat16)

        def one_block(blocks):
            normed, act, gate_cot, up_cot, part = main_rows(group_in, group_cot, widen, main_gain, blocks[0], blocks[1], blocks[2])
            return (jnp.dot(normed.T, gate_cot, preferred_element_type=jnp.float32), jnp.dot(normed.T, up_cot, preferred_element_type=jnp.float32), jnp.dot(act.T, group_cot, preferred_element_type=jnp.float32), part.astype(jnp.bfloat16))
        gate_part, up_part, down_part, parts = lax.map(one_block, (gate_blocks, up_blocks, down_blocks))
        widen_cot = lax.optimization_barrier(jnp.sum(parts.astype(jnp.float32), 0)).astype(jnp.bfloat16)
        group_total = group_cot.astype(jnp.float32) + widen_cot.astype(jnp.float32)
        enc_cot = cotangent.astype(jnp.float32) + mark32 * group_total[group_of]
        grad = pullback(enc_cot)[0].astype(jnp.bfloat16)
        return ((carry[0] + gate_part, carry[1] + up_part, carry[2] + down_part), grad)
    start = (jnp.zeros((N_SEQ, D, block_width), jnp.float32), jnp.zeros((N_SEQ, D, block_width), jnp.float32), jnp.zeros((N_SEQ, block_width, E), jnp.float32))
    sums, bytes_grad = lax.scan(one_sequence, start, (bytes_in, flags, out_cot))
    gate_grad = sums[0].transpose(1, 0, 2).reshape(D, FF)
    up_grad = sums[1].transpose(1, 0, 2).reshape(D, FF)
    down_grad = sums[2].reshape(FF, E)
    return (bytes_grad, gate_grad, up_grad, down_grad)
```

```python
import jax
import jax.numpy as jnp
from jax import lax
from jax.experimental import pallas as pl
from jax.experimental.pallas import tpu as pltpu
from jax.sharding import PartitionSpec as P

MESH = pl.DeviceIdType.MESH
F32 = jnp.float32
BF16 = jnp.bfloat16

KW = 4
CAP = 48
EPS = 1e-05
LINE = 4
PARTS = 2
CHUNK = 32

Y_ORDER = (0, -1, 1, -2, 2, -3, 3, 4)
X_ORDER = (0, -1, 1, 2)


def dot(left, right):
    return jnp.dot(left, right, preferred_element_type=F32)


def dot_rows(left, right):
    return lax.dot_general(left, right, (((0,), (0,)), ((), ())), preferred_element_type=F32)


def dot_lanes(left, right):
    return lax.dot_general(left, right, (((1,), (1,)), ((), ())), preferred_element_type=F32)


def kernel(
    params,
    x_ref,
    marks_ref,
    gw_ref,
    uw_ref,
    dw_ref,
    oc_ref,
    bg_ref,
    gg_ref,
    ug_ref,
    dg_ref,
    w_all,
    tails,
    tail_b,
    halo,
    lead_out,
    lead_in,
    norm_x,
    inv_x,
    enc_out,
    slope,
    in_all,
    cot_all,
    normed,
    normed_t,
    cot_t,
    inv_all,
    tin_all,
    act_all,
    cots_all,
    back,
    part_all,
    rs_in,
    v_out,
    v_in,
    v_pair,
    v_sib,
    v_all,
    g_out,
    g_own,
    g_in,
    g_x,
    x_opp,
    x_in,
    h_all,
    z_in,
    final,
    ecot,
    g_mix,
    edge,
    send_sems,
    recv_sems,
):
    n_seq = lax.axis_size("seq")
    n_y = n_seq // LINE
    n_z = lax.axis_size("dp") // 2
    dp = lax.axis_index("dp")
    seq = lax.axis_index("seq")
    z, core = dp // 2, dp % 2
    y, x = seq // LINE, seq % LINE
    width = x_ref.shape[1]
    rows = x_ref.shape[0]
    half = width // 2
    piece = half // PARTS
    z_rows = piece // n_z

    def y_dev(step):
        return {"seq": lax.rem(y + step + n_y, n_y) * LINE + x}

    def x_dev(step):
        return {"seq": y * LINE + lax.rem(x + step + LINE, LINE)}

    def z_dev(step):
        return {"dp": lax.rem(z + step + n_z, n_z) * 2 + core}

    sibling = {"dp": z * 2 + 1 - core}
    after = {"seq": lax.rem(seq + 1, n_seq)}
    before = {"seq": lax.rem(seq + n_seq - 1, n_seq)}

    started = []

    def send(source, target, device):
        index = len(started)
        copy = pltpu.make_async_remote_copy(
            src_ref=source,
            dst_ref=target,
            send_sem=send_sems.at[index],
            recv_sem=recv_sems.at[index],
            device_id=device,
            device_id_type=MESH,
        )
        copy.start()
        started.append(copy)
        return copy

    barrier = pltpu.get_barrier_semaphore()
    peers = [y_dev(step) for step in range(1, n_y)]
    peers += [x_dev(step) for step in range(1, LINE)]
    peers += [z_dev(step) for step in range(1, n_z)]
    peers += [sibling, after, before]
    for peer in peers:
        pl.semaphore_signal(barrier, inc=1, device_id=peer, device_id_type=MESH)

    enc_gain = params[0:1, :]
    taps = [params[1 + tap : 2 + tap, :] for tap in range(KW)]
    widen = params[5:6, :]
    gain_head = params[6:7, :]
    tail_vec = widen * params[7:8, :]
    tail_square = jnp.sum(widen * widen, axis=1, keepdims=True)

    w_all[0, :, 0:128] = gw_ref[0:width, :]
    w_all[0, :, 128:256] = uw_ref[0:width, :]
    w_all[0, :, 256:384] = dw_ref[...].astype(F32).T.astype(BF16)

    marks = marks_ref[...].astype(F32)
    upper = (
        lax.broadcasted_iota(jnp.int32, (rows, rows), 0)
        <= lax.broadcasted_iota(jnp.int32, (rows, rows), 1)
    ).astype(F32).astype(BF16)
    running = dot(jnp.broadcast_to(marks, (16, rows)).astype(BF16), upper)
    lead = jnp.where(running == 0.0, 1.0, 0.0).astype(BF16)
    lead_out[...] = dot(lead, oc_ref[...])[0:8]

    pl.semaphore_wait(barrier, len(peers))

    halo_copy = send(x_ref.at[rows - 16 : rows], halo, after)
    lead_copy = send(lead_out, lead_in, before)

    def w_rows(slot, part):
        start = pl.multiple_of(core * half + part * (half // 2), half // 2)
        return w_all.at[slot, pl.ds(start, half // 2)]

    w_right = [None, None]
    w_left = [None, None]
    for part in (0, 1):
        w_right[part] = send(w_rows(0, part), w_rows(1, part), x_dev(1))
        w_left[1 - part] = send(w_rows(0, 1 - part), w_rows(2, 1 - part), x_dev(-1))

    for r in range(0, rows, CHUNK):
        value = x_ref[r : r + CHUNK].astype(F32)
        inverse = lax.rsqrt(jnp.mean(value * value, axis=1, keepdims=True) + EPS)
        inv_x[r : r + CHUNK] = inverse
        norm_x[16 + r : 16 + r + CHUNK] = value * inverse * enc_gain
    halo_copy.wait_recv()
    value = halo[...].astype(F32) * (seq > 0).astype(F32)
    inverse = lax.rsqrt(jnp.mean(value * value, axis=1, keepdims=True) + EPS)
    norm_x[0:16] = value * inverse * enc_gain
    for r in range(0, rows, CHUNK):
        mixed = taps[0] * norm_x[16 + r : 16 + r + CHUNK]
        for tap in range(1, KW):
            mixed = mixed + taps[tap] * norm_x[16 + r - tap : 16 + r - tap + CHUNK]
        sigma = jax.nn.sigmoid(mixed)
        enc_out[r : r + CHUNK] = (x_ref[r : r + CHUNK].astype(F32) + mixed * sigma).astype(BF16)
        slope[r : r + CHUNK] = sigma * (1.0 + mixed * (1.0 - sigma))

    slot_of = running[0:1] - 1.0
    slot_ids = lax.broadcasted_iota(jnp.int32, (CAP, rows), 0).astype(F32)
    member = jnp.where(slot_ids == slot_of, 1.0, 0.0)
    chosen = (member * marks).astype(BF16)
    in_all[0:CAP] = dot(chosen, enc_out[...]).astype(BF16)

    ring = {}

    def pass_on(which, direction, step):
        buffer = (in_all, cot_all)[which]
        here = Y_ORDER.index(-direction * step)
        there = Y_ORDER.index(4 if step == 3 else -direction * (step + 1))
        ring[which, direction, step] = send(
            buffer.at[here * CAP : (here + 1) * CAP],
            buffer.at[there * CAP : (there + 1) * CAP],
            y_dev(direction),
        )

    pass_on(0, 1, 0)
    pass_on(0, -1, 0)

    own_sums = dot(member.astype(BF16), oc_ref[...])
    lead_copy.wait_recv()
    carried = lead_in[0:1] * (seq < n_seq - 1).astype(F32)
    last_slot = jnp.where(slot_ids[:, 0:1] == running[0:1, rows - 1 : rows] - 1.0, 1.0, 0.0)
    cot_all[0:CAP] = (own_sums + last_slot * carried).astype(BF16)
    pass_on(1, 1, 0)
    pass_on(1, -1, 0)

    w_twin = []

    def swap(slot, part):
        w_twin.append(send(w_rows(slot, part), w_rows(slot, part), sibling))

    w_right[0].wait_recv()
    w_far_a = send(w_rows(1, 0), w_rows(3, 0), x_dev(1))
    w_left[1].wait_recv()
    w_far_b = send(w_rows(2, 1), w_rows(3, 1), x_dev(-1))
    swap(1, 0)
    swap(2, 1)

    tail_b[...] = jnp.broadcast_to(tail_vec, (128, width)).T
    tail_gate = jnp.sum(gw_ref[width : 2 * width].astype(F32) * tail_b[...], axis=0, keepdims=True)
    tail_up = jnp.sum(uw_ref[width : 2 * width].astype(F32) * tail_b[...], axis=0, keepdims=True)
    tails[0, :, 0:128] = jnp.broadcast_to(tail_gate, (8, 128))
    tails[0, :, 128:256] = jnp.broadcast_to(tail_up, (8, 128))
    tail_copies = [
        send(tails.at[0], tails.at[1], x_dev(1)),
        send(tails.at[0], tails.at[2], x_dev(-1)),
        send(tails.at[0], tails.at[3], x_dev(2)),
    ]

    for step in (1, 2):
        for which in (0, 1):
            for direction in (1, -1):
                ring[which, direction, step - 1].wait_recv()
                pass_on(which, direction, step)
        if step == 1:
            w_right[1].wait_recv()
            swap(1, 1)
            w_left[0].wait_recv()
            swap(2, 0)
    w_far_a.wait_recv()
    swap(3, 0)
    w_far_b.wait_recv()
    swap(3, 1)
    ring[0, 1, 2].wait_recv()
    pass_on(0, 1, 3)
    ring[1, -1, 2].wait_recv()
    pass_on(1, -1, 3)
    for copy in tail_copies + w_twin:
        copy.wait_recv()

    def forward(first, last):
        for r in range(first, last, CAP):
            head = in_all[r : r + CAP].astype(F32)
            square = jnp.sum(head * head, axis=1, keepdims=True) + tail_square
            inverse = lax.rsqrt(square / (2 * width) + EPS)
            inv_all[r : r + CAP] = inverse
            normed[r : r + CAP] = (head * inverse * gain_head).astype(BF16)

        tin_all[first:last] = jnp.zeros((last - first, 1), F32)

        def block(slot, carry):
            tail = tails[slot, 0:1, :]
            both = dot(normed[first:last], w_all[slot, :, 0:256]) + inv_all[first:last] * tail
            act_cot = dot(cot_all[first:last], w_all[slot, :, 256:384])
            gate, up = both[:, 0:128], both[:, 128:256]
            sigma = jax.nn.sigmoid(gate)
            swish = gate * sigma
            act_all[slot, first:last, :] = (swish * up).astype(BF16)
            gate_cot = (act_cot * up * sigma * (1.0 + gate * (1.0 - sigma))).astype(BF16)
            up_cot = (act_cot * swish).astype(BF16)
            cots_all[slot, first:last, 0:128] = gate_cot
            cots_all[slot, first:last, 128:256] = up_cot
            tin_all[first:last] += jnp.sum(
                gate_cot.astype(F32) * tail[:, 0:128] + up_cot.astype(F32) * tail[:, 128:256],
                axis=1,
                keepdims=True,
            )
            return carry

        lax.fori_loop(0, LINE, block, 0)

    near = 5 * CAP
    total_rows = len(Y_ORDER) * CAP
    forward(0, near)
    ring[0, -1, 2].wait_recv()
    ring[1, 1, 2].wait_recv()
    ring[0, 1, 3].wait_recv()
    ring[1, -1, 3].wait_recv()
    forward(near, total_rows)

    normed_t[...] = normed[...].T
    cot_t[...] = cot_all[...].T

    def product(start, slot):
        start = pl.multiple_of(start, piece)
        wide = dot(normed_t[pl.ds(start, piece), :], cots_all[slot])
        narrow = dot(cot_t[pl.ds(start, piece), :], act_all[slot])
        return wide, narrow

    pair_copies = []
    for part in range(PARTS):

        def theirs(slot, carry, part=part):
            wide, narrow = product((1 - core) * half + part * piece, slot)
            g_out[part, slot, :, 0:256] = wide.astype(BF16)
            g_out[part, slot, :, 256:384] = narrow.astype(BF16)
            return carry

        lax.fori_loop(0, LINE, theirs, 0)
        pair_copies.append(send(g_out.at[part], g_in.at[part], sibling))

    for part in range(PARTS):

        def ours(slot, carry, part=part):
            wide, narrow = product(core * half + part * piece, slot)
            g_own[part, slot, :, 0:256] = wide
            g_own[part, slot, :, 256:384] = narrow
            return carry

        lax.fori_loop(0, LINE, ours, 0)

    def tail_rows(slot, carry):
        row = jnp.sum(cots_all[slot].astype(F32) * inv_all[...], axis=0, keepdims=True)
        v_out[slot] = jnp.broadcast_to(row, (8, 256))
        return carry

    lax.fori_loop(0, LINE, tail_rows, 0)
    v_copies = [
        send(v_out.at[1], v_in.at[0], x_dev(-1)),
        send(v_out.at[2], v_in.at[1], x_dev(1)),
        send(v_out.at[3], v_in.at[2], x_dev(2)),
    ]

    x_first = []

    def x_start(part):
        pair_copies[part].wait_recv()

        def add(slot, carry):
            g_x[part, slot] = (g_own[part, slot] + g_in[part, slot].astype(F32)).astype(BF16)
            return carry

        lax.fori_loop(1, LINE, add, 0)
        mid = piece // 2
        x_first.append(
            (
                send(g_x.at[part, 3, 0:mid], x_opp.at[part, 0], x_dev(1)),
                send(g_x.at[part, 3, mid:piece], x_opp.at[part, 1], x_dev(-1)),
                send(g_x.at[part, 2, mid:piece], x_in.at[part, 0, mid:piece], x_dev(1)),
                send(g_x.at[part, 1, 0:mid], x_in.at[part, 1, 0:mid], x_dev(-1)),
            )
        )

    rs_copies = []

    def backward(first, last):
        def block(slot, carry):
            back[first:last] += dot_lanes(cots_all[slot, first:last], w_all[slot, :, 0:256])
            return carry

        back[first:last] = dot_lanes(cots_all[0, first:last], w_all[0, :, 0:256])
        lax.fori_loop(1, LINE, block, 0)
        for r in range(first, last, CAP):
            inverse = inv_all[r : r + CAP]
            unit = in_all[r : r + CAP].astype(F32) * inverse
            scaled = back[r : r + CAP] * gain_head
            inner = jnp.sum(scaled * unit, axis=1, keepdims=True) + tin_all[r : r + CAP] * inverse
            part_all[r : r + CAP] = (
                (scaled - unit * (inner / (2 * width))) * inverse
            ).astype(BF16)
            step = Y_ORDER[r // CAP]
            if step:
                there = Y_ORDER.index(4 if step == 4 else -step)
                rs_copies.append(
                    send(part_all.at[r : r + CAP], rs_in.at[there], y_dev(step))
                )

    backward(4 * CAP, 8 * CAP)
    x_start(0)
    backward(0, 4 * CAP)
    x_start(1)

    for copy in v_copies:
        copy.wait_recv()
    v_pair[...] = v_out[0] + v_in[0] + v_in[1] + v_in[2]
    v_swap = send(v_pair, v_sib, sibling)

    x_second = []
    mid = piece // 2
    for part in range(PARTS):
        x_first[part][0].wait_recv()
        g_x[part, 2, 0:mid] = (
            g_x[part, 2, 0:mid].astype(F32) + x_opp[part, 0].astype(F32)
        ).astype(BF16)
        second_a = send(g_x.at[part, 2, 0:mid], x_in.at[part, 0, 0:mid], x_dev(1))
        x_first[part][1].wait_recv()
        g_x[part, 1, mid:piece] = (
            g_x[part, 1, mid:piece].astype(F32) + x_opp[part, 1].astype(F32)
        ).astype(BF16)
        second_b = send(g_x.at[part, 1, mid:piece], x_in.at[part, 1, mid:piece], x_dev(-1))
        x_second.append((second_a, second_b))

    v_swap.wait_recv()
    v_all[z] = v_pair[...] + v_sib[...]
    v_spread = [send(v_all.at[z], v_all.at[z], z_dev(step)) for step in range(1, n_z)]

    z_first = []
    for part in range(PARTS):
        for copy in x_first[part][2:] + x_second[part]:
            copy.wait_recv()
        h_all[part] = (
            g_own[part, 0]
            + g_in[part, 0].astype(F32)
            + x_in[part, 0].astype(F32)
            + x_in[part, 1].astype(F32)
        ).astype(BF16)
        copies = []
        for step in range(1, n_z):
            start = pl.multiple_of(lax.rem(z + step, n_z) * z_rows, z_rows)
            copies.append(
                send(h_all.at[part, pl.ds(start, z_rows)], z_in.at[part, step - 1], z_dev(step))
            )
        z_first.append(copies)

    for copy in rs_copies:
        copy.wait_recv()
    widen_cot = part_all[0:CAP].astype(F32)
    for slot in range(1, len(Y_ORDER)):
        widen_cot = widen_cot + rs_in[slot].astype(F32)
    spread = dot_rows(chosen, cot_all[0:CAP]) + dot_rows(chosen, widen_cot.astype(BF16))
    ecot[...] = oc_ref[...].astype(F32) + spread
    for r in range(0, rows, CHUNK):
        g_mix[r : r + CHUNK] = ecot[r : r + CHUNK] * slope[r : r + CHUNK]
    edge_copy = send(g_mix.at[0:8], edge, before)

    z_second = []
    for part in range(PARTS):
        own = pl.multiple_of(z * z_rows, z_rows)
        total = h_all[part, pl.ds(own, z_rows)].astype(F32)
        for step in range(1, n_z):
            z_first[part][step - 1].wait_recv()
            total = total + z_in[part, step - 1].astype(F32)
        start = pl.multiple_of(core * half + part * piece + z * z_rows, z_rows)
        final[pl.ds(start, z_rows)] = total.astype(BF16)
        mine = final.at[pl.ds(start, z_rows)]
        z_second.append([send(mine, mine, z_dev(step)) for step in range(1, n_z)])

    edge_copy.wait_recv()
    g_mix[rows : rows + 8] = edge[...] * (seq < n_seq - 1).astype(F32)
    for r in range(0, rows, CHUNK):
        grad = taps[0] * g_mix[r : r + CHUNK]
        for tap in range(1, KW):
            grad = grad + taps[tap] * g_mix[r + tap : r + tap + CHUNK]
        grad = grad * enc_gain
        value = x_ref[r : r + CHUNK].astype(F32)
        inverse = inv_x[r : r + CHUNK]
        inner = jnp.mean(grad * value, axis=1, keepdims=True) * (inverse * inverse)
        bg_ref[r : r + CHUNK] = (
            ecot[r : r + CHUNK] + (grad - value * inner) * inverse
        ).astype(BF16)

    for copy in v_spread:
        copy.wait_recv()
    v_total = v_all[0]
    for chip in range(1, n_z):
        v_total = v_total + v_all[chip]
    gg_ref[width : 2 * width] = tail_b[...] * v_total[0:1, 0:128]
    ug_ref[width : 2 * width] = tail_b[...] * v_total[0:1, 128:256]

    last_copies = []
    for part in range(PARTS):
        for copy in z_second[part]:
            copy.wait_recv()
        start = pl.multiple_of(core * half + part * piece, piece)
        mine = final.at[pl.ds(start, piece)]
        last_copies.append(send(mine, mine, sibling))
    for copy in last_copies:
        copy.wait_recv()
    gg_ref[0:width] = final[:, 0:128].astype(F32)
    ug_ref[0:width] = final[:, 128:256].astype(F32)
    dg_ref[...] = final[:, 256:384].astype(F32).T

    for copy in started:
        copy.wait_send()


def body(
    bytes_in,
    flags,
    enc_gain,
    conv_weight,
    widen,
    main_gain,
    gate_weight,
    up_weight,
    down_weight,
    out_cot,
):
    rows, width = bytes_in.shape[1:]
    n_y = lax.axis_size("seq") // LINE
    n_z = lax.axis_size("dp") // 2
    assert n_y == len(Y_ORDER)
    piece = width // 2 // PARTS
    groups = n_y * CAP
    params = jnp.concatenate(
        [enc_gain[None], conv_weight, widen[None], main_gain.reshape(2, width)], 0
    ).astype(F32)
    vmem = pl.BlockSpec(memory_space=pltpu.VMEM)
    scratch = [
        ((LINE, width, 384), BF16),
        ((LINE, 8, 256), F32),
        ((width, 128), F32),
        ((16, width), BF16),
        ((8, width), F32),
        ((8, width), F32),
        ((rows + 16, width), F32),
        ((rows, 1), F32),
        ((rows, width), BF16),
        ((rows, width), F32),
        ((groups, width), BF16),
        ((groups, width), BF16),
        ((groups, width), BF16),
        ((width, groups), BF16),
        ((width, groups), BF16),
        ((groups, 1), F32),
        ((groups, 1), F32),
        ((LINE, groups, 128), BF16),
        ((LINE, groups, 256), BF16),
        ((groups, width), F32),
        ((groups, width), BF16),
        ((n_y, CAP, width), BF16),
        ((LINE, 8, 256), F32),
        ((LINE - 1, 8, 256), F32),
        ((8, 256), F32),
        ((8, 256), F32),
        ((n_z, 8, 256), F32),
        ((PARTS, LINE, piece, 384), BF16),
        ((PARTS, LINE, piece, 384), F32),
        ((PARTS, LINE, piece, 384), BF16),
        ((PARTS, LINE, piece, 384), BF16),
        ((PARTS, 2, piece // 2, 384), BF16),
        ((PARTS, 2, piece, 384), BF16),
        ((PARTS, piece, 384), BF16),
        ((PARTS, n_z - 1, piece // n_z, 384), BF16),
        ((width, 384), BF16),
        ((rows, width), F32),
        ((rows + 8, width), F32),
        ((8, width), F32),
    ]
    outs = pl.pallas_call(
        kernel,
        out_shape=(
            jax.ShapeDtypeStruct((rows, width), BF16),
            jax.ShapeDtypeStruct((2 * width, 128), F32),
            jax.ShapeDtypeStruct((2 * width, 128), F32),
            jax.ShapeDtypeStruct((128, width), F32),
        ),
        in_specs=[vmem] * 7,
        out_specs=[vmem] * 4,
        scratch_shapes=[pltpu.VMEM(shape, kind) for shape, kind in scratch]
        + [pltpu.SemaphoreType.DMA((112,)), pltpu.SemaphoreType.DMA((112,))],
        compiler_params=pltpu.CompilerParams(
            collective_id=0, has_side_effects=True, vmem_limit_bytes=48 * 1024 * 1024
        ),
    )(params, bytes_in[0], flags, gate_weight, up_weight, down_weight, out_cot[0])
    return (outs[0][None], outs[1], outs[2], outs[3])


def solution(mesh):
    in_specs = (
        P("dp", "seq", None),
        P("dp", "seq"),
        P(),
        P(),
        P(),
        P(),
        P(None, "seq"),
        P(None, "seq"),
        P("seq", None),
        P("dp", "seq", None),
    )
    out_specs = (P("dp", "seq", None), P(None, "seq"), P(None, "seq"), P("seq", None))
    return jax.shard_map(body, mesh=mesh, in_specs=in_specs, out_specs=out_specs, check_vma=False)
```

```python
import jax
import jax.numpy as jnp
from jax import lax
from jax.experimental import pallas as pl
from jax.experimental.pallas import tpu as pltpu
from jax.sharding import PartitionSpec as P

MESH = pl.DeviceIdType.MESH
F32 = jnp.float32
BF16 = jnp.bfloat16

KW = 4
CAP = 48
EPS = 1e-05
LINE = 4
PARTS = 4
CHUNK = 32

Y_ORDER = (0, -1, 1, -2, 2, -3, 3, 4)
Y_ROW = (0, 48, 96, 144, 192, 256, 304, 352)
NEAR = (0, 240)
FAR = (256, 400)
ROWS = 512
X_ORDER = (0, -1, 1, 2)


def dot(left, right):
    return jnp.dot(left, right, preferred_element_type=F32)


def dot_rows(left, right):
    return lax.dot_general(left, right, (((0,), (0,)), ((), ())), preferred_element_type=F32)


def dot_lanes(left, right):
    return lax.dot_general(left, right, (((1,), (1,)), ((), ())), preferred_element_type=F32)


def as_row(value):
    value = value.astype(F32)
    return jnp.concatenate([value[i : i + 1] for i in range(value.shape[0])], axis=1)


def kernel(
    x_hbm,
    marks_hbm,
    enc_gain_hbm,
    conv_hbm,
    widen_hbm,
    main_gain_hbm,
    gw_hbm,
    uw_hbm,
    dw_hbm,
    oc_hbm,
    bg_ref,
    final,
    tail_b,
    v_ref,
    x_ref,
    marks_ref,
    enc_gain_ref,
    conv_ref,
    widen_ref,
    main_gain_ref,
    gw_tail,
    uw_tail,
    dw_ref,
    oc_ref,
    w_all,
    tails,
    halo,
    lead_out,
    lead_in,
    norm_x,
    inv_x,
    enc_out,
    slope,
    in_all,
    cot_all,
    normed,
    normed_t,
    cot_t,
    inv_all,
    tin_all,
    act_all,
    cots_all,
    back,
    part_all,
    y_in,
    y_relay,
    y_cross,
    y_mid,
    v_out,
    v_in,
    v_pair,
    v_sib,
    v_all,
    g_acc,
    g_out,
    g_in,
    g_x,
    x_opp,
    x_in,
    h_all,
    z_in,
    z_relay,
    z_cross,
    z_mid,
    ecot,
    g_mix,
    edge,
    load_sems,
    send_sems,
    recv_sems,
):
    n_seq = lax.axis_size("seq")
    n_y = n_seq // LINE
    n_z = lax.axis_size("dp") // 2
    dp = lax.axis_index("dp")
    seq = lax.axis_index("seq")
    z, core = dp // 2, dp % 2
    y, x = seq // LINE, seq % LINE
    rows, width = x_ref.shape
    half = width // 2
    piece = half // PARTS
    mid = piece // 2
    z_rows = piece // n_z

    def y_dev(step):
        return {"seq": lax.rem(y + step + n_y, n_y) * LINE + x}

    def x_dev(step):
        return {"seq": y * LINE + lax.rem(x + step + LINE, LINE)}

    def z_dev(step):
        return {"dp": lax.rem(z + step + n_z, n_z) * 2 + core}

    sibling = {"dp": z * 2 + 1 - core}
    after = {"seq": lax.rem(seq + 1, n_seq)}
    before = {"seq": lax.rem(seq + n_seq - 1, n_seq)}

    loads = []

    def load(source, target):
        copy = pltpu.make_async_copy(source, target, load_sems.at[len(loads)])
        copy.start()
        loads.append(copy)
        return copy

    load_marks = load(marks_hbm, marks_ref)
    load_oc = load(oc_hbm, oc_ref)
    load_x = load(x_hbm, x_ref)
    load_gain = load(enc_gain_hbm, enc_gain_ref)
    load_conv = load(conv_hbm, conv_ref)
    load_w = [
        load(dw_hbm, dw_ref),
        load(gw_hbm.at[0:width], w_all.at[0, :, 0:128]),
        load(uw_hbm.at[0:width], w_all.at[0, :, 128:256]),
    ]
    load_tail = [
        load(widen_hbm, widen_ref),
        load(main_gain_hbm, main_gain_ref),
        load(gw_hbm.at[width : 2 * width], gw_tail),
        load(uw_hbm.at[width : 2 * width], uw_tail),
    ]

    started = []

    def send(source, target, device):
        index = len(started)
        copy = pltpu.make_async_remote_copy(
            src_ref=source,
            dst_ref=target,
            send_sem=send_sems.at[index],
            recv_sem=recv_sems.at[index],
            device_id=device,
            device_id_type=MESH,
        )
        copy.start()
        started.append(copy)
        return copy

    barrier = pltpu.get_barrier_semaphore()
    peers = [y_dev(step) for step in (1, -1, 2, -2)]
    peers += [x_dev(step) for step in (1, -1, 2)]
    peers += [z_dev(step) for step in range(1, n_z)]
    peers += [sibling, after, before]
    for peer in peers:
        pl.semaphore_signal(barrier, inc=1, device_id=peer, device_id_type=MESH)

    load_marks.wait()
    marks = marks_ref[...].astype(F32)
    upper = (
        lax.broadcasted_iota(jnp.int32, (rows, rows), 0)
        <= lax.broadcasted_iota(jnp.int32, (rows, rows), 1)
    ).astype(F32).astype(BF16)
    running = dot(jnp.broadcast_to(marks, (16, rows)).astype(BF16), upper)
    lead = jnp.where(running == 0.0, 1.0, 0.0).astype(BF16)
    slot_ids = lax.broadcasted_iota(jnp.int32, (CAP, rows), 0).astype(F32)
    member = jnp.where(slot_ids == running[0:1] - 1.0, 1.0, 0.0)
    chosen = (member * marks).astype(BF16)
    last_slot = jnp.where(slot_ids[:, 0:1] == running[0:1, rows - 1 : rows] - 1.0, 1.0, 0.0)
    load_oc.wait()
    lead_out[...] = dot(lead, oc_ref[...])[0:8]

    pl.semaphore_wait(barrier, len(peers))

    halo_copy = send(x_hbm.at[rows - 16 : rows], halo, after)
    lead_copy = send(lead_out, lead_in, before)
    own_sums = dot(member.astype(BF16), oc_ref[...])

    for copy in load_w:
        copy.wait()
    w_all[0, :, 256:384] = dw_ref[...].astype(F32).T.astype(BF16)

    def w_rows(slot, part):
        start = pl.multiple_of(core * half + part * (half // 2), half // 2)
        return w_all.at[slot, pl.ds(start, half // 2)]

    w_right = [None, None]
    w_left = [None, None]
    for part in (0, 1):
        w_right[part] = send(w_rows(0, part), w_rows(1, part), x_dev(1))
        w_left[1 - part] = send(w_rows(0, 1 - part), w_rows(2, 1 - part), x_dev(-1))

    ring = {}

    def pass_on(which, direction, step):
        buffer = (in_all, cot_all)[which]
        here = Y_ROW[Y_ORDER.index(-direction * step)]
        there = Y_ROW[Y_ORDER.index(4 if step == 3 else -direction * (step + 1))]
        ring[which, direction, step] = send(
            buffer.at[here : here + CAP], buffer.at[there : there + CAP], y_dev(direction)
        )

    lead_copy.wait_recv()
    carried = lead_in[0:1] * (seq < n_seq - 1).astype(F32)
    cot_all[0:CAP] = (own_sums + last_slot * carried).astype(BF16)
    pass_on(1, 1, 0)
    pass_on(1, -1, 0)

    load_gain.wait()
    load_conv.wait()
    load_x.wait()
    enc_gain = as_row(enc_gain_ref[...])
    taps = [conv_ref[tap : tap + 1, :].astype(F32) for tap in range(KW)]
    for r in range(0, rows, CHUNK):
        value = x_ref[r : r + CHUNK].astype(F32)
        inverse = lax.rsqrt(jnp.mean(value * value, axis=1, keepdims=True) + EPS)
        inv_x[r : r + CHUNK] = inverse
        norm_x[16 + r : 16 + r + CHUNK] = value * inverse * enc_gain
    halo_copy.wait_recv()
    value = halo[...].astype(F32) * (seq > 0).astype(F32)
    inverse = lax.rsqrt(jnp.mean(value * value, axis=1, keepdims=True) + EPS)
    norm_x[0:16] = value * inverse * enc_gain
    for r in range(0, rows, CHUNK):
        mixed = taps[0] * norm_x[16 + r : 16 + r + CHUNK]
        for tap in range(1, KW):
            mixed = mixed + taps[tap] * norm_x[16 + r - tap : 16 + r - tap + CHUNK]
        sigma = jax.nn.sigmoid(mixed)
        enc_out[r : r + CHUNK] = (x_ref[r : r + CHUNK].astype(F32) + mixed * sigma).astype(BF16)
        slope[r : r + CHUNK] = sigma * (1.0 + mixed * (1.0 - sigma))
    in_all[0:CAP] = dot(chosen, enc_out[...]).astype(BF16)
    pass_on(0, 1, 0)
    pass_on(0, -1, 0)

    w_twin = []

    def swap(slot, part):
        w_twin.append(send(w_rows(slot, part), w_rows(slot, part), sibling))

    w_right[0].wait_recv()
    w_far_a = send(w_rows(1, 0), w_rows(3, 0), x_dev(1))
    w_left[1].wait_recv()
    w_far_b = send(w_rows(2, 1), w_rows(3, 1), x_dev(-1))
    swap(1, 0)
    swap(2, 1)

    for copy in load_tail:
        copy.wait()
    widen = as_row(widen_ref[...])
    main_gain = as_row(main_gain_ref[...])
    gain_head = main_gain[:, 0:width]
    tail_vec = widen * main_gain[:, width : 2 * width]
    tail_square = jnp.sum(widen * widen, axis=1, keepdims=True)
    tail_b[...] = jnp.broadcast_to(tail_vec, (128, width)).T
    tail_gate = jnp.sum(gw_tail[...].astype(F32) * tail_b[...], axis=0, keepdims=True)
    tail_up = jnp.sum(uw_tail[...].astype(F32) * tail_b[...], axis=0, keepdims=True)
    tails[0, :, 0:128] = jnp.broadcast_to(tail_gate, (8, 128))
    tails[0, :, 128:256] = jnp.broadcast_to(tail_up, (8, 128))
    tail_copies = [
        send(tails.at[0], tails.at[1], x_dev(1)),
        send(tails.at[0], tails.at[2], x_dev(-1)),
        send(tails.at[0], tails.at[3], x_dev(2)),
    ]

    def relay(step):
        for which in (1, 0):
            for direction in (1, -1):
                ring[which, direction, step - 1].wait_recv()
                pass_on(which, direction, step)

    relay(1)
    w_right[1].wait_recv()
    swap(1, 1)
    w_left[0].wait_recv()
    swap(2, 0)
    for first, last in ((NEAR[1], FAR[0]), (FAR[1], ROWS)):
        count = last - first
        normed[first:last] = jnp.zeros((count, width), BF16)
        cot_all[first:last] = jnp.zeros((count, width), BF16)
        inv_all[first:last] = jnp.zeros((count, 1), F32)
        act_all[:, first:last] = jnp.zeros((LINE, count, 128), BF16)
        cots_all[:, first:last] = jnp.zeros((LINE, count, 256), BF16)
    relay(2)

    def normalise(first, last):
        for r in range(first, last, CAP):
            head = in_all[r : r + CAP].astype(F32)
            square = jnp.sum(head * head, axis=1, keepdims=True) + tail_square
            inverse = lax.rsqrt(square / (2 * width) + EPS)
            inv_all[r : r + CAP] = inverse
            normed[r : r + CAP] = (head * inverse * gain_head).astype(BF16)
        tin_all[first:last] = jnp.zeros((last - first, 1), F32)

    def forward(first, last, low, high):
        def block(slot, carry):
            tail = tails[slot, 0:1, :]
            both = dot(normed[first:last], w_all[slot, :, 0:256]) + inv_all[first:last] * tail
            act_cot = dot(cot_all[first:last], w_all[slot, :, 256:384])
            gate, up = both[:, 0:128], both[:, 128:256]
            sigma = jax.nn.sigmoid(gate)
            swish = gate * sigma
            act_all[slot, first:last, :] = (swish * up).astype(BF16)
            gate_cot = (act_cot * up * sigma * (1.0 + gate * (1.0 - sigma))).astype(BF16)
            up_cot = (act_cot * swish).astype(BF16)
            cots_all[slot, first:last, 0:128] = gate_cot
            cots_all[slot, first:last, 128:256] = up_cot
            tin_all[first:last] += jnp.sum(
                gate_cot.astype(F32) * tail[:, 0:128] + up_cot.astype(F32) * tail[:, 128:256],
                axis=1,
                keepdims=True,
            )
            return carry

        lax.fori_loop(low, high, block, 0)

    def backward(first, last):
        def block(slot, carry):
            back[first:last] += dot_lanes(cots_all[slot, first:last], w_all[slot, :, 0:256])
            return carry

        back[first:last] = dot_lanes(cots_all[0, first:last], w_all[0, :, 0:256])
        lax.fori_loop(1, LINE, block, 0)
        for r in range(first, last, CAP):
            inverse = inv_all[r : r + CAP]
            unit = in_all[r : r + CAP].astype(F32) * inverse
            scaled = back[r : r + CAP] * gain_head
            inner = jnp.sum(scaled * unit, axis=1, keepdims=True) + tin_all[r : r + CAP] * inverse
            part_all[r : r + CAP] = (
                (scaled - unit * (inner / (2 * width))) * inverse
            ).astype(BF16)

    def part_of(step, lanes=slice(None)):
        row = Y_ROW[Y_ORDER.index(step)]
        return part_all.at[row : row + CAP, lanes]

    normalise(*NEAR)
    for copy in tail_copies + w_twin:
        copy.wait_recv()
    forward(*NEAR, 0, LINE - 1)
    ring[1, -1, 2].wait_recv()
    pass_on(1, -1, 3)
    ring[0, 1, 2].wait_recv()
    pass_on(0, 1, 3)
    first_twins = len(w_twin)
    w_far_a.wait_recv()
    swap(3, 0)
    w_far_b.wait_recv()
    swap(3, 1)
    normed_t[0] = normed[0 : FAR[0]].T
    cot_t[0] = cot_all[0 : FAR[0]].T
    for copy in w_twin[first_twins:]:
        copy.wait_recv()
    forward(*NEAR, LINE - 1, LINE)

    def near_product(slot, carry):
        g_acc[slot, :, 0:256] = dot(normed_t[0], cots_all[slot, 0 : FAR[0]])
        g_acc[slot, :, 256:384] = dot(cot_t[0], act_all[slot, 0 : FAR[0]])
        return carry

    lax.fori_loop(0, LINE, near_product, 0)
    backward(*NEAR)
    y_first = [
        send(part_of(1), y_in.at[0], y_dev(1)),
        send(part_of(-1), y_in.at[1], y_dev(-1)),
    ]

    ring[1, 1, 2].wait_recv()
    ring[0, -1, 2].wait_recv()
    ring[1, -1, 3].wait_recv()
    ring[0, 1, 3].wait_recv()
    normalise(*FAR)
    forward(*FAR, 0, LINE)
    normed_t[1] = normed[FAR[0] : ROWS].T
    cot_t[1] = cot_all[FAR[0] : ROWS].T

    def far_product(start, slot):
        wide = dot(normed_t[1, pl.ds(start, half)], cots_all[slot, FAR[0] : ROWS])
        narrow = dot(cot_t[1, pl.ds(start, half)], act_all[slot, FAR[0] : ROWS])
        return (
            wide + g_acc[slot, pl.ds(start, half), 0:256],
            narrow + g_acc[slot, pl.ds(start, half), 256:384],
        )

    their_start = pl.multiple_of((1 - core) * half, half)
    our_start = pl.multiple_of(core * half, half)

    def theirs(slot, carry):
        wide, narrow = far_product(their_start, slot)
        g_out[slot, :, 0:256] = wide.astype(BF16)
        g_out[slot, :, 256:384] = narrow.astype(BF16)
        return carry

    lax.fori_loop(0, LINE, theirs, 0)

    def cut(part):
        return slice(part * piece, (part + 1) * piece)

    pair_copies = [
        send(g_out.at[:, cut(part)], g_in.at[:, cut(part)], sibling) for part in range(PARTS)
    ]

    def ours(slot, carry):
        wide, narrow = far_product(our_start, slot)
        g_acc[slot, pl.ds(our_start, half), 0:256] = wide
        g_acc[slot, pl.ds(our_start, half), 256:384] = narrow
        return carry

    lax.fori_loop(0, LINE, ours, 0)

    x_first, x_second, z_first, z_second, z_near, z_far, last_copies = ({} for _ in range(7))

    def own_rows(part):
        return pl.ds(pl.multiple_of(core * half + part * piece, piece), piece)

    def x_start(part):
        pair_copies[part].wait_recv()

        def add(slot, carry):
            total = g_acc[slot, own_rows(part)] + g_in[slot, cut(part)].astype(F32)
            g_x[slot, cut(part)] = total.astype(BF16)
            return carry

        lax.fori_loop(1, LINE, add, 0)
        low = slice(part * piece, part * piece + mid)
        high = slice(part * piece + mid, (part + 1) * piece)
        x_first[part] = (
            send(g_x.at[3, low], x_opp.at[part, 0], x_dev(1)),
            send(g_x.at[3, high], x_opp.at[part, 1], x_dev(-1)),
            send(g_x.at[2, high], x_in.at[0, high], x_dev(1)),
            send(g_x.at[1, low], x_in.at[1, low], x_dev(-1)),
        )

    def x_relay(part):
        low = slice(part * piece, part * piece + mid)
        high = slice(part * piece + mid, (part + 1) * piece)
        x_first[part][0].wait_recv()
        g_x[2, low] = (g_x[2, low].astype(F32) + x_opp[part, 0].astype(F32)).astype(BF16)
        right = send(g_x.at[2, low], x_in.at[0, low], x_dev(1))
        x_first[part][1].wait_recv()
        g_x[1, high] = (g_x[1, high].astype(F32) + x_opp[part, 1].astype(F32)).astype(BF16)
        left = send(g_x.at[1, high], x_in.at[1, high], x_dev(-1))
        x_second[part] = (right, left)

    def z_cut(part, step):
        start = part * piece + lax.rem(z + step + n_z, n_z) * z_rows
        return pl.ds(pl.multiple_of(start, z_rows), z_rows)

    def z_start(part):
        for copy in x_first[part][2:] + x_second[part]:
            copy.wait_recv()
        h_all[cut(part)] = (
            g_acc[0, own_rows(part)]
            + g_in[0, cut(part)].astype(F32)
            + x_in[0, cut(part)].astype(F32)
            + x_in[1, cut(part)].astype(F32)
        ).astype(BF16)
        way = 1 if part % 2 == 0 else -1
        z_first[part] = (
            send(h_all.at[z_cut(part, 3)], z_relay.at[part, 0], z_dev(1)),
            send(h_all.at[z_cut(part, -3)], z_relay.at[part, 1], z_dev(-1)),
            send(h_all.at[z_cut(part, 4)], z_cross.at[part], z_dev(2 * way)),
            send(h_all.at[z_cut(part, 1)], z_in.at[part, 0], z_dev(1)),
            send(h_all.at[z_cut(part, -1)], z_in.at[part, 1], z_dev(-1)),
        )

    def z_join(part):
        for copy in z_first[part][:3]:
            copy.wait_recv()
        copies = []
        for side, step in ((0, 2), (1, -2)):
            total = h_all[z_cut(part, step)].astype(F32) + z_relay[part, side].astype(F32)
            if side == part % 2:
                total = total + z_cross[part].astype(F32)
            z_mid[part, side] = total.astype(BF16)
            copies.append(send(z_mid.at[part, side], z_in.at[part, 2 + side], z_dev(step)))
        z_second[part] = copies

    def z_final(part, step):
        start = core * half + part * piece + lax.rem(z + step + n_z, n_z) * z_rows
        return pl.ds(pl.multiple_of(start, z_rows), z_rows)

    def z_sum(part):
        for copy in z_first[part][3:] + tuple(z_second[part]):
            copy.wait_recv()
        total = h_all[z_cut(part, 0)].astype(F32)
        for index in range(4):
            total = total + z_in[part, index].astype(F32)
        final[z_final(part, 0)] = total.astype(BF16)
        mine = final.at[z_final(part, 0)]
        z_near[part] = [send(mine, mine, z_dev(step)) for step in (2, -2, 1, -1)]

    def z_spread(part):
        copies = []
        for side, step in ((0, 1), (1, -1)):
            z_near[part][side].wait_recv()
            theirs = final.at[z_final(part, -2 * step)]
            copies.append(send(theirs, theirs, z_dev(step)))
            if side == part % 2:
                copies.append(send(theirs, theirs, z_dev(2 * step)))
        z_far[part] = copies

    def z_end(part):
        for copy in z_near[part][2:] + z_far[part]:
            copy.wait_recv()
        mine = final.at[own_rows(part)]
        last_copies[part] = send(mine, mine, sibling)

    x_start(0)
    x_start(1)
    backward(*FAR)
    y_relays = [
        send(part_of(3), y_relay.at[0], y_dev(1)),
        send(part_of(-3), y_relay.at[1], y_dev(-1)),
        send(part_of(4, slice(0, half)), y_cross.at[0], y_dev(2)),
        send(part_of(4, slice(half, width)), y_cross.at[1], y_dev(-2)),
    ]
    x_relay(0)
    x_start(2)

    def tail_rows(slot, carry):
        row = jnp.sum(cots_all[slot].astype(F32) * inv_all[...], axis=0, keepdims=True)
        v_out[slot] = jnp.broadcast_to(row, (8, 256))
        return carry

    lax.fori_loop(0, LINE, tail_rows, 0)
    v_copies = [
        send(v_out.at[1], v_in.at[0], x_dev(-1)),
        send(v_out.at[2], v_in.at[1], x_dev(1)),
        send(v_out.at[3], v_in.at[2], x_dev(2)),
    ]

    z_start(0)
    x_relay(1)
    x_start(3)

    for copy in y_relays:
        copy.wait_recv()
    for side, step in ((0, 2), (1, -2)):
        row = Y_ROW[Y_ORDER.index(step)]
        total = part_all[row : row + CAP].astype(F32) + y_relay[side].astype(F32)
        cross = y_cross[side].astype(F32)
        lanes = slice(side * half, (side + 1) * half)
        other = slice((1 - side) * half, (2 - side) * half)
        y_mid[side, :, lanes] = (total[:, lanes] + cross).astype(BF16)
        y_mid[side, :, other] = total[:, other].astype(BF16)
        y_first.append(send(y_mid.at[side], y_in.at[2 + side], y_dev(step)))

    z_join(0)
    z_start(1)
    x_relay(2)

    for copy in v_copies:
        copy.wait_recv()
    v_pair[...] = v_out[0] + v_in[0] + v_in[1] + v_in[2]
    v_swap = send(v_pair, v_sib, sibling)

    z_sum(0)
    z_join(1)
    z_start(2)
    x_relay(3)

    v_swap.wait_recv()
    v_all[z] = v_pair[...] + v_sib[...]
    v_spread = [send(v_all.at[z], v_all.at[z], z_dev(step)) for step in range(1, n_z)]

    z_spread(0)
    z_sum(1)
    z_join(2)
    z_start(3)

    z_end(0)
    z_spread(1)
    z_sum(2)
    z_join(3)

    for copy in y_first:
        copy.wait_recv()
    widen_cot = part_all[0:CAP].astype(F32)
    for index in range(4):
        widen_cot = widen_cot + y_in[index].astype(F32)
    spread = dot_rows(chosen, cot_all[0:CAP]) + dot_rows(chosen, widen_cot.astype(BF16))
    ecot[...] = oc_ref[...].astype(F32) + spread
    for r in range(0, rows, CHUNK):
        g_mix[r : r + CHUNK] = ecot[r : r + CHUNK] * slope[r : r + CHUNK]
    edge_copy = send(g_mix.at[0:8], edge, before)

    z_end(1)
    z_spread(2)
    z_sum(3)

    z_end(2)
    z_spread(3)

    edge_copy.wait_recv()
    g_mix[rows : rows + 8] = edge[...] * (seq < n_seq - 1).astype(F32)
    for r in range(0, rows, CHUNK):
        grad = taps[0] * g_mix[r : r + CHUNK]
        for tap in range(1, KW):
            grad = grad + taps[tap] * g_mix[r + tap : r + tap + CHUNK]
        grad = grad * enc_gain
        value = x_ref[r : r + CHUNK].astype(F32)
        inverse = inv_x[r : r + CHUNK]
        inner = jnp.mean(grad * value, axis=1, keepdims=True) * (inverse * inverse)
        bg_ref[r : r + CHUNK] = (
            ecot[r : r + CHUNK] + (grad - value * inner) * inverse
        ).astype(BF16)

    for copy in v_spread:
        copy.wait_recv()
    v_total = v_all[0]
    for chip in range(1, n_z):
        v_total = v_total + v_all[chip]
    v_ref[...] = v_total

    z_end(3)
    for part in range(PARTS):
        last_copies[part].wait_recv()
    for copy in started:
        copy.wait_send()


def finish(
    bg, final, tail_b, v_ref, bg_out, gg_out, ug_out, dg_out, gg, ug, dg, sems
):
    width = final.shape[0]
    copies = []

    def store(source, target):
        copy = pltpu.make_async_copy(source, target, sems.at[len(copies)])
        copy.start()
        copies.append(copy)

    store(bg, bg_out)
    head, tail = slice(0, width), slice(width, 2 * width)
    gg[head] = final[:, 0:128].astype(F32)
    store(gg.at[head], gg_out.at[head])
    ug[head] = final[:, 128:256].astype(F32)
    store(ug.at[head], ug_out.at[head])
    gg[tail] = tail_b[...] * v_ref[0:1, 0:128]
    store(gg.at[tail], gg_out.at[tail])
    ug[tail] = tail_b[...] * v_ref[0:1, 128:256]
    store(ug.at[tail], ug_out.at[tail])
    dg[...] = final[:, 256:384].astype(F32).T
    store(dg, dg_out)
    for copy in copies:
        copy.wait()


def body(
    bytes_in,
    flags,
    enc_gain,
    conv_weight,
    widen,
    main_gain,
    gate_weight,
    up_weight,
    down_weight,
    out_cot,
):
    rows, width = bytes_in.shape[1:]
    n_y = lax.axis_size("seq") // LINE
    n_z = lax.axis_size("dp") // 2
    assert n_y == len(Y_ORDER)
    half = width // 2
    piece = half // PARTS
    z_rows = piece // n_z
    vmem = pl.BlockSpec(memory_space=pltpu.VMEM)
    hbm = pl.BlockSpec(memory_space=pltpu.HBM)
    scratch = [
        ((rows, width), BF16),
        ((1, rows), jnp.int32),
        ((8, width // 8), BF16),
        ((KW, width), BF16),
        ((8, width // 8), BF16),
        ((16, width // 8), BF16),
        ((width, 128), BF16),
        ((width, 128), BF16),
        ((128, width), BF16),
        ((rows, width), BF16),
        ((LINE, width, 384), BF16),
        ((LINE, 8, 256), F32),
        ((16, width), BF16),
        ((8, width), F32),
        ((8, width), F32),
        ((rows + 16, width), F32),
        ((rows, 1), F32),
        ((rows, width), BF16),
        ((rows, width), F32),
        ((ROWS, width), BF16),
        ((ROWS, width), BF16),
        ((ROWS, width), BF16),
        ((2, width, ROWS // 2), BF16),
        ((2, width, ROWS // 2), BF16),
        ((ROWS, 1), F32),
        ((ROWS, 1), F32),
        ((LINE, ROWS, 128), BF16),
        ((LINE, ROWS, 256), BF16),
        ((ROWS, width), F32),
        ((ROWS, width), BF16),
        ((4, CAP, width), BF16),
        ((2, CAP, width), BF16),
        ((2, CAP, half), BF16),
        ((2, CAP, width), BF16),
        ((LINE, 8, 256), F32),
        ((LINE - 1, 8, 256), F32),
        ((8, 256), F32),
        ((8, 256), F32),
        ((n_z, 8, 256), F32),
        ((LINE, width, 384), F32),
        ((LINE, half, 384), BF16),
        ((LINE, half, 384), BF16),
        ((LINE, half, 384), BF16),
        ((PARTS, 2, piece // 2, 384), BF16),
        ((2, half, 384), BF16),
        ((half, 384), BF16),
        ((PARTS, 4, z_rows, 384), BF16),
        ((PARTS, 2, z_rows, 384), BF16),
        ((PARTS, z_rows, 384), BF16),
        ((PARTS, 2, z_rows, 384), BF16),
        ((rows, width), F32),
        ((rows + 8, width), F32),
        ((8, width), F32),
    ]
    sums = pl.pallas_call(
        kernel,
        out_shape=(
            jax.ShapeDtypeStruct((rows, width), BF16),
            jax.ShapeDtypeStruct((width, 384), BF16),
            jax.ShapeDtypeStruct((width, 128), F32),
            jax.ShapeDtypeStruct((8, 256), F32),
        ),
        in_specs=[hbm] * 10,
        out_specs=[vmem] * 4,
        scratch_shapes=[pltpu.VMEM(shape, kind) for shape, kind in scratch]
        + [
            pltpu.SemaphoreType.DMA((12,)),
            pltpu.SemaphoreType.DMA((144,)),
            pltpu.SemaphoreType.DMA((144,)),
        ],
        compiler_params=pltpu.CompilerParams(
            collective_id=0, has_side_effects=True, vmem_limit_bytes=50 * 1024 * 1024
        ),
    )(
        bytes_in[0],
        flags,
        enc_gain.reshape(8, width // 8),
        conv_weight,
        widen.reshape(8, width // 8),
        main_gain.reshape(16, width // 8),
        gate_weight,
        up_weight,
        down_weight,
        out_cot[0],
    )
    outs = pl.pallas_call(
        finish,
        out_shape=(
            jax.ShapeDtypeStruct((rows, width), BF16),
            jax.ShapeDtypeStruct((2 * width, 128), F32),
            jax.ShapeDtypeStruct((2 * width, 128), F32),
            jax.ShapeDtypeStruct((128, width), F32),
        ),
        in_specs=[vmem] * 4,
        out_specs=[hbm] * 4,
        scratch_shapes=[
            pltpu.VMEM((2 * width, 128), F32),
            pltpu.VMEM((2 * width, 128), F32),
            pltpu.VMEM((128, width), F32),
            pltpu.SemaphoreType.DMA((6,)),
        ],
        compiler_params=pltpu.CompilerParams(vmem_limit_bytes=8 * 1024 * 1024),
    )(*sums)
    return (outs[0][None], outs[1], outs[2], outs[3])


def solution(mesh):
    in_specs = (
        P("dp", "seq", None),
        P("dp", "seq"),
        P(),
        P(),
        P(),
        P(),
        P(None, "seq"),
        P(None, "seq"),
        P("seq", None),
        P("dp", "seq", None),
    )
    out_specs = (P("dp", "seq", None), P(None, "seq"), P(None, "seq"), P("seq", None))
    return jax.shard_map(body, mesh=mesh, in_specs=in_specs, out_specs=out_specs, check_vma=False)
```

```python
import jax
import jax.numpy as jnp
from jax import lax
from jax.experimental import pallas as pl
from jax.experimental.pallas import tpu as pltpu
from jax.sharding import PartitionSpec as P

MESH = pl.DeviceIdType.MESH
F32 = jnp.float32
BF16 = jnp.bfloat16

KW = 4
CAP = 48
EPS = 1e-05
LINE = 4
PIECES = (0, 256, 384, 512)
PARTS = len(PIECES) - 1
CHUNK = 32

Y_ORDER = (0, -1, 1, -2, 2, -3, 3, 4)
Y_ROW = (0, 48, 96, 144, 192, 256, 304, 352)
NEAR = (0, 240)
FAR = (256, 400)
ROWS = 512
X_ORDER = (0, -1, 1, 2)


def dot(left, right):
    return jnp.dot(left, right, preferred_element_type=F32)


def dot_rows(left, right):
    return lax.dot_general(left, right, (((0,), (0,)), ((), ())), preferred_element_type=F32)


def dot_lanes(left, right):
    return lax.dot_general(left, right, (((1,), (1,)), ((), ())), preferred_element_type=F32)


def as_row(value):
    value = value.astype(F32)
    return jnp.concatenate([value[i : i + 1] for i in range(value.shape[0])], axis=1)


def kernel(
    x_hbm,
    marks_hbm,
    enc_gain_hbm,
    conv_hbm,
    widen_hbm,
    main_gain_hbm,
    gw_hbm,
    uw_hbm,
    dw_hbm,
    oc_hbm,
    bg_hbm,
    final_hbm,
    tail_hbm,
    v_hbm,
    bg_ref,
    final,
    tail_b,
    v_ref,
    x_ref,
    marks_ref,
    enc_gain_ref,
    conv_ref,
    widen_ref,
    main_gain_ref,
    gw_tail,
    uw_tail,
    dw_ref,
    oc_ref,
    w_all,
    tails,
    halo,
    lead_out,
    lead_in,
    norm_x,
    inv_x,
    enc_out,
    slope,
    in_all,
    cot_all,
    normed,
    normed_t,
    cot_t,
    inv_all,
    tin_all,
    act_all,
    cots_all,
    back,
    part_all,
    y_in,
    v_out,
    v_in,
    v_pair,
    v_sib,
    v_all,
    g_acc,
    g_out,
    g_in,
    g_x,
    x_opp,
    x_in,
    h_all,
    z_in,
    ecot,
    g_mix,
    edge,
    load_sems,
    store_sems,
    send_sems,
    recv_sems,
):
    n_seq = lax.axis_size("seq")
    n_y = n_seq // LINE
    n_z = lax.axis_size("dp") // 2
    dp = lax.axis_index("dp")
    seq = lax.axis_index("seq")
    z, core = dp // 2, dp % 2
    y, x = seq // LINE, seq % LINE
    rows, width = x_ref.shape
    half = width // 2

    def y_dev(step):
        return {"seq": lax.rem(y + step + n_y, n_y) * LINE + x}

    def x_dev(step):
        return {"seq": y * LINE + lax.rem(x + step + LINE, LINE)}

    def z_dev(step):
        return {"dp": lax.rem(z + step + n_z, n_z) * 2 + core}

    sibling = {"dp": z * 2 + 1 - core}
    after = {"seq": lax.rem(seq + 1, n_seq)}
    before = {"seq": lax.rem(seq + n_seq - 1, n_seq)}

    loads = []
    stores = []

    def load(source, target):
        copy = pltpu.make_async_copy(source, target, load_sems.at[len(loads)])
        copy.start()
        loads.append(copy)
        return copy

    def store(source, target):
        copy = pltpu.make_async_copy(source, target, store_sems.at[len(stores)])
        copy.start()
        stores.append(copy)

    load_marks = load(marks_hbm, marks_ref)
    load_oc = load(oc_hbm, oc_ref)

    started = []

    def send(source, target, device):
        index = len(started)
        copy = pltpu.make_async_remote_copy(
            src_ref=source,
            dst_ref=target,
            send_sem=send_sems.at[index],
            recv_sem=recv_sems.at[index],
            device_id=device,
            device_id_type=MESH,
        )
        copy.start()
        started.append(copy)
        return copy

    barrier = pltpu.get_barrier_semaphore()
    peers = [y_dev(step) for step in range(1, n_y)]
    peers += [x_dev(step) for step in (1, -1, 2)]
    peers += [z_dev(step) for step in range(1, n_z)]
    peers += [sibling, after, before]
    for peer in peers:
        pl.semaphore_signal(barrier, inc=1, device_id=peer, device_id_type=MESH)

    load_x = load(x_hbm, x_ref)
    load_gain = load(enc_gain_hbm, enc_gain_ref)
    load_conv = load(conv_hbm, conv_ref)
    load_w = [
        load(dw_hbm, dw_ref),
        load(gw_hbm.at[0:width], w_all.at[0, :, 0:128]),
        load(uw_hbm.at[0:width], w_all.at[0, :, 128:256]),
    ]
    load_tail = [
        load(widen_hbm, widen_ref),
        load(main_gain_hbm, main_gain_ref),
        load(gw_hbm.at[width : 2 * width], gw_tail),
        load(uw_hbm.at[width : 2 * width], uw_tail),
    ]

    load_marks.wait()
    marks = marks_ref[...].astype(F32)
    upper = (
        lax.broadcasted_iota(jnp.int32, (rows, rows), 0)
        <= lax.broadcasted_iota(jnp.int32, (rows, rows), 1)
    ).astype(F32).astype(BF16)
    running = dot(jnp.broadcast_to(marks, (16, rows)).astype(BF16), upper)
    lead = jnp.where(running == 0.0, 1.0, 0.0).astype(BF16)
    slot_ids = lax.broadcasted_iota(jnp.int32, (CAP, rows), 0).astype(F32)
    member = jnp.where(slot_ids == running[0:1] - 1.0, 1.0, 0.0)
    chosen = (member * marks).astype(BF16)
    last_slot = jnp.where(slot_ids[:, 0:1] == running[0:1, rows - 1 : rows] - 1.0, 1.0, 0.0)
    load_oc.wait()
    lead_out[...] = dot(lead, oc_ref[...])[0:8]

    pl.semaphore_wait(barrier, len(peers))

    halo_copy = send(x_hbm.at[rows - 16 : rows], halo, after)
    lead_copy = send(lead_out, lead_in, before)
    own_sums = dot(member.astype(BF16), oc_ref[...])

    for copy in load_w:
        copy.wait()
    w_all[0, :, 256:384] = dw_ref[...].astype(F32).T.astype(BF16)

    def w_rows(slot, part):
        start = pl.multiple_of(core * half + part * (half // 2), half // 2)
        return w_all.at[slot, pl.ds(start, half // 2)]

    w_right = [None, None]
    w_left = [None, None]
    for part in (0, 1):
        w_right[part] = send(w_rows(0, part), w_rows(1, part), x_dev(1))
        w_left[1 - part] = send(w_rows(0, 1 - part), w_rows(2, 1 - part), x_dev(-1))

    ring = {}

    def pass_on(which, direction, step):
        buffer = (in_all, cot_all)[which]
        here = Y_ROW[Y_ORDER.index(-direction * step)]
        there = Y_ROW[Y_ORDER.index(4 if step == 3 else -direction * (step + 1))]
        ring[which, direction, step] = send(
            buffer.at[here : here + CAP], buffer.at[there : there + CAP], y_dev(direction)
        )

    lead_copy.wait_recv()
    carried = lead_in[0:1] * (seq < n_seq - 1).astype(F32)
    cot_all[0:CAP] = (own_sums + last_slot * carried).astype(BF16)
    pass_on(1, 1, 0)
    pass_on(1, -1, 0)

    load_gain.wait()
    load_conv.wait()
    load_x.wait()
    enc_gain = as_row(enc_gain_ref[...])
    taps = [conv_ref[tap : tap + 1, :].astype(F32) for tap in range(KW)]
    for r in range(0, rows, CHUNK):
        value = x_ref[r : r + CHUNK].astype(F32)
        inverse = lax.rsqrt(jnp.mean(value * value, axis=1, keepdims=True) + EPS)
        inv_x[r : r + CHUNK] = inverse
        norm_x[16 + r : 16 + r + CHUNK] = value * inverse * enc_gain
    halo_copy.wait_recv()
    value = halo[...].astype(F32) * (seq > 0).astype(F32)
    inverse = lax.rsqrt(jnp.mean(value * value, axis=1, keepdims=True) + EPS)
    norm_x[0:16] = value * inverse * enc_gain
    for r in range(0, rows, CHUNK):
        mixed = taps[0] * norm_x[16 + r : 16 + r + CHUNK]
        for tap in range(1, KW):
            mixed = mixed + taps[tap] * norm_x[16 + r - tap : 16 + r - tap + CHUNK]
        sigma = jax.nn.sigmoid(mixed)
        enc_out[r : r + CHUNK] = (x_ref[r : r + CHUNK].astype(F32) + mixed * sigma).astype(BF16)
        slope[r : r + CHUNK] = sigma * (1.0 + mixed * (1.0 - sigma))
    in_all[0:CAP] = dot(chosen, enc_out[...]).astype(BF16)
    pass_on(0, 1, 0)
    pass_on(0, -1, 0)

    w_twin = []

    def swap(slot, part):
        w_twin.append(send(w_rows(slot, part), w_rows(slot, part), sibling))

    w_right[0].wait_recv()
    w_far_a = send(w_rows(1, 0), w_rows(3, 0), x_dev(1))
    w_left[1].wait_recv()
    w_far_b = send(w_rows(2, 1), w_rows(3, 1), x_dev(-1))
    swap(1, 0)
    swap(2, 1)

    for copy in load_tail:
        copy.wait()
    widen = as_row(widen_ref[...])
    main_gain = as_row(main_gain_ref[...])
    gain_head = main_gain[:, 0:width]
    tail_vec = widen * main_gain[:, width : 2 * width]
    tail_square = jnp.sum(widen * widen, axis=1, keepdims=True)
    tail_b[...] = jnp.broadcast_to(tail_vec, (128, width)).T
    store(tail_b, tail_hbm)
    tail_gate = jnp.sum(gw_tail[...].astype(F32) * tail_b[...], axis=0, keepdims=True)
    tail_up = jnp.sum(uw_tail[...].astype(F32) * tail_b[...], axis=0, keepdims=True)
    tails[0, :, 0:128] = jnp.broadcast_to(tail_gate, (8, 128))
    tails[0, :, 128:256] = jnp.broadcast_to(tail_up, (8, 128))
    tail_copies = [
        send(tails.at[0], tails.at[1], x_dev(1)),
        send(tails.at[0], tails.at[2], x_dev(-1)),
        send(tails.at[0], tails.at[3], x_dev(2)),
    ]

    def relay(step):
        for which in (1, 0):
            for direction in (1, -1):
                ring[which, direction, step - 1].wait_recv()
                pass_on(which, direction, step)

    relay(1)
    w_right[1].wait_recv()
    swap(1, 1)
    w_left[0].wait_recv()
    swap(2, 0)
    for first, last in ((NEAR[1], FAR[0]), (FAR[1], ROWS)):
        count = last - first
        normed[first:last] = jnp.zeros((count, width), BF16)
        cot_all[first:last] = jnp.zeros((count, width), BF16)
        inv_all[first:last] = jnp.zeros((count, 1), F32)
        act_all[:, first:last] = jnp.zeros((LINE, count, 128), BF16)
        cots_all[:, first:last] = jnp.zeros((LINE, count, 256), BF16)
    relay(2)

    def normalise(first, last):
        for r in range(first, last, CAP):
            head = in_all[r : r + CAP].astype(F32)
            square = jnp.sum(head * head, axis=1, keepdims=True) + tail_square
            inverse = lax.rsqrt(square / (2 * width) + EPS)
            inv_all[r : r + CAP] = inverse
            normed[r : r + CAP] = (head * inverse * gain_head).astype(BF16)
        tin_all[first:last] = jnp.zeros((last - first, 1), F32)

    def forward(first, last, low, high):
        def block(slot, carry):
            tail = tails[slot, 0:1, :]
            both = dot(normed[first:last], w_all[slot, :, 0:256]) + inv_all[first:last] * tail
            act_cot = dot(cot_all[first:last], w_all[slot, :, 256:384])
            gate, up = both[:, 0:128], both[:, 128:256]
            sigma = jax.nn.sigmoid(gate)
            swish = gate * sigma
            act_all[slot, first:last, :] = (swish * up).astype(BF16)
            gate_cot = (act_cot * up * sigma * (1.0 + gate * (1.0 - sigma))).astype(BF16)
            up_cot = (act_cot * swish).astype(BF16)
            cots_all[slot, first:last, 0:128] = gate_cot
            cots_all[slot, first:last, 128:256] = up_cot
            tin_all[first:last] += jnp.sum(
                gate_cot.astype(F32) * tail[:, 0:128] + up_cot.astype(F32) * tail[:, 128:256],
                axis=1,
                keepdims=True,
            )
            return carry

        lax.fori_loop(low, high, block, 0)

    def backward(first, last):
        def block(slot, carry):
            back[first:last] += dot_lanes(cots_all[slot, first:last], w_all[slot, :, 0:256])
            return carry

        back[first:last] = dot_lanes(cots_all[0, first:last], w_all[0, :, 0:256])
        lax.fori_loop(1, LINE, block, 0)
        for r in range(first, last, CAP):
            inverse = inv_all[r : r + CAP]
            unit = in_all[r : r + CAP].astype(F32) * inverse
            scaled = back[r : r + CAP] * gain_head
            inner = jnp.sum(scaled * unit, axis=1, keepdims=True) + tin_all[r : r + CAP] * inverse
            part_all[r : r + CAP] = (
                (scaled - unit * (inner / (2 * width))) * inverse
            ).astype(BF16)

    y_copies = []

    def y_send(step):
        row = Y_ROW[Y_ORDER.index(step)]
        there = Y_ORDER.index(4 if step == 4 else -step)
        y_copies.append(send(part_all.at[row : row + CAP], y_in.at[there], y_dev(step)))

    normalise(*NEAR)
    for copy in tail_copies + w_twin:
        copy.wait_recv()
    forward(*NEAR, 0, LINE - 1)
    ring[1, -1, 2].wait_recv()
    pass_on(1, -1, 3)
    ring[0, 1, 2].wait_recv()
    pass_on(0, 1, 3)
    first_twins = len(w_twin)
    w_far_a.wait_recv()
    swap(3, 0)
    w_far_b.wait_recv()
    swap(3, 1)
    normed_t[0] = normed[0 : FAR[0]].T
    cot_t[0] = cot_all[0 : FAR[0]].T
    for copy in w_twin[first_twins:]:
        copy.wait_recv()
    forward(*NEAR, LINE - 1, LINE)

    def near_product(slot, carry):
        g_acc[slot, :, 0:256] = dot(normed_t[0], cots_all[slot, 0 : FAR[0]])
        g_acc[slot, :, 256:384] = dot(cot_t[0], act_all[slot, 0 : FAR[0]])
        return carry

    lax.fori_loop(0, LINE, near_product, 0)
    backward(*NEAR)
    for step in (2, -2, 1, -1):
        y_send(step)

    ring[1, 1, 2].wait_recv()
    ring[0, -1, 2].wait_recv()
    ring[1, -1, 3].wait_recv()
    ring[0, 1, 3].wait_recv()
    normalise(*FAR)
    forward(*FAR, 0, LINE)
    normed_t[1] = normed[FAR[0] : ROWS].T
    cot_t[1] = cot_all[FAR[0] : ROWS].T

    def far_product(start, slot):
        wide = dot(normed_t[1, pl.ds(start, half)], cots_all[slot, FAR[0] : ROWS])
        narrow = dot(cot_t[1, pl.ds(start, half)], act_all[slot, FAR[0] : ROWS])
        return (
            wide + g_acc[slot, pl.ds(start, half), 0:256],
            narrow + g_acc[slot, pl.ds(start, half), 256:384],
        )

    their_start = pl.multiple_of((1 - core) * half, half)
    our_start = pl.multiple_of(core * half, half)

    def theirs(slot, carry):
        wide, narrow = far_product(their_start, slot)
        g_out[slot, :, 0:256] = wide.astype(BF16)
        g_out[slot, :, 256:384] = narrow.astype(BF16)
        return carry

    lax.fori_loop(0, LINE, theirs, 0)

    def cut(part):
        return slice(PIECES[part], PIECES[part + 1])

    def halves(part):
        first, last = PIECES[part], PIECES[part + 1]
        mid = (first + last) // 2
        return slice(first, mid), slice(mid, last)

    pair_copies = [
        send(g_out.at[:, cut(part)], g_in.at[:, cut(part)], sibling) for part in range(PARTS)
    ]

    def ours(slot, carry):
        wide, narrow = far_product(our_start, slot)
        g_acc[slot, pl.ds(our_start, half), 0:256] = wide
        g_acc[slot, pl.ds(our_start, half), 256:384] = narrow
        return carry

    lax.fori_loop(0, LINE, ours, 0)

    x_first, x_second, z_first, z_near, z_far, last_copies = ({} for _ in range(6))

    def rows_of(which, part):
        count = PIECES[part + 1] - PIECES[part]
        return pl.ds(pl.multiple_of(which * half + PIECES[part], 128), count)

    def own_rows(part):
        return rows_of(core, part)

    def x_start(part):
        pair_copies[part].wait_recv()

        def add(slot, carry):
            total = g_acc[slot, own_rows(part)] + g_in[slot, cut(part)].astype(F32)
            g_x[slot, cut(part)] = total.astype(BF16)
            return carry

        lax.fori_loop(1, LINE, add, 0)
        low, high = halves(part)
        x_first[part] = (
            send(g_x.at[3, low], x_opp.at[low], x_dev(1)),
            send(g_x.at[3, high], x_opp.at[high], x_dev(-1)),
            send(g_x.at[2, high], x_in.at[0, high], x_dev(1)),
            send(g_x.at[1, low], x_in.at[1, low], x_dev(-1)),
        )

    def x_relay(part):
        low, high = halves(part)
        x_first[part][0].wait_recv()
        g_x[2, low] = (g_x[2, low].astype(F32) + x_opp[low].astype(F32)).astype(BF16)
        right = send(g_x.at[2, low], x_in.at[0, low], x_dev(1))
        x_first[part][1].wait_recv()
        g_x[1, high] = (g_x[1, high].astype(F32) + x_opp[high].astype(F32)).astype(BF16)
        left = send(g_x.at[1, high], x_in.at[1, high], x_dev(-1))
        x_second[part] = (right, left)

    def z_cut(part, step, base=0):
        count = (PIECES[part + 1] - PIECES[part]) // n_z
        start = base + PIECES[part] + lax.rem(z + step + n_z, n_z) * count
        return pl.ds(pl.multiple_of(start, 16), count)

    def z_slot(part):
        return slice(PIECES[part] // n_z, PIECES[part + 1] // n_z)

    def z_start(part):
        for copy in x_first[part][2:] + x_second[part]:
            copy.wait_recv()
        h_all[cut(part)] = (
            g_acc[0, own_rows(part)]
            + g_in[0, cut(part)].astype(F32)
            + x_in[0, cut(part)].astype(F32)
            + x_in[1, cut(part)].astype(F32)
        ).astype(BF16)
        z_first[part] = [
            send(h_all.at[z_cut(part, step)], z_in.at[index, z_slot(part)], z_dev(step))
            for index, step in enumerate((4, 3, -3, 2, -2, 1, -1))
        ]

    def z_final(part, step):
        return z_cut(part, step, core * half)

    def z_sum(part):
        total = h_all[z_cut(part, 0)].astype(F32)
        for index, copy in enumerate(z_first[part]):
            copy.wait_recv()
            total = total + z_in[index, z_slot(part)].astype(F32)
        final[z_final(part, 0)] = total.astype(BF16)
        mine = final.at[z_final(part, 0)]
        z_near[part] = [send(mine, mine, z_dev(step)) for step in (2, -2, 1, -1)]

    def z_spread(part):
        copies = []
        for side, step in ((0, 1), (1, -1)):
            z_near[part][side].wait_recv()
            theirs = final.at[z_final(part, -2 * step)]
            copies.append(send(theirs, theirs, z_dev(step)))
            if side == min(part, 1):
                copies.append(send(theirs, theirs, z_dev(2 * step)))
        z_far[part] = copies

    def z_end(part):
        for copy in z_near[part][2:] + z_far[part]:
            copy.wait_recv()
        mine = final.at[own_rows(part)]
        last_copies[part] = send(mine, mine, sibling)

    x_start(0)
    x_start(1)
    backward(*FAR)
    for step in (4, 3, -3):
        y_send(step)
    x_relay(0)
    x_start(2)
    x_relay(1)

    def tail_rows(slot, carry):
        row = jnp.sum(cots_all[slot].astype(F32) * inv_all[...], axis=0, keepdims=True)
        v_out[slot] = jnp.broadcast_to(row, (8, 256))
        return carry

    lax.fori_loop(0, LINE, tail_rows, 0)
    v_copies = [
        send(v_out.at[1], v_in.at[0], x_dev(-1)),
        send(v_out.at[2], v_in.at[1], x_dev(1)),
        send(v_out.at[3], v_in.at[2], x_dev(2)),
    ]
    x_relay(2)
    z_start(0)

    for copy in v_copies:
        copy.wait_recv()
    v_pair[...] = v_out[0] + v_in[0] + v_in[1] + v_in[2]
    v_swap = send(v_pair, v_sib, sibling)

    z_start(1)
    v_swap.wait_recv()
    v_all[z] = v_pair[...] + v_sib[...]
    v_spread = [send(v_all.at[z], v_all.at[z], z_dev(step)) for step in range(1, n_z)]
    z_sum(0)
    z_start(2)
    z_sum(1)
    z_spread(0)
    z_sum(2)
    z_spread(1)
    early = len(started)

    for copy in y_copies:
        copy.wait_recv()
    widen_cot = part_all[0:CAP].astype(F32)
    for index in range(1, n_y):
        widen_cot = widen_cot + y_in[index].astype(F32)
    spread = dot_rows(chosen, cot_all[0:CAP]) + dot_rows(chosen, widen_cot.astype(BF16))
    ecot[...] = oc_ref[...].astype(F32) + spread
    for r in range(0, rows, CHUNK):
        g_mix[r : r + CHUNK] = ecot[r : r + CHUNK] * slope[r : r + CHUNK]
    edge_copy = send(g_mix.at[0:8], edge, before)

    z_spread(2)
    z_end(0)

    edge_copy.wait_recv()
    g_mix[rows : rows + 8] = edge[...] * (seq < n_seq - 1).astype(F32)
    for r in range(0, rows, CHUNK):
        grad = taps[0] * g_mix[r : r + CHUNK]
        for tap in range(1, KW):
            grad = grad + taps[tap] * g_mix[r + tap : r + tap + CHUNK]
        grad = grad * enc_gain
        value = x_ref[r : r + CHUNK].astype(F32)
        inverse = inv_x[r : r + CHUNK]
        inner = jnp.mean(grad * value, axis=1, keepdims=True) * (inverse * inverse)
        bg_ref[r : r + CHUNK] = (
            ecot[r : r + CHUNK] + (grad - value * inner) * inverse
        ).astype(BF16)
    store(bg_ref, bg_hbm)

    for copy in v_spread:
        copy.wait_recv()
    v_total = v_all[0]
    for chip in range(1, n_z):
        v_total = v_total + v_all[chip]
    v_ref[...] = v_total
    store(v_ref, v_hbm)

    z_end(1)
    for copy in started[:early]:
        copy.wait_send()
    z_end(2)
    for part in range(PARTS):
        store(final.at[own_rows(part)], final_hbm.at[own_rows(part)])
    for part in range(PARTS):
        last_copies[part].wait_recv()
        store(final.at[rows_of(1 - core, part)], final_hbm.at[rows_of(1 - core, part)])
    for copy in started[early:]:
        copy.wait_send()
    for copy in stores:
        copy.wait()


def finish(
    bg_hbm, final_hbm, tail_hbm, v_hbm, bg_out, gg_out, ug_out, dg_out, bg, final, tail_b, v_ref, gg, ug, dg, sems
):
    width = final.shape[0]
    copies = []

    def copy(source, target):
        step = pltpu.make_async_copy(source, target, sems.at[len(copies)])
        step.start()
        copies.append(step)
        return step

    load_final = copy(final_hbm, final)
    load_tail = copy(tail_hbm, tail_b)
    load_v = copy(v_hbm, v_ref)
    load_bg = copy(bg_hbm, bg)
    head, tail = slice(0, width), slice(width, 2 * width)
    load_final.wait()
    gg[head] = final[:, 0:128].astype(F32)
    copy(gg.at[head], gg_out.at[head])
    ug[head] = final[:, 128:256].astype(F32)
    copy(ug.at[head], ug_out.at[head])
    load_bg.wait()
    copy(bg, bg_out)
    load_tail.wait()
    load_v.wait()
    gg[tail] = tail_b[...] * v_ref[0:1, 0:128]
    copy(gg.at[tail], gg_out.at[tail])
    ug[tail] = tail_b[...] * v_ref[0:1, 128:256]
    copy(ug.at[tail], ug_out.at[tail])
    dg[...] = final[:, 256:384].astype(F32).T
    copy(dg, dg_out)
    for step in copies[4:]:
        step.wait()


def body(
    bytes_in,
    flags,
    enc_gain,
    conv_weight,
    widen,
    main_gain,
    gate_weight,
    up_weight,
    down_weight,
    out_cot,
):
    rows, width = bytes_in.shape[1:]
    n_y = lax.axis_size("seq") // LINE
    n_z = lax.axis_size("dp") // 2
    assert n_y == len(Y_ORDER)
    half = width // 2
    hbm = pl.BlockSpec(memory_space=pltpu.HBM)
    scratch = [
        ((rows, width), BF16),
        ((width, 384), BF16),
        ((width, 128), F32),
        ((8, 256), F32),
        ((rows, width), BF16),
        ((1, rows), jnp.int32),
        ((8, width // 8), BF16),
        ((KW, width), BF16),
        ((8, width // 8), BF16),
        ((16, width // 8), BF16),
        ((width, 128), BF16),
        ((width, 128), BF16),
        ((128, width), BF16),
        ((rows, width), BF16),
        ((LINE, width, 384), BF16),
        ((LINE, 8, 256), F32),
        ((16, width), BF16),
        ((8, width), F32),
        ((8, width), F32),
        ((rows + 16, width), F32),
        ((rows, 1), F32),
        ((rows, width), BF16),
        ((rows, width), F32),
        ((ROWS, width), BF16),
        ((ROWS, width), BF16),
        ((ROWS, width), BF16),
        ((2, width, ROWS // 2), BF16),
        ((2, width, ROWS // 2), BF16),
        ((ROWS, 1), F32),
        ((ROWS, 1), F32),
        ((LINE, ROWS, 128), BF16),
        ((LINE, ROWS, 256), BF16),
        ((ROWS, width), F32),
        ((ROWS, width), BF16),
        ((n_y, CAP, width), BF16),
        ((LINE, 8, 256), F32),
        ((LINE - 1, 8, 256), F32),
        ((8, 256), F32),
        ((8, 256), F32),
        ((n_z, 8, 256), F32),
        ((LINE, width, 384), F32),
        ((LINE, half, 384), BF16),
        ((LINE, half, 384), BF16),
        ((LINE, half, 384), BF16),
        ((half, 384), BF16),
        ((2, half, 384), BF16),
        ((half, 384), BF16),
        ((n_z - 1, half // n_z, 384), BF16),
        ((rows, width), F32),
        ((rows + 8, width), F32),
        ((8, width), F32),
    ]
    sums = pl.pallas_call(
        kernel,
        out_shape=(
            jax.ShapeDtypeStruct((rows, width), BF16),
            jax.ShapeDtypeStruct((width, 384), BF16),
            jax.ShapeDtypeStruct((width, 128), F32),
            jax.ShapeDtypeStruct((8, 256), F32),
        ),
        in_specs=[hbm] * 10,
        out_specs=[hbm] * 4,
        scratch_shapes=[pltpu.VMEM(shape, kind) for shape, kind in scratch]
        + [
            pltpu.SemaphoreType.DMA((12,)),
            pltpu.SemaphoreType.DMA((9,)),
            pltpu.SemaphoreType.DMA((120,)),
            pltpu.SemaphoreType.DMA((120,)),
        ],
        compiler_params=pltpu.CompilerParams(
            collective_id=0, has_side_effects=True, vmem_limit_bytes=60 * 1024 * 1024
        ),
    )(
        bytes_in[0],
        flags,
        enc_gain.reshape(8, width // 8),
        conv_weight,
        widen.reshape(8, width // 8),
        main_gain.reshape(16, width // 8),
        gate_weight,
        up_weight,
        down_weight,
        out_cot[0],
    )
    outs = pl.pallas_call(
        finish,
        out_shape=(
            jax.ShapeDtypeStruct((rows, width), BF16),
            jax.ShapeDtypeStruct((2 * width, 128), F32),
            jax.ShapeDtypeStruct((2 * width, 128), F32),
            jax.ShapeDtypeStruct((128, width), F32),
        ),
        in_specs=[hbm] * 4,
        out_specs=[hbm] * 4,
        scratch_shapes=[
            pltpu.VMEM((rows, width), BF16),
            pltpu.VMEM((width, 384), BF16),
            pltpu.VMEM((width, 128), F32),
            pltpu.VMEM((8, 256), F32),
            pltpu.VMEM((2 * width, 128), F32),
            pltpu.VMEM((2 * width, 128), F32),
            pltpu.VMEM((128, width), F32),
            pltpu.SemaphoreType.DMA((10,)),
        ],
        compiler_params=pltpu.CompilerParams(vmem_limit_bytes=60 * 1024 * 1024),
    )(*sums)
    return (outs[0][None], outs[1], outs[2], outs[3])


def solution(mesh):
    in_specs = (
        P("dp", "seq", None),
        P("dp", "seq"),
        P(),
        P(),
        P(),
        P(),
        P(None, "seq"),
        P(None, "seq"),
        P("seq", None),
        P("dp", "seq", None),
    )
    out_specs = (P("dp", "seq", None), P(None, "seq"), P(None, "seq"), P("seq", None))
    return jax.shard_map(body, mesh=mesh, in_specs=in_specs, out_specs=out_specs, check_vma=False)
```

```python
import jax
import jax.numpy as jnp
from jax import lax
from jax.experimental import pallas as pl
from jax.experimental.pallas import tpu as pltpu
from jax.sharding import PartitionSpec as P

MESH = pl.DeviceIdType.MESH
F32 = jnp.float32
BF16 = jnp.bfloat16

KW = 4
CAP = 48
EPS = 1e-05
LINE = 4
PIECES = (0, 128, 384, 512)
PARTS = len(PIECES) - 1
CHUNK = 32

Y_ORDER = (0, -1, 1, -2, 2, -3, 3, 4)
Y_ROW = (0, 48, 96, 144, 192, 256, 304, 352)
NEAR = (0, 240)
FAR = (256, 400)
ROWS = 512
X_ORDER = (0, -1, 1, 2)


def dot(left, right):
    return jnp.dot(left, right, preferred_element_type=F32)


def dot_rows(left, right):
    return lax.dot_general(left, right, (((0,), (0,)), ((), ())), preferred_element_type=F32)


def dot_lanes(left, right):
    return lax.dot_general(left, right, (((1,), (1,)), ((), ())), preferred_element_type=F32)


def as_row(value):
    value = value.astype(F32)
    return jnp.concatenate([value[i : i + 1] for i in range(value.shape[0])], axis=1)


def kernel(
    x_hbm,
    marks_hbm,
    enc_gain_hbm,
    conv_hbm,
    widen_hbm,
    main_gain_hbm,
    gw_hbm,
    uw_hbm,
    dw_hbm,
    oc_hbm,
    bg_hbm,
    final_hbm,
    tail_hbm,
    v_hbm,
    bg_ref,
    final,
    tail_b,
    v_ref,
    x_ref,
    marks_ref,
    enc_gain_ref,
    conv_ref,
    widen_ref,
    main_gain_ref,
    gw_tail,
    uw_tail,
    dw_ref,
    oc_ref,
    w_all,
    tails,
    halo,
    lead_out,
    lead_in,
    norm_x,
    inv_x,
    enc_out,
    slope,
    in_all,
    cot_all,
    normed,
    normed_t,
    cot_t,
    inv_all,
    tin_all,
    act_all,
    cots_all,
    back,
    part_all,
    y_in,
    v_out,
    v_in,
    v_pair,
    v_sib,
    v_all,
    g_acc,
    g_out,
    g_in,
    g_x,
    x_opp,
    x_in,
    h_all,
    z_in,
    ecot,
    g_mix,
    edge,
    load_sems,
    store_sems,
    send_sems,
    recv_sems,
):
    n_seq = lax.axis_size("seq")
    n_y = n_seq // LINE
    n_z = lax.axis_size("dp") // 2
    dp = lax.axis_index("dp")
    seq = lax.axis_index("seq")
    z, core = dp // 2, dp % 2
    y, x = seq // LINE, seq % LINE
    rows, width = x_ref.shape
    half = width // 2

    def y_dev(step):
        return {"seq": lax.rem(y + step + n_y, n_y) * LINE + x}

    def x_dev(step):
        return {"seq": y * LINE + lax.rem(x + step + LINE, LINE)}

    def z_dev(step):
        return {"dp": lax.rem(z + step + n_z, n_z) * 2 + core}

    sibling = {"dp": z * 2 + 1 - core}
    after = {"seq": lax.rem(seq + 1, n_seq)}
    before = {"seq": lax.rem(seq + n_seq - 1, n_seq)}

    loads = []
    stores = []

    def load(source, target):
        copy = pltpu.make_async_copy(source, target, load_sems.at[len(loads)])
        copy.start()
        loads.append(copy)
        return copy

    def store(source, target):
        copy = pltpu.make_async_copy(source, target, store_sems.at[len(stores)])
        copy.start()
        stores.append(copy)

    load_marks = load(marks_hbm, marks_ref)
    load_oc = load(oc_hbm, oc_ref)

    started = []

    def send(source, target, device):
        index = len(started)
        copy = pltpu.make_async_remote_copy(
            src_ref=source,
            dst_ref=target,
            send_sem=send_sems.at[index],
            recv_sem=recv_sems.at[index],
            device_id=device,
            device_id_type=MESH,
        )
        copy.start()
        started.append(copy)
        return copy

    barrier = pltpu.get_barrier_semaphore()
    peers = [y_dev(step) for step in range(1, n_y)]
    peers += [x_dev(step) for step in (1, -1, 2)]
    peers += [z_dev(step) for step in range(1, n_z)]
    peers += [sibling, after, before]
    for peer in peers:
        pl.semaphore_signal(barrier, inc=1, device_id=peer, device_id_type=MESH)

    load_x = load(x_hbm, x_ref)
    load_gain = load(enc_gain_hbm, enc_gain_ref)
    load_conv = load(conv_hbm, conv_ref)
    load_w = [
        load(dw_hbm, dw_ref),
        load(gw_hbm.at[0:width], w_all.at[0, :, 0:128]),
        load(uw_hbm.at[0:width], w_all.at[0, :, 128:256]),
    ]
    load_tail = [
        load(widen_hbm, widen_ref),
        load(main_gain_hbm, main_gain_ref),
        load(gw_hbm.at[width : 2 * width], gw_tail),
        load(uw_hbm.at[width : 2 * width], uw_tail),
    ]

    load_marks.wait()
    marks = marks_ref[...].astype(F32)
    upper = (
        lax.broadcasted_iota(jnp.int32, (rows, rows), 0)
        <= lax.broadcasted_iota(jnp.int32, (rows, rows), 1)
    ).astype(F32).astype(BF16)
    running = dot(jnp.broadcast_to(marks, (16, rows)).astype(BF16), upper)
    lead = jnp.where(running == 0.0, 1.0, 0.0).astype(BF16)
    slot_ids = lax.broadcasted_iota(jnp.int32, (CAP, rows), 0).astype(F32)
    member = jnp.where(slot_ids == running[0:1] - 1.0, 1.0, 0.0)
    chosen = (member * marks).astype(BF16)
    last_slot = jnp.where(slot_ids[:, 0:1] == running[0:1, rows - 1 : rows] - 1.0, 1.0, 0.0)
    load_oc.wait()
    lead_out[...] = dot(lead, oc_ref[...])[0:8]

    pl.semaphore_wait(barrier, len(peers))

    halo_copy = send(x_hbm.at[rows - 16 : rows], halo, after)
    lead_copy = send(lead_out, lead_in, before)
    own_sums = dot(member.astype(BF16), oc_ref[...])

    for copy in load_w:
        copy.wait()
    w_all[0, :, 256:384] = dw_ref[...].astype(F32).T.astype(BF16)

    def w_rows(slot, part):
        start = pl.multiple_of(core * half + part * (half // 2), half // 2)
        return w_all.at[slot, pl.ds(start, half // 2)]

    w_right = [None, None]
    w_left = [None, None]
    for part in (0, 1):
        w_right[part] = send(w_rows(0, part), w_rows(1, part), x_dev(1))
        w_left[1 - part] = send(w_rows(0, 1 - part), w_rows(2, 1 - part), x_dev(-1))

    ring = {}

    def pass_on(which, direction, step):
        buffer = (in_all, cot_all)[which]
        here = Y_ROW[Y_ORDER.index(-direction * step)]
        there = Y_ROW[Y_ORDER.index(-direction * (step + 1))]
        ring[which, direction, step] = send(
            buffer.at[here : here + CAP], buffer.at[there : there + CAP], y_dev(direction)
        )

    lead_copy.wait_recv()
    carried = lead_in[0:1] * (seq < n_seq - 1).astype(F32)
    cot_all[0:CAP] = (own_sums + last_slot * carried).astype(BF16)
    pass_on(1, 1, 0)
    pass_on(1, -1, 0)

    load_gain.wait()
    load_conv.wait()
    load_x.wait()
    enc_gain = as_row(enc_gain_ref[...])
    taps = [conv_ref[tap : tap + 1, :].astype(F32) for tap in range(KW)]
    for r in range(0, rows, CHUNK):
        value = x_ref[r : r + CHUNK].astype(F32)
        inverse = lax.rsqrt(jnp.mean(value * value, axis=1, keepdims=True) + EPS)
        inv_x[r : r + CHUNK] = inverse
        norm_x[16 + r : 16 + r + CHUNK] = value * inverse * enc_gain
    halo_copy.wait_recv()
    value = halo[...].astype(F32) * (seq > 0).astype(F32)
    inverse = lax.rsqrt(jnp.mean(value * value, axis=1, keepdims=True) + EPS)
    norm_x[0:16] = value * inverse * enc_gain
    for r in range(0, rows, CHUNK):
        mixed = taps[0] * norm_x[16 + r : 16 + r + CHUNK]
        for tap in range(1, KW):
            mixed = mixed + taps[tap] * norm_x[16 + r - tap : 16 + r - tap + CHUNK]
        sigma = jax.nn.sigmoid(mixed)
        enc_out[r : r + CHUNK] = (x_ref[r : r + CHUNK].astype(F32) + mixed * sigma).astype(BF16)
        slope[r : r + CHUNK] = sigma * (1.0 + mixed * (1.0 - sigma))
    in_all[0:CAP] = dot(chosen, enc_out[...]).astype(BF16)
    pass_on(0, 1, 0)
    pass_on(0, -1, 0)

    w_twin = []

    def swap(slot, part):
        w_twin.append(send(w_rows(slot, part), w_rows(slot, part), sibling))

    for copy in load_tail:
        copy.wait()
    widen = as_row(widen_ref[...])
    main_gain = as_row(main_gain_ref[...])
    gain_head = main_gain[:, 0:width]
    tail_vec = widen * main_gain[:, width : 2 * width]
    tail_square = jnp.sum(widen * widen, axis=1, keepdims=True)
    tail_b[...] = jnp.broadcast_to(tail_vec, (128, width)).T
    store(tail_b, tail_hbm)
    tail_gate = jnp.sum(gw_tail[...].astype(F32) * tail_b[...], axis=0, keepdims=True)
    tail_up = jnp.sum(uw_tail[...].astype(F32) * tail_b[...], axis=0, keepdims=True)
    tails[0, :, 0:128] = jnp.broadcast_to(tail_gate, (8, 128))
    tails[0, :, 128:256] = jnp.broadcast_to(tail_up, (8, 128))
    tail_copies = [
        send(tails.at[0], tails.at[1], x_dev(1)),
        send(tails.at[0], tails.at[2], x_dev(-1)),
        send(tails.at[0], tails.at[3], x_dev(2)),
    ]

    def relay(which, step):
        for direction in (1, -1):
            ring[which, direction, step - 1].wait_recv()
            pass_on(which, direction, step)

    def relay_last(which):
        buffer = (in_all, cot_all)[which]
        there = Y_ROW[Y_ORDER.index(4)]
        for direction in (1, -1):
            ring[which, direction, 2].wait_recv()
            here = Y_ROW[Y_ORDER.index(-3 * direction)]
            lanes = slice(0, half) if direction == 1 else slice(half, width)
            ring[which, direction, 3] = send(
                buffer.at[here : here + CAP, lanes],
                buffer.at[there : there + CAP, lanes],
                y_dev(direction),
            )

    relay(1, 1)
    relay(0, 1)
    w_right[0].wait_recv()
    w_far_a = send(w_rows(1, 0), w_rows(3, 0), x_dev(1))
    w_left[1].wait_recv()
    w_far_b = send(w_rows(2, 1), w_rows(3, 1), x_dev(-1))
    swap(1, 0)
    swap(2, 1)
    for first, last in ((NEAR[1], FAR[0]), (FAR[1], ROWS)):
        count = last - first
        normed[first:last] = jnp.zeros((count, width), BF16)
        cot_all[first:last] = jnp.zeros((count, width), BF16)
        inv_all[first:last] = jnp.zeros((count, 1), F32)
        act_all[:, first:last] = jnp.zeros((LINE, count, 128), BF16)
        cots_all[:, first:last] = jnp.zeros((LINE, count, 256), BF16)
    relay(1, 2)
    relay(0, 2)
    w_right[1].wait_recv()
    swap(1, 1)
    w_left[0].wait_recv()
    swap(2, 0)

    def normalise(first, last):
        for r in range(first, last, CAP):
            head = in_all[r : r + CAP].astype(F32)
            square = jnp.sum(head * head, axis=1, keepdims=True) + tail_square
            inverse = lax.rsqrt(square / (2 * width) + EPS)
            inv_all[r : r + CAP] = inverse
            normed[r : r + CAP] = (head * inverse * gain_head).astype(BF16)
        tin_all[first:last] = jnp.zeros((last - first, 1), F32)

    def forward(first, last, low, high):
        def block(slot, carry):
            tail = tails[slot, 0:1, :]
            both = dot(normed[first:last], w_all[slot, :, 0:256]) + inv_all[first:last] * tail
            act_cot = dot(cot_all[first:last], w_all[slot, :, 256:384])
            gate, up = both[:, 0:128], both[:, 128:256]
            sigma = jax.nn.sigmoid(gate)
            swish = gate * sigma
            act_all[slot, first:last, :] = (swish * up).astype(BF16)
            gate_cot = (act_cot * up * sigma * (1.0 + gate * (1.0 - sigma))).astype(BF16)
            up_cot = (act_cot * swish).astype(BF16)
            cots_all[slot, first:last, 0:128] = gate_cot
            cots_all[slot, first:last, 128:256] = up_cot
            tin_all[first:last] += jnp.sum(
                gate_cot.astype(F32) * tail[:, 0:128] + up_cot.astype(F32) * tail[:, 128:256],
                axis=1,
                keepdims=True,
            )
            return carry

        lax.fori_loop(low, high, block, 0)

    def backward(first, last):
        def block(slot, carry):
            back[first:last] += dot_lanes(cots_all[slot, first:last], w_all[slot, :, 0:256])
            return carry

        back[first:last] = dot_lanes(cots_all[0, first:last], w_all[0, :, 0:256])
        lax.fori_loop(1, LINE, block, 0)
        for r in range(first, last, CAP):
            inverse = inv_all[r : r + CAP]
            unit = in_all[r : r + CAP].astype(F32) * inverse
            scaled = back[r : r + CAP] * gain_head
            inner = jnp.sum(scaled * unit, axis=1, keepdims=True) + tin_all[r : r + CAP] * inverse
            part_all[r : r + CAP] = (
                (scaled - unit * (inner / (2 * width))) * inverse
            ).astype(BF16)

    y_copies = []

    def y_send(step):
        row = Y_ROW[Y_ORDER.index(step)]
        there = Y_ORDER.index(4 if step == 4 else -step)
        y_copies.append(send(part_all.at[row : row + CAP], y_in.at[there], y_dev(step)))

    normalise(*NEAR)
    for copy in tail_copies + w_twin:
        copy.wait_recv()
    forward(*NEAR, 0, LINE - 1)
    relay_last(1)
    normed_t[0] = normed[0 : FAR[0]].T
    cot_t[0] = cot_all[0 : FAR[0]].T
    first_twins = len(w_twin)
    w_far_a.wait_recv()
    swap(3, 0)
    w_far_b.wait_recv()
    swap(3, 1)
    relay_last(0)
    for copy in w_twin[first_twins:]:
        copy.wait_recv()
    forward(*NEAR, LINE - 1, LINE)

    def near_product(slot, carry):
        g_acc[slot, :, 0:256] = dot(normed_t[0], cots_all[slot, 0 : FAR[0]])
        g_acc[slot, :, 256:384] = dot(cot_t[0], act_all[slot, 0 : FAR[0]])
        return carry

    lax.fori_loop(0, LINE, near_product, 0)

    for direction in (1, -1):
        ring[1, direction, 3].wait_recv()
    cot_t[1] = cot_all[FAR[0] : ROWS].T
    for direction in (1, -1):
        ring[0, direction, 3].wait_recv()
    normalise(*FAR)
    forward(*FAR, 0, LINE)
    normed_t[1] = normed[FAR[0] : ROWS].T

    def far_product(start, count, slot):
        some = pl.ds(pl.multiple_of(start, 128), count)
        wide = dot(normed_t[1, some], cots_all[slot, FAR[0] : ROWS])
        narrow = dot(cot_t[1, some], act_all[slot, FAR[0] : ROWS])
        return wide + g_acc[slot, some, 0:256], narrow + g_acc[slot, some, 256:384]

    def theirs(low, high):
        def block(slot, carry):
            wide, narrow = far_product((1 - core) * half + low, high - low, slot)
            g_out[slot, low:high, 0:256] = wide.astype(BF16)
            g_out[slot, low:high, 256:384] = narrow.astype(BF16)
            return carry

        lax.fori_loop(0, LINE, block, 0)

    def cut(part):
        return slice(PIECES[part], PIECES[part + 1])

    def halves(part):
        first, last = PIECES[part], PIECES[part + 1]
        mid = (first + last) // 2
        return slice(first, mid), slice(mid, last)

    def pair(part):
        return send(g_out.at[:, cut(part)], g_in.at[:, cut(part)], sibling)

    theirs(0, PIECES[1])
    pair_copies = [pair(0)]
    theirs(PIECES[1], half)
    pair_copies += [pair(part) for part in range(1, PARTS)]

    def ours(slot, carry):
        wide, narrow = far_product(core * half, half, slot)
        some = pl.ds(pl.multiple_of(core * half, half), half)
        g_acc[slot, some, 0:256] = wide
        g_acc[slot, some, 256:384] = narrow
        return carry

    lax.fori_loop(0, LINE, ours, 0)
    backward(*NEAR)
    for step in (2, -2, 1, -1):
        y_send(step)

    x_first, x_second, z_first, z_near, z_far, last_copies = ({} for _ in range(6))

    def rows_of(which, part):
        count = PIECES[part + 1] - PIECES[part]
        return pl.ds(pl.multiple_of(which * half + PIECES[part], 128), count)

    def own_rows(part):
        return rows_of(core, part)

    def x_start(part):
        pair_copies[part].wait_recv()

        def add(slot, carry):
            total = g_acc[slot, own_rows(part)] + g_in[slot, cut(part)].astype(F32)
            g_x[slot, cut(part)] = total.astype(BF16)
            return carry

        lax.fori_loop(1, LINE, add, 0)
        low, high = halves(part)
        x_first[part] = (
            send(g_x.at[3, low], x_opp.at[low], x_dev(1)),
            send(g_x.at[3, high], x_opp.at[high], x_dev(-1)),
            send(g_x.at[2, high], x_in.at[0, high], x_dev(1)),
            send(g_x.at[1, low], x_in.at[1, low], x_dev(-1)),
        )

    def x_relay(part):
        low, high = halves(part)
        x_first[part][0].wait_recv()
        g_x[2, low] = (g_x[2, low].astype(F32) + x_opp[low].astype(F32)).astype(BF16)
        right = send(g_x.at[2, low], x_in.at[0, low], x_dev(1))
        x_first[part][1].wait_recv()
        g_x[1, high] = (g_x[1, high].astype(F32) + x_opp[high].astype(F32)).astype(BF16)
        left = send(g_x.at[1, high], x_in.at[1, high], x_dev(-1))
        x_second[part] = (right, left)

    def z_cut(part, step, base=0):
        count = (PIECES[part + 1] - PIECES[part]) // n_z
        start = base + PIECES[part] + lax.rem(z + step + n_z, n_z) * count
        return pl.ds(pl.multiple_of(start, 16), count)

    def z_slot(part):
        return slice(PIECES[part] // n_z, PIECES[part + 1] // n_z)

    def z_start(part):
        for copy in x_first[part][2:] + x_second[part]:
            copy.wait_recv()
        h_all[cut(part)] = (
            g_acc[0, own_rows(part)]
            + g_in[0, cut(part)].astype(F32)
            + x_in[0, cut(part)].astype(F32)
            + x_in[1, cut(part)].astype(F32)
        ).astype(BF16)
        z_first[part] = [
            send(h_all.at[z_cut(part, step)], z_in.at[index, z_slot(part)], z_dev(step))
            for index, step in enumerate((4, 3, -3, 2, -2, 1, -1))
        ]

    def z_final(part, step):
        return z_cut(part, step, core * half)

    def z_sum(part):
        total = h_all[z_cut(part, 0)].astype(F32)
        for index, copy in enumerate(z_first[part]):
            copy.wait_recv()
            total = total + z_in[index, z_slot(part)].astype(F32)
        final[z_final(part, 0)] = total.astype(BF16)
        mine = final.at[z_final(part, 0)]
        z_near[part] = [send(mine, mine, z_dev(step)) for step in (2, -2, 1, -1)]

    def z_spread(part):
        copies = []
        for side, step in ((0, 1), (1, -1)):
            z_near[part][side].wait_recv()
            theirs = final.at[z_final(part, -2 * step)]
            copies.append(send(theirs, theirs, z_dev(step)))
            if side == (0 if part == 1 else 1):
                copies.append(send(theirs, theirs, z_dev(2 * step)))
        z_far[part] = copies

    def z_end(part):
        for copy in z_near[part][2:] + z_far[part]:
            copy.wait_recv()
        mine = final.at[own_rows(part)]
        last_copies[part] = send(mine, mine, sibling)

    x_start(0)
    x_start(1)
    backward(*FAR)
    for step in (4, 3, -3):
        y_send(step)
    x_relay(0)
    x_start(2)
    x_relay(1)

    def tail_rows(slot, carry):
        row = jnp.sum(cots_all[slot].astype(F32) * inv_all[...], axis=0, keepdims=True)
        v_out[slot] = jnp.broadcast_to(row, (8, 256))
        return carry

    lax.fori_loop(0, LINE, tail_rows, 0)
    v_copies = [
        send(v_out.at[1], v_in.at[0], x_dev(-1)),
        send(v_out.at[2], v_in.at[1], x_dev(1)),
        send(v_out.at[3], v_in.at[2], x_dev(2)),
    ]
    x_relay(2)
    z_start(0)

    for copy in v_copies:
        copy.wait_recv()
    v_pair[...] = v_out[0] + v_in[0] + v_in[1] + v_in[2]
    v_swap = send(v_pair, v_sib, sibling)

    z_start(1)
    v_swap.wait_recv()
    v_all[z] = v_pair[...] + v_sib[...]
    v_spread = [send(v_all.at[z], v_all.at[z], z_dev(step)) for step in range(1, n_z)]
    z_sum(0)
    z_start(2)
    z_sum(1)
    z_spread(0)
    z_sum(2)
    z_spread(1)
    early = len(started)

    for copy in y_copies:
        copy.wait_recv()
    widen_cot = part_all[0:CAP].astype(F32)
    for index in range(1, n_y):
        widen_cot = widen_cot + y_in[index].astype(F32)
    spread = dot_rows(chosen, cot_all[0:CAP]) + dot_rows(chosen, widen_cot.astype(BF16))
    ecot[...] = oc_ref[...].astype(F32) + spread
    for r in range(0, rows, CHUNK):
        g_mix[r : r + CHUNK] = ecot[r : r + CHUNK] * slope[r : r + CHUNK]
    edge_copy = send(g_mix.at[0:8], edge, before)

    z_spread(2)
    z_end(0)

    edge_copy.wait_recv()
    g_mix[rows : rows + 8] = edge[...] * (seq < n_seq - 1).astype(F32)
    for r in range(0, rows, CHUNK):
        grad = taps[0] * g_mix[r : r + CHUNK]
        for tap in range(1, KW):
            grad = grad + taps[tap] * g_mix[r + tap : r + tap + CHUNK]
        grad = grad * enc_gain
        value = x_ref[r : r + CHUNK].astype(F32)
        inverse = inv_x[r : r + CHUNK]
        inner = jnp.mean(grad * value, axis=1, keepdims=True) * (inverse * inverse)
        bg_ref[r : r + CHUNK] = (
            ecot[r : r + CHUNK] + (grad - value * inner) * inverse
        ).astype(BF16)
    store(bg_ref, bg_hbm)

    for copy in v_spread:
        copy.wait_recv()
    v_total = v_all[0]
    for chip in range(1, n_z):
        v_total = v_total + v_all[chip]
    v_ref[...] = v_total
    store(v_ref, v_hbm)

    z_end(1)
    for copy in started[:early]:
        copy.wait_send()
    z_end(2)
    for part in range(PARTS):
        store(final.at[own_rows(part)], final_hbm.at[own_rows(part)])
    for part in range(PARTS):
        last_copies[part].wait_recv()
        store(final.at[rows_of(1 - core, part)], final_hbm.at[rows_of(1 - core, part)])
    for copy in started[early:]:
        copy.wait_send()
    for copy in stores:
        copy.wait()


def finish(
    bg_hbm, final_hbm, tail_hbm, v_hbm, bg_out, gg_out, ug_out, dg_out, bg, final, tail_b, v_ref, gg, ug, dg, sems
):
    width = final.shape[0]
    copies = []

    def copy(source, target):
        step = pltpu.make_async_copy(source, target, sems.at[len(copies)])
        step.start()
        copies.append(step)
        return step

    load_final = copy(final_hbm, final)
    load_tail = copy(tail_hbm, tail_b)
    load_v = copy(v_hbm, v_ref)
    load_bg = copy(bg_hbm, bg)
    head, tail = slice(0, width), slice(width, 2 * width)
    load_final.wait()
    gg[head] = final[:, 0:128].astype(F32)
    copy(gg.at[head], gg_out.at[head])
    ug[head] = final[:, 128:256].astype(F32)
    copy(ug.at[head], ug_out.at[head])
    load_bg.wait()
    copy(bg, bg_out)
    load_tail.wait()
    load_v.wait()
    gg[tail] = tail_b[...] * v_ref[0:1, 0:128]
    copy(gg.at[tail], gg_out.at[tail])
    ug[tail] = tail_b[...] * v_ref[0:1, 128:256]
    copy(ug.at[tail], ug_out.at[tail])
    dg[...] = final[:, 256:384].astype(F32).T
    copy(dg, dg_out)
    for step in copies[4:]:
        step.wait()


def body(
    bytes_in,
    flags,
    enc_gain,
    conv_weight,
    widen,
    main_gain,
    gate_weight,
    up_weight,
    down_weight,
    out_cot,
):
    rows, width = bytes_in.shape[1:]
    n_y = lax.axis_size("seq") // LINE
    n_z = lax.axis_size("dp") // 2
    assert n_y == len(Y_ORDER)
    half = width // 2
    hbm = pl.BlockSpec(memory_space=pltpu.HBM)
    scratch = [
        ((rows, width), BF16),
        ((width, 384), BF16),
        ((width, 128), F32),
        ((8, 256), F32),
        ((rows, width), BF16),
        ((1, rows), jnp.int32),
        ((8, width // 8), BF16),
        ((KW, width), BF16),
        ((8, width // 8), BF16),
        ((16, width // 8), BF16),
        ((width, 128), BF16),
        ((width, 128), BF16),
        ((128, width), BF16),
        ((rows, width), BF16),
        ((LINE, width, 384), BF16),
        ((LINE, 8, 256), F32),
        ((16, width), BF16),
        ((8, width), F32),
        ((8, width), F32),
        ((rows + 16, width), F32),
        ((rows, 1), F32),
        ((rows, width), BF16),
        ((rows, width), F32),
        ((ROWS, width), BF16),
        ((ROWS, width), BF16),
        ((ROWS, width), BF16),
        ((2, width, ROWS // 2), BF16),
        ((2, width, ROWS // 2), BF16),
        ((ROWS, 1), F32),
        ((ROWS, 1), F32),
        ((LINE, ROWS, 128), BF16),
        ((LINE, ROWS, 256), BF16),
        ((ROWS, width), F32),
        ((ROWS, width), BF16),
        ((n_y, CAP, width), BF16),
        ((LINE, 8, 256), F32),
        ((LINE - 1, 8, 256), F32),
        ((8, 256), F32),
        ((8, 256), F32),
        ((n_z, 8, 256), F32),
        ((LINE, width, 384), F32),
        ((LINE, half, 384), BF16),
        ((LINE, half, 384), BF16),
        ((LINE, half, 384), BF16),
        ((half, 384), BF16),
        ((2, half, 384), BF16),
        ((half, 384), BF16),
        ((n_z - 1, half // n_z, 384), BF16),
        ((rows, width), F32),
        ((rows + 8, width), F32),
        ((8, width), F32),
    ]
    sums = pl.pallas_call(
        kernel,
        out_shape=(
            jax.ShapeDtypeStruct((rows, width), BF16),
            jax.ShapeDtypeStruct((width, 384), BF16),
            jax.ShapeDtypeStruct((width, 128), F32),
            jax.ShapeDtypeStruct((8, 256), F32),
        ),
        in_specs=[hbm] * 10,
        out_specs=[hbm] * 4,
        scratch_shapes=[pltpu.VMEM(shape, kind) for shape, kind in scratch]
        + [
            pltpu.SemaphoreType.DMA((12,)),
            pltpu.SemaphoreType.DMA((9,)),
            pltpu.SemaphoreType.DMA((120,)),
            pltpu.SemaphoreType.DMA((120,)),
        ],
        compiler_params=pltpu.CompilerParams(
            collective_id=0, has_side_effects=True, vmem_limit_bytes=60 * 1024 * 1024
        ),
    )(
        bytes_in[0],
        flags,
        enc_gain.reshape(8, width // 8),
        conv_weight,
        widen.reshape(8, width // 8),
        main_gain.reshape(16, width // 8),
        gate_weight,
        up_weight,
        down_weight,
        out_cot[0],
    )
    outs = pl.pallas_call(
        finish,
        out_shape=(
            jax.ShapeDtypeStruct((rows, width), BF16),
            jax.ShapeDtypeStruct((2 * width, 128), F32),
            jax.ShapeDtypeStruct((2 * width, 128), F32),
            jax.ShapeDtypeStruct((128, width), F32),
        ),
        in_specs=[hbm] * 4,
        out_specs=[hbm] * 4,
        scratch_shapes=[
            pltpu.VMEM((rows, width), BF16),
            pltpu.VMEM((width, 384), BF16),
            pltpu.VMEM((width, 128), F32),
            pltpu.VMEM((8, 256), F32),
            pltpu.VMEM((2 * width, 128), F32),
            pltpu.VMEM((2 * width, 128), F32),
            pltpu.VMEM((128, width), F32),
            pltpu.SemaphoreType.DMA((10,)),
        ],
        compiler_params=pltpu.CompilerParams(vmem_limit_bytes=60 * 1024 * 1024),
    )(*sums)
    return (outs[0][None], outs[1], outs[2], outs[3])


def solution(mesh):
    in_specs = (
        P("dp", "seq", None),
        P("dp", "seq"),
        P(),
        P(),
        P(),
        P(),
        P(None, "seq"),
        P(None, "seq"),
        P("seq", None),
        P("dp", "seq", None),
    )
    out_specs = (P("dp", "seq", None), P(None, "seq"), P(None, "seq"), P("seq", None))
    return jax.shard_map(body, mesh=mesh, in_specs=in_specs, out_specs=out_specs, check_vma=False)
```

```python
import jax
import jax.numpy as jnp
from jax import lax
from jax.experimental import pallas as pl
from jax.experimental.pallas import tpu as pltpu
from jax.sharding import PartitionSpec as P

MESH = pl.DeviceIdType.MESH
F32 = jnp.float32
BF16 = jnp.bfloat16

KW = 4
CAP = 48
EPS = 1e-05
LINE = 4
PIECES = (0, 256, 512)
PARTS = len(PIECES) - 1
CHUNK = 32

Y_ORDER = (0, -1, 1, -2, 2, -3, 3, 4)
Y_ROW = (0, 48, 96, 144, 192, 256, 304, 352)
NEAR = (0, 240)
FAR = (256, 400)
ROWS = 512
X_ORDER = (0, -1, 1, 2)


def dot(left, right):
    return jnp.dot(left, right, preferred_element_type=F32)


def dot_rows(left, right):
    return lax.dot_general(left, right, (((0,), (0,)), ((), ())), preferred_element_type=F32)


def dot_lanes(left, right):
    return lax.dot_general(left, right, (((1,), (1,)), ((), ())), preferred_element_type=F32)


def as_row(value):
    value = value.astype(F32)
    return jnp.concatenate([value[i : i + 1] for i in range(value.shape[0])], axis=1)


def kernel(
    x_hbm,
    marks_hbm,
    enc_gain_hbm,
    conv_hbm,
    widen_hbm,
    main_gain_hbm,
    gw_hbm,
    uw_hbm,
    dw_hbm,
    oc_hbm,
    bg_hbm,
    final_hbm,
    tail_hbm,
    v_hbm,
    bg_ref,
    final,
    tail_b,
    x_ref,
    marks_ref,
    enc_gain_ref,
    conv_ref,
    widen_ref,
    main_gain_ref,
    gw_tail,
    uw_tail,
    dw_ref,
    oc_ref,
    w_all,
    tails,
    halo,
    lead_out,
    lead_in,
    norm_x,
    inv_x,
    enc_out,
    slope,
    in_all,
    cot_all,
    normed,
    normed_t,
    cot_t,
    inv_all,
    tin_all,
    act_all,
    cots_all,
    back,
    part_all,
    y_in,
    v_out,
    v_in,
    v_step,
    v_other,
    g_acc,
    g_out,
    g_in,
    g_x,
    x_opp,
    x_in,
    h_all,
    z_in,
    ecot,
    g_mix,
    edge,
    load_sems,
    store_sems,
    send_sems,
    recv_sems,
):
    n_seq = lax.axis_size("seq")
    n_y = n_seq // LINE
    n_z = lax.axis_size("dp") // 2
    dp = lax.axis_index("dp")
    seq = lax.axis_index("seq")
    z, core = dp // 2, dp % 2
    y, x = seq // LINE, seq % LINE
    rows, width = x_ref.shape
    half = width // 2

    def y_dev(step):
        return {"seq": lax.rem(y + step + n_y, n_y) * LINE + x}

    def x_dev(step):
        return {"seq": y * LINE + lax.rem(x + step + LINE, LINE)}

    def z_dev(step):
        return {"dp": lax.rem(z + step + n_z, n_z) * 2 + core}

    sibling = {"dp": z * 2 + 1 - core}
    after = {"seq": lax.rem(seq + 1, n_seq)}
    before = {"seq": lax.rem(seq + n_seq - 1, n_seq)}

    loads = []
    stores = []

    def load(source, target):
        copy = pltpu.make_async_copy(source, target, load_sems.at[len(loads)])
        copy.start()
        loads.append(copy)
        return copy

    def store(source, target):
        copy = pltpu.make_async_copy(source, target, store_sems.at[len(stores)])
        copy.start()
        stores.append(copy)

    load_marks = load(marks_hbm, marks_ref)
    load_oc = load(oc_hbm, oc_ref)

    started = []

    def send(source, target, device):
        index = len(started)
        copy = pltpu.make_async_remote_copy(
            src_ref=source,
            dst_ref=target,
            send_sem=send_sems.at[index],
            recv_sem=recv_sems.at[index],
            device_id=device,
            device_id_type=MESH,
        )
        copy.start()
        started.append(copy)
        return copy

    barrier = pltpu.get_barrier_semaphore()
    peers = [y_dev(step) for step in range(1, n_y)]
    peers += [x_dev(step) for step in (1, -1, 2)]
    peers += [z_dev(step) for step in range(1, n_z)]
    peers += [sibling, after, before]
    for peer in peers:
        pl.semaphore_signal(barrier, inc=1, device_id=peer, device_id_type=MESH)

    load_x = load(x_hbm, x_ref)
    load_gain = load(enc_gain_hbm, enc_gain_ref)
    load_conv = load(conv_hbm, conv_ref)
    load_w = [
        load(dw_hbm, dw_ref),
        load(gw_hbm.at[0:width], w_all.at[0, :, 0:128]),
        load(uw_hbm.at[0:width], w_all.at[0, :, 128:256]),
    ]
    load_tail = [
        load(widen_hbm, widen_ref),
        load(main_gain_hbm, main_gain_ref),
        load(gw_hbm.at[width : 2 * width], gw_tail),
        load(uw_hbm.at[width : 2 * width], uw_tail),
    ]

    load_marks.wait()
    marks = marks_ref[...].astype(F32)
    upper = (
        lax.broadcasted_iota(jnp.int32, (rows, rows), 0)
        <= lax.broadcasted_iota(jnp.int32, (rows, rows), 1)
    ).astype(F32).astype(BF16)
    running = dot(jnp.broadcast_to(marks, (16, rows)).astype(BF16), upper)
    lead = jnp.where(running == 0.0, 1.0, 0.0).astype(BF16)
    slot_ids = lax.broadcasted_iota(jnp.int32, (CAP, rows), 0).astype(F32)
    member = jnp.where(slot_ids == running[0:1] - 1.0, 1.0, 0.0)
    chosen = (member * marks).astype(BF16)
    last_slot = jnp.where(slot_ids[:, 0:1] == running[0:1, rows - 1 : rows] - 1.0, 1.0, 0.0)
    load_oc.wait()
    lead_out[...] = dot(lead, oc_ref[...])[0:8]

    pl.semaphore_wait(barrier, len(peers))

    halo_copy = send(x_hbm.at[rows - 16 : rows], halo, after)
    lead_copy = send(lead_out, lead_in, before)
    own_sums = dot(member.astype(BF16), oc_ref[...])

    for copy in load_w:
        copy.wait()
    w_all[0, :, 256:384] = dw_ref[...].astype(F32).T.astype(BF16)

    def w_rows(slot):
        return w_all.at[slot, pl.ds(pl.multiple_of(core * half, half), half)]

    def w_part(slot, part):
        start = pl.multiple_of(core * half + part * (half // 2), half // 2)
        return w_all.at[slot, pl.ds(start, half // 2)]

    w_near = [
        send(w_rows(0), w_rows(1), x_dev(1)),
        send(w_rows(0), w_rows(2), x_dev(-1)),
    ]

    ring = {}

    def pass_on(which, direction, step):
        buffer = (in_all, cot_all)[which]
        here = Y_ROW[Y_ORDER.index(-direction * step)]
        there = Y_ROW[Y_ORDER.index(-direction * (step + 1))]
        ring[which, direction, step] = send(
            buffer.at[here : here + CAP], buffer.at[there : there + CAP], y_dev(direction)
        )

    lead_copy.wait_recv()
    carried = lead_in[0:1] * (seq < n_seq - 1).astype(F32)
    cot_all[0:CAP] = (own_sums + last_slot * carried).astype(BF16)
    pass_on(1, 1, 0)
    pass_on(1, -1, 0)

    load_gain.wait()
    load_conv.wait()
    load_x.wait()
    enc_gain = as_row(enc_gain_ref[...])
    taps = [conv_ref[tap : tap + 1, :].astype(F32) for tap in range(KW)]
    def chunk(index):
        return pl.ds(pl.multiple_of(index * CHUNK, CHUNK), CHUNK)

    def enc_norm(index, carry):
        value = x_ref[chunk(index)].astype(F32)
        inverse = lax.rsqrt(jnp.mean(value * value, axis=1, keepdims=True) + EPS)
        inv_x[chunk(index)] = inverse
        norm_x[pl.ds(pl.multiple_of(16 + index * CHUNK, 16), CHUNK)] = value * inverse * enc_gain
        return carry

    lax.fori_loop(0, rows // CHUNK, enc_norm, 0)
    halo_copy.wait_recv()
    value = halo[...].astype(F32) * (seq > 0).astype(F32)
    inverse = lax.rsqrt(jnp.mean(value * value, axis=1, keepdims=True) + EPS)
    norm_x[0:16] = value * inverse * enc_gain

    def enc_mix(index, carry):
        block = norm_x[pl.ds(pl.multiple_of(index * CHUNK, CHUNK), CHUNK + 16)]
        mixed = taps[0] * block[16:]
        for tap in range(1, KW):
            mixed = mixed + taps[tap] * block[16 - tap : 16 - tap + CHUNK]
        sigma = jax.nn.sigmoid(mixed)
        enc_out[chunk(index)] = (x_ref[chunk(index)].astype(F32) + mixed * sigma).astype(BF16)
        slope[chunk(index)] = sigma * (1.0 + mixed * (1.0 - sigma))
        return carry

    lax.fori_loop(0, rows // CHUNK, enc_mix, 0)
    in_all[0:CAP] = dot(chosen, enc_out[...]).astype(BF16)
    pass_on(0, 1, 0)
    pass_on(0, -1, 0)

    for copy in load_tail:
        copy.wait()
    widen = as_row(widen_ref[...])
    main_gain = as_row(main_gain_ref[...])
    gain_head = main_gain[:, 0:width]
    tail_vec = widen * main_gain[:, width : 2 * width]
    tail_square = jnp.sum(widen * widen, axis=1, keepdims=True)
    tail_b[...] = jnp.broadcast_to(tail_vec, (128, width)).T
    store(tail_b, tail_hbm)
    tail_gate = jnp.sum(gw_tail[...].astype(F32) * tail_b[...], axis=0, keepdims=True)
    tail_up = jnp.sum(uw_tail[...].astype(F32) * tail_b[...], axis=0, keepdims=True)
    tails[0, :, 0:128] = jnp.broadcast_to(tail_gate, (8, 128))
    tails[0, :, 128:256] = jnp.broadcast_to(tail_up, (8, 128))
    tail_copies = [
        send(tails.at[0], tails.at[1], x_dev(1)),
        send(tails.at[0], tails.at[2], x_dev(-1)),
        send(tails.at[0], tails.at[3], x_dev(2)),
    ]

    def relay(which, step):
        for direction in (1, -1):
            ring[which, direction, step - 1].wait_recv()
            pass_on(which, direction, step)

    def relay_last(which, direction):
        buffer = (in_all, cot_all)[which]
        here, there = (Y_ROW[Y_ORDER.index(rel)] for rel in (-3 * direction, 4))
        ring[which, direction, 2].wait_recv()
        ring[which, direction, 3] = send(
            buffer.at[here : here + CAP], buffer.at[there : there + CAP], y_dev(direction)
        )

    relay(1, 1)
    relay(0, 1)
    w_near[0].wait_recv()
    w_far = [send(w_part(1, 0), w_part(3, 0), x_dev(1))]
    w_near[1].wait_recv()
    w_far.append(send(w_part(2, 1), w_part(3, 1), x_dev(-1)))
    w_twin = [send(w_rows(slot), w_rows(slot), sibling) for slot in (1, 2)]
    for first, last in ((NEAR[1], FAR[0]), (FAR[1], ROWS)):
        count = last - first
        normed[first:last] = jnp.zeros((count, width), BF16)
        cot_all[first:last] = jnp.zeros((count, width), BF16)
        inv_all[first:last] = jnp.zeros((count, 1), F32)
        act_all[:, first:last] = jnp.zeros((LINE, count, 128), BF16)
        cots_all[:, first:last] = jnp.zeros((LINE, count, 256), BF16)
    relay(1, 2)
    relay(0, 2)

    def normalise(first, last):
        def block(index, carry):
            some = pl.ds(pl.multiple_of(first + index * CAP, 16), CAP)
            head = in_all[some].astype(F32)
            square = jnp.sum(head * head, axis=1, keepdims=True) + tail_square
            inverse = lax.rsqrt(square / (2 * width) + EPS)
            inv_all[some] = inverse
            normed[some] = (head * inverse * gain_head).astype(BF16)
            return carry

        lax.fori_loop(0, (last - first) // CAP, block, 0)
        tin_all[first:last] = jnp.zeros((last - first, 1), F32)

    def forward(first, last):
        def block(slot, carry):
            tail = tails[slot, 0:1, :]
            both = dot(normed[first:last], w_all[slot, :, 0:256]) + inv_all[first:last] * tail
            act_cot = dot(cot_all[first:last], w_all[slot, :, 256:384])
            gate, up = both[:, 0:128], both[:, 128:256]
            sigma = jax.nn.sigmoid(gate)
            swish = gate * sigma
            act_all[slot, first:last, :] = (swish * up).astype(BF16)
            gate_cot = (act_cot * up * sigma * (1.0 + gate * (1.0 - sigma))).astype(BF16)
            up_cot = (act_cot * swish).astype(BF16)
            cots_all[slot, first:last, 0:128] = gate_cot
            cots_all[slot, first:last, 128:256] = up_cot
            tin_all[first:last] += jnp.sum(
                gate_cot.astype(F32) * tail[:, 0:128] + up_cot.astype(F32) * tail[:, 128:256],
                axis=1,
                keepdims=True,
            )
            return carry

        lax.fori_loop(0, LINE, block, 0)

    def backward():
        def features(index, carry):
            some = pl.ds(pl.multiple_of(index * 256, 256), 256)
            total = dot_lanes(cots_all[0, 0 : FAR[1]], w_all[0, some, 0:256])
            for slot in range(1, LINE):
                total = total + dot_lanes(cots_all[slot, 0 : FAR[1]], w_all[slot, some, 0:256])
            back[0 : FAR[1], some] = total
            return carry

        lax.fori_loop(0, width // 256, features, 0)

        def block(index, carry):
            some = pl.ds(pl.multiple_of(index * 16, 16), 16)
            inverse = inv_all[some]
            unit = in_all[some].astype(F32) * inverse
            scaled = back[some] * gain_head
            inner = jnp.sum(scaled * unit, axis=1, keepdims=True) + tin_all[some] * inverse
            part_all[some] = ((scaled - unit * (inner / (2 * width))) * inverse).astype(BF16)
            return carry

        lax.fori_loop(0, FAR[1] // 16, block, 0)

    y_copies = []

    def y_send(step):
        row = Y_ROW[Y_ORDER.index(step)]
        there = Y_ORDER.index(4 if step == 4 else -step)
        y_copies.append(send(part_all.at[row : row + CAP], y_in.at[there], y_dev(step)))

    normalise(*NEAR)
    normed_t[0] = normed[0 : FAR[0]].T
    cot_t[0] = cot_all[0 : FAR[0]].T
    relay_last(1, -1)
    for copy in w_far:
        copy.wait_recv()
    w_twin.append(send(w_rows(3), w_rows(3), sibling))
    relay_last(0, 1)
    for copy in tail_copies + w_twin:
        copy.wait_recv()
    forward(*NEAR)

    def near_product(slot, carry):
        g_acc[slot, :, 0:256] = dot(normed_t[0], cots_all[slot, 0 : FAR[0]])
        g_acc[slot, :, 256:384] = dot(cot_t[0], act_all[slot, 0 : FAR[0]])
        return carry

    lax.fori_loop(0, LINE, near_product, 0)

    ring[1, 1, 2].wait_recv()
    ring[1, -1, 3].wait_recv()
    cot_t[1] = cot_all[FAR[0] : ROWS].T
    ring[0, -1, 2].wait_recv()
    ring[0, 1, 3].wait_recv()
    normalise(*FAR)
    forward(*FAR)
    normed_t[1] = normed[FAR[0] : ROWS].T

    def far_product(start, count, slot):
        some = pl.ds(pl.multiple_of(start, 128), count)
        wide = dot(normed_t[1, some], cots_all[slot, FAR[0] : ROWS])
        narrow = dot(cot_t[1, some], act_all[slot, FAR[0] : ROWS])
        return wide + g_acc[slot, some, 0:256], narrow + g_acc[slot, some, 256:384]

    def theirs(slot, carry):
        wide, narrow = far_product((1 - core) * half, half, slot)
        g_out[slot, :, 0:256] = wide.astype(BF16)
        g_out[slot, :, 256:384] = narrow.astype(BF16)
        return carry

    lax.fori_loop(0, LINE, theirs, 0)

    def cut(part):
        return slice(PIECES[part], PIECES[part + 1])

    def halves(part):
        first, last = PIECES[part], PIECES[part + 1]
        mid = (first + last) // 2
        return slice(first, mid), slice(mid, last)

    pair_copies = [
        send(g_out.at[:, cut(part)], g_in.at[:, cut(part)], sibling) for part in range(PARTS)
    ]

    def ours(slot, carry):
        wide, narrow = far_product(core * half, half, slot)
        some = pl.ds(pl.multiple_of(core * half, half), half)
        g_acc[slot, some, 0:256] = wide
        g_acc[slot, some, 256:384] = narrow
        return carry

    lax.fori_loop(0, LINE, ours, 0)

    x_first, x_second, z_first, z_near, z_far, last_copies = ({} for _ in range(6))

    def rows_of(which, part):
        count = PIECES[part + 1] - PIECES[part]
        return pl.ds(pl.multiple_of(which * half + PIECES[part], 128), count)

    def own_rows(part):
        return rows_of(core, part)

    def x_start(part):
        pair_copies[part].wait_recv()

        def add(slot, carry):
            total = g_acc[slot, own_rows(part)] + g_in[slot, cut(part)].astype(F32)
            g_x[slot, cut(part)] = total.astype(BF16)
            return carry

        lax.fori_loop(1, LINE, add, 0)
        low, high = halves(part)
        x_first[part] = (
            send(g_x.at[3, low], x_opp.at[low], x_dev(1)),
            send(g_x.at[3, high], x_opp.at[high], x_dev(-1)),
            send(g_x.at[2, high], x_in.at[0, high], x_dev(1)),
            send(g_x.at[1, low], x_in.at[1, low], x_dev(-1)),
        )

    def x_relay(part):
        low, high = halves(part)
        x_first[part][0].wait_recv()
        g_x[2, low] = (g_x[2, low].astype(F32) + x_opp[low].astype(F32)).astype(BF16)
        right = send(g_x.at[2, low], x_in.at[0, low], x_dev(1))
        x_first[part][1].wait_recv()
        g_x[1, high] = (g_x[1, high].astype(F32) + x_opp[high].astype(F32)).astype(BF16)
        left = send(g_x.at[1, high], x_in.at[1, high], x_dev(-1))
        x_second[part] = (right, left)

    def z_cut(part, step, base=0):
        count = (PIECES[part + 1] - PIECES[part]) // n_z
        start = base + PIECES[part] + lax.rem(z + step + n_z, n_z) * count
        return pl.ds(pl.multiple_of(start, 16), count)

    def z_slot(part):
        return slice(PIECES[part] // n_z, PIECES[part + 1] // n_z)

    def z_start(part):
        for copy in x_first[part][2:] + x_second[part]:
            copy.wait_recv()
        h_all[cut(part)] = (
            g_acc[0, own_rows(part)]
            + g_in[0, cut(part)].astype(F32)
            + x_in[0, cut(part)].astype(F32)
            + x_in[1, cut(part)].astype(F32)
        ).astype(BF16)
        z_first[part] = [
            send(h_all.at[z_cut(part, step)], z_in.at[index, z_slot(part)], z_dev(step))
            for index, step in enumerate((4, 3, -3, 2, -2, 1, -1))
        ]

    def z_final(part, step):
        return z_cut(part, step, core * half)

    def z_sum(part):
        total = h_all[z_cut(part, 0)].astype(F32)
        for index, copy in enumerate(z_first[part]):
            copy.wait_recv()
            total = total + z_in[index, z_slot(part)].astype(F32)
        final[z_final(part, 0)] = total.astype(BF16)
        mine = final.at[z_final(part, 0)]
        z_near[part] = [send(mine, mine, z_dev(step)) for step in (2, -2, 1, -1)]

    def z_spread(part):
        copies = []
        for side, step in ((0, 1), (1, -1)):
            z_near[part][side].wait_recv()
            theirs = final.at[z_final(part, -2 * step)]
            copies.append(send(theirs, theirs, z_dev(step)))
            if side == part:
                copies.append(send(theirs, theirs, z_dev(2 * step)))
        z_far[part] = copies

    def z_end(part):
        for copy in z_near[part][2:] + z_far[part]:
            copy.wait_recv()
        mine = final.at[own_rows(part)]
        last_copies[part] = send(mine, mine, sibling)

    x_start(0)
    x_start(1)
    backward()
    for step in (4, 3, -3, 2, -2, 1, -1):
        y_send(step)
    x_relay(0)
    x_relay(1)

    def tail_rows(slot, carry):
        row = jnp.sum(cots_all[slot].astype(F32) * inv_all[...], axis=0, keepdims=True)
        v_out[slot] = jnp.broadcast_to(row, (8, 256))
        return carry

    lax.fori_loop(0, LINE, tail_rows, 0)
    v_copies = [
        send(v_out.at[1], v_in.at[0], x_dev(-1)),
        send(v_out.at[2], v_in.at[1], x_dev(1)),
        send(v_out.at[3], v_in.at[2], x_dev(2)),
    ]
    z_start(0)

    for copy in v_copies:
        copy.wait_recv()
    v_step[0] = v_out[0] + v_in[0] + v_in[1] + v_in[2]
    v_peers = [sibling] + [
        {"dp": (z + size - 2 * size * ((z // size) % 2)) * 2 + core} for size in (1, 2, 4)
    ]

    def v_send(index):
        return send(v_step.at[index], v_other.at[index], v_peers[index])

    def v_join(index, copy):
        copy.wait_recv()
        v_step[index + 1] = v_step[index] + v_other[index]

    v_copy = v_send(0)
    z_start(1)
    v_join(0, v_copy)
    v_copy = v_send(1)
    z_sum(0)
    v_join(1, v_copy)
    v_copy = v_send(2)
    z_spread(0)
    v_join(2, v_copy)
    v_copy = v_send(3)
    z_sum(1)
    z_end(0)
    z_spread(1)
    early = len(started)

    for copy in y_copies:
        copy.wait_recv()
    widen_cot = part_all[0:CAP].astype(F32)
    for index in range(1, n_y):
        widen_cot = widen_cot + y_in[index].astype(F32)
    spread = dot_rows(chosen, cot_all[0:CAP]) + dot_rows(chosen, widen_cot.astype(BF16))
    ecot[...] = oc_ref[...].astype(F32) + spread
    g_mix[0:rows] = ecot[...] * slope[...]
    edge_copy = send(g_mix.at[0:8], edge, before)

    edge_copy.wait_recv()
    g_mix[rows : rows + 8] = edge[...] * (seq < n_seq - 1).astype(F32)

    def enc_back(index, carry):
        block = g_mix[pl.ds(pl.multiple_of(index * CHUNK, CHUNK), CHUNK + 8)]
        grad = taps[0] * block[0:CHUNK]
        for tap in range(1, KW):
            grad = grad + taps[tap] * block[tap : tap + CHUNK]
        grad = grad * enc_gain
        value = x_ref[chunk(index)].astype(F32)
        inverse = inv_x[chunk(index)]
        inner = jnp.mean(grad * value, axis=1, keepdims=True) * (inverse * inverse)
        bg_ref[chunk(index)] = (ecot[chunk(index)] + (grad - value * inner) * inverse).astype(BF16)
        return carry

    lax.fori_loop(0, rows // CHUNK, enc_back, 0)
    store(bg_ref, bg_hbm)

    v_join(3, v_copy)
    store(v_step.at[4], v_hbm)

    for copy in started[:early]:
        copy.wait_send()
    z_end(1)
    for part in range(PARTS):
        store(final.at[own_rows(part)], final_hbm.at[own_rows(part)])
    for part in range(PARTS):
        last_copies[part].wait_recv()
        store(final.at[rows_of(1 - core, part)], final_hbm.at[rows_of(1 - core, part)])
    for copy in started[early:]:
        copy.wait_send()
    for copy in stores:
        copy.wait()


def finish(
    bg_hbm, final_hbm, tail_hbm, v_hbm, bg_out, gg_out, ug_out, dg_out, bg, final, tail_b, v_ref, gg, ug, dg, sems
):
    width = final.shape[0]
    copies = []

    def copy(source, target):
        step = pltpu.make_async_copy(source, target, sems.at[len(copies)])
        step.start()
        copies.append(step)
        return step

    load_final = copy(final_hbm, final)
    load_tail = copy(tail_hbm, tail_b)
    load_v = copy(v_hbm, v_ref)
    load_bg = copy(bg_hbm, bg)
    head, tail = slice(0, width), slice(width, 2 * width)
    load_final.wait()
    gg[head] = final[:, 0:128].astype(F32)
    copy(gg.at[head], gg_out.at[head])
    ug[head] = final[:, 128:256].astype(F32)
    copy(ug.at[head], ug_out.at[head])
    load_bg.wait()
    copy(bg, bg_out)
    load_tail.wait()
    load_v.wait()
    gg[tail] = tail_b[...] * v_ref[0:1, 0:128]
    copy(gg.at[tail], gg_out.at[tail])
    ug[tail] = tail_b[...] * v_ref[0:1, 128:256]
    copy(ug.at[tail], ug_out.at[tail])
    dg[...] = final[:, 256:384].astype(F32).T
    copy(dg, dg_out)
    for step in copies[4:]:
        step.wait()


def body(
    bytes_in,
    flags,
    enc_gain,
    conv_weight,
    widen,
    main_gain,
    gate_weight,
    up_weight,
    down_weight,
    out_cot,
):
    rows, width = bytes_in.shape[1:]
    n_y = lax.axis_size("seq") // LINE
    n_z = lax.axis_size("dp") // 2
    assert n_y == len(Y_ORDER)
    half = width // 2
    hbm = pl.BlockSpec(memory_space=pltpu.HBM)
    scratch = [
        ((rows, width), BF16),
        ((width, 384), BF16),
        ((width, 128), F32),
        ((rows, width), BF16),
        ((1, rows), jnp.int32),
        ((8, width // 8), BF16),
        ((KW, width), BF16),
        ((8, width // 8), BF16),
        ((16, width // 8), BF16),
        ((width, 128), BF16),
        ((width, 128), BF16),
        ((128, width), BF16),
        ((rows, width), BF16),
        ((LINE, width, 384), BF16),
        ((LINE, 8, 256), F32),
        ((16, width), BF16),
        ((8, width), F32),
        ((8, width), F32),
        ((rows + 16, width), F32),
        ((rows, 1), F32),
        ((rows, width), BF16),
        ((rows, width), F32),
        ((ROWS, width), BF16),
        ((ROWS, width), BF16),
        ((ROWS, width), BF16),
        ((2, width, ROWS // 2), BF16),
        ((2, width, ROWS // 2), BF16),
        ((ROWS, 1), F32),
        ((ROWS, 1), F32),
        ((LINE, ROWS, 128), BF16),
        ((LINE, ROWS, 256), BF16),
        ((ROWS, width), F32),
        ((ROWS, width), BF16),
        ((n_y, CAP, width), BF16),
        ((LINE, 8, 256), F32),
        ((LINE - 1, 8, 256), F32),
        ((5, 8, 256), F32),
        ((4, 8, 256), F32),
        ((LINE, width, 384), F32),
        ((LINE, half, 384), BF16),
        ((LINE, half, 384), BF16),
        ((LINE, half, 384), BF16),
        ((half, 384), BF16),
        ((2, half, 384), BF16),
        ((half, 384), BF16),
        ((n_z - 1, half // n_z, 384), BF16),
        ((rows, width), F32),
        ((rows + 8, width), F32),
        ((8, width), F32),
    ]
    sums = pl.pallas_call(
        kernel,
        out_shape=(
            jax.ShapeDtypeStruct((rows, width), BF16),
            jax.ShapeDtypeStruct((width, 384), BF16),
            jax.ShapeDtypeStruct((width, 128), F32),
            jax.ShapeDtypeStruct((8, 256), F32),
        ),
        in_specs=[hbm] * 10,
        out_specs=[hbm] * 4,
        scratch_shapes=[pltpu.VMEM(shape, kind) for shape, kind in scratch]
        + [
            pltpu.SemaphoreType.DMA((12,)),
            pltpu.SemaphoreType.DMA((9,)),
            pltpu.SemaphoreType.DMA((96,)),
            pltpu.SemaphoreType.DMA((96,)),
        ],
        compiler_params=pltpu.CompilerParams(
            collective_id=0, has_side_effects=True, vmem_limit_bytes=60 * 1024 * 1024
        ),
    )(
        bytes_in[0],
        flags,
        enc_gain.reshape(8, width // 8),
        conv_weight,
        widen.reshape(8, width // 8),
        main_gain.reshape(16, width // 8),
        gate_weight,
        up_weight,
        down_weight,
        out_cot[0],
    )
    outs = pl.pallas_call(
        finish,
        out_shape=(
            jax.ShapeDtypeStruct((rows, width), BF16),
            jax.ShapeDtypeStruct((2 * width, 128), F32),
            jax.ShapeDtypeStruct((2 * width, 128), F32),
            jax.ShapeDtypeStruct((128, width), F32),
        ),
        in_specs=[hbm] * 4,
        out_specs=[hbm] * 4,
        scratch_shapes=[
            pltpu.VMEM((rows, width), BF16),
            pltpu.VMEM((width, 384), BF16),
            pltpu.VMEM((width, 128), F32),
            pltpu.VMEM((8, 256), F32),
            pltpu.VMEM((2 * width, 128), F32),
            pltpu.VMEM((2 * width, 128), F32),
            pltpu.VMEM((128, width), F32),
            pltpu.SemaphoreType.DMA((10,)),
        ],
        compiler_params=pltpu.CompilerParams(vmem_limit_bytes=60 * 1024 * 1024),
    )(*sums)
    return (outs[0][None], outs[1], outs[2], outs[3])


def solution(mesh):
    in_specs = (
        P("dp", "seq", None),
        P("dp", "seq"),
        P(),
        P(),
        P(),
        P(),
        P(None, "seq"),
        P(None, "seq"),
        P("seq", None),
        P("dp", "seq", None),
    )
    out_specs = (P("dp", "seq", None), P(None, "seq"), P(None, "seq"), P("seq", None))
    return jax.shard_map(body, mesh=mesh, in_specs=in_specs, out_specs=out_specs, check_vma=False)
```

```python
import jax
import jax.numpy as jnp
from jax import lax
from jax.experimental import pallas as pl
from jax.experimental.pallas import tpu as pltpu
from jax.sharding import PartitionSpec as P

MESH = pl.DeviceIdType.MESH
F32 = jnp.float32
BF16 = jnp.bfloat16

KW = 4
CAP = 48
EPS = 1e-05
LINE = 4
PIECES = (0, 256, 384, 512)
PARTS = len(PIECES) - 1
CHUNK = 32

Y_ORDER = (0, -1, 1, -2, 2, -3, 3, 4)
Y_ROW = (0, 48, 96, 144, 192, 256, 304, 352)
NEAR = (0, 240)
FAR = (256, 400)
ROWS = 512
X_ORDER = (0, -1, 1, 2)


def dot(left, right):
    return jnp.dot(left, right, preferred_element_type=F32)


def dot_rows(left, right):
    return lax.dot_general(left, right, (((0,), (0,)), ((), ())), preferred_element_type=F32)


def dot_lanes(left, right):
    return lax.dot_general(left, right, (((1,), (1,)), ((), ())), preferred_element_type=F32)


def as_row(value):
    value = value.astype(F32)
    return jnp.concatenate([value[i : i + 1] for i in range(value.shape[0])], axis=1)


def kernel(
    x_hbm,
    marks_hbm,
    enc_gain_hbm,
    conv_hbm,
    widen_hbm,
    main_gain_hbm,
    gw_hbm,
    uw_hbm,
    dw_hbm,
    oc_hbm,
    bg_hbm,
    final_hbm,
    tail_hbm,
    v_hbm,
    bg_ref,
    final,
    tail_b,
    v_ref,
    x_ref,
    marks_ref,
    enc_gain_ref,
    conv_ref,
    widen_ref,
    main_gain_ref,
    gw_tail,
    uw_tail,
    dw_ref,
    oc_ref,
    w_all,
    tails,
    halo,
    lead_out,
    lead_in,
    norm_x,
    inv_x,
    enc_out,
    slope,
    in_all,
    cot_all,
    normed,
    normed_t,
    cot_t,
    inv_all,
    tin_all,
    act_all,
    cots_all,
    back,
    part_all,
    y_in,
    v_out,
    v_in,
    v_pair,
    v_sib,
    v_all,
    g_acc,
    g_out,
    g_in,
    g_x,
    x_opp,
    x_in,
    h_all,
    z_in,
    ecot,
    g_mix,
    edge,
    load_sems,
    store_sems,
    send_sems,
    recv_sems,
):
    n_seq = lax.axis_size("seq")
    n_y = n_seq // LINE
    n_z = lax.axis_size("dp") // 2
    dp = lax.axis_index("dp")
    seq = lax.axis_index("seq")
    z, core = dp // 2, dp % 2
    y, x = seq // LINE, seq % LINE
    rows, width = x_ref.shape
    half = width // 2

    def y_dev(step):
        return {"seq": lax.rem(y + step + n_y, n_y) * LINE + x}

    def x_dev(step):
        return {"seq": y * LINE + lax.rem(x + step + LINE, LINE)}

    def z_dev(step):
        return {"dp": lax.rem(z + step + n_z, n_z) * 2 + core}

    sibling = {"dp": z * 2 + 1 - core}
    after = {"seq": lax.rem(seq + 1, n_seq)}
    before = {"seq": lax.rem(seq + n_seq - 1, n_seq)}

    loads = []
    stores = []

    def load(source, target):
        copy = pltpu.make_async_copy(source, target, load_sems.at[len(loads)])
        copy.start()
        loads.append(copy)
        return copy

    def store(source, target):
        copy = pltpu.make_async_copy(source, target, store_sems.at[len(stores)])
        copy.start()
        stores.append(copy)

    load_marks = load(marks_hbm, marks_ref)
    load_oc = load(oc_hbm, oc_ref)

    started = []

    def send(source, target, device):
        index = len(started)
        copy = pltpu.make_async_remote_copy(
            src_ref=source,
            dst_ref=target,
            send_sem=send_sems.at[index],
            recv_sem=recv_sems.at[index],
            device_id=device,
            device_id_type=MESH,
        )
        copy.start()
        started.append(copy)
        return copy

    barrier = pltpu.get_barrier_semaphore()
    peers = [y_dev(step) for step in range(1, n_y)]
    peers += [x_dev(step) for step in (1, -1, 2)]
    peers += [z_dev(step) for step in range(1, n_z)]
    peers += [sibling, after, before]
    for peer in peers:
        pl.semaphore_signal(barrier, inc=1, device_id=peer, device_id_type=MESH)

    load_x = load(x_hbm, x_ref)
    load_gain = load(enc_gain_hbm, enc_gain_ref)
    load_conv = load(conv_hbm, conv_ref)
    load_w = [
        load(dw_hbm, dw_ref),
        load(gw_hbm.at[0:width], w_all.at[0, :, 0:128]),
        load(uw_hbm.at[0:width], w_all.at[0, :, 128:256]),
    ]
    load_tail = [
        load(widen_hbm, widen_ref),
        load(main_gain_hbm, main_gain_ref),
        load(gw_hbm.at[width : 2 * width], gw_tail),
        load(uw_hbm.at[width : 2 * width], uw_tail),
    ]

    load_marks.wait()
    marks = marks_ref[...].astype(F32)
    upper = (
        lax.broadcasted_iota(jnp.int32, (rows, rows), 0)
        <= lax.broadcasted_iota(jnp.int32, (rows, rows), 1)
    ).astype(F32).astype(BF16)
    running = dot(jnp.broadcast_to(marks, (16, rows)).astype(BF16), upper)
    lead = jnp.where(running == 0.0, 1.0, 0.0).astype(BF16)
    slot_ids = lax.broadcasted_iota(jnp.int32, (CAP, rows), 0).astype(F32)
    member = jnp.where(slot_ids == running[0:1] - 1.0, 1.0, 0.0)
    chosen = (member * marks).astype(BF16)
    last_slot = jnp.where(slot_ids[:, 0:1] == running[0:1, rows - 1 : rows] - 1.0, 1.0, 0.0)
    load_oc.wait()
    lead_out[...] = dot(lead, oc_ref[...])[0:8]

    pl.semaphore_wait(barrier, len(peers))

    halo_copy = send(x_hbm.at[rows - 16 : rows], halo, after)
    lead_copy = send(lead_out, lead_in, before)
    own_sums = dot(member.astype(BF16), oc_ref[...])

    for copy in load_w:
        copy.wait()
    w_all[0, :, 256:384] = dw_ref[...].astype(F32).T.astype(BF16)

    def w_rows(slot, part):
        start = pl.multiple_of(core * half + part * (half // 2), half // 2)
        return w_all.at[slot, pl.ds(start, half // 2)]

    w_right = [None, None]
    w_left = [None, None]

    def w_send(part):
        w_right[part] = send(w_rows(0, part), w_rows(1, part), x_dev(1))
        w_left[1 - part] = send(w_rows(0, 1 - part), w_rows(2, 1 - part), x_dev(-1))

    w_send(0)

    ring = {}

    def pass_on(which, direction, step):
        buffer = (in_all, cot_all)[which]
        here = Y_ROW[Y_ORDER.index(-direction * step)]
        there = Y_ROW[Y_ORDER.index(-direction * (step + 1))]
        ring[which, direction, step] = send(
            buffer.at[here : here + CAP], buffer.at[there : there + CAP], y_dev(direction)
        )

    load_gain.wait()
    load_conv.wait()
    load_x.wait()
    enc_gain = as_row(enc_gain_ref[...])
    taps = [conv_ref[tap : tap + 1, :].astype(F32) for tap in range(KW)]
    for r in range(0, rows, CHUNK):
        value = x_ref[r : r + CHUNK].astype(F32)
        inverse = lax.rsqrt(jnp.mean(value * value, axis=1, keepdims=True) + EPS)
        inv_x[r : r + CHUNK] = inverse
        norm_x[16 + r : 16 + r + CHUNK] = value * inverse * enc_gain
    lead_copy.wait_recv()
    carried = lead_in[0:1] * (seq < n_seq - 1).astype(F32)
    cot_all[0:CAP] = (own_sums + last_slot * carried).astype(BF16)
    pass_on(1, 1, 0)
    pass_on(1, -1, 0)

    halo_copy.wait_recv()
    value = halo[...].astype(F32) * (seq > 0).astype(F32)
    inverse = lax.rsqrt(jnp.mean(value * value, axis=1, keepdims=True) + EPS)
    norm_x[0:16] = value * inverse * enc_gain
    for r in range(0, rows, CHUNK):
        mixed = taps[0] * norm_x[16 + r : 16 + r + CHUNK]
        for tap in range(1, KW):
            mixed = mixed + taps[tap] * norm_x[16 + r - tap : 16 + r - tap + CHUNK]
        sigma = jax.nn.sigmoid(mixed)
        enc_out[r : r + CHUNK] = (x_ref[r : r + CHUNK].astype(F32) + mixed * sigma).astype(BF16)
        slope[r : r + CHUNK] = sigma * (1.0 + mixed * (1.0 - sigma))
    in_all[0:CAP] = dot(chosen, enc_out[...]).astype(BF16)
    pass_on(0, 1, 0)
    pass_on(0, -1, 0)
    w_send(1)

    w_twin = []

    def swap(slot, part):
        w_twin.append(send(w_rows(slot, part), w_rows(slot, part), sibling))

    for copy in load_tail:
        copy.wait()
    widen = as_row(widen_ref[...])
    main_gain = as_row(main_gain_ref[...])
    gain_head = main_gain[:, 0:width]
    tail_vec = widen * main_gain[:, width : 2 * width]
    tail_square = jnp.sum(widen * widen, axis=1, keepdims=True)
    tail_b[...] = jnp.broadcast_to(tail_vec, (128, width)).T
    store(tail_b, tail_hbm)
    tail_gate = jnp.sum(gw_tail[...].astype(F32) * tail_b[...], axis=0, keepdims=True)
    tail_up = jnp.sum(uw_tail[...].astype(F32) * tail_b[...], axis=0, keepdims=True)
    tails[0, :, 0:128] = jnp.broadcast_to(tail_gate, (8, 128))
    tails[0, :, 128:256] = jnp.broadcast_to(tail_up, (8, 128))
    tail_copies = [
        send(tails.at[0], tails.at[1], x_dev(1)),
        send(tails.at[0], tails.at[2], x_dev(-1)),
        send(tails.at[0], tails.at[3], x_dev(2)),
    ]

    def relay(which, step):
        for direction in (1, -1):
            ring[which, direction, step - 1].wait_recv()
            pass_on(which, direction, step)

    def relay_last(which):
        buffer = (in_all, cot_all)[which]
        there = Y_ROW[Y_ORDER.index(4)]
        for direction in (1, -1):
            ring[which, direction, 2].wait_recv()
            here = Y_ROW[Y_ORDER.index(-3 * direction)]
            lanes = slice(0, half) if direction == 1 else slice(half, width)
            ring[which, direction, 3] = send(
                buffer.at[here : here + CAP, lanes],
                buffer.at[there : there + CAP, lanes],
                y_dev(direction),
            )

    relay(1, 1)
    relay(0, 1)
    w_right[0].wait_recv()
    w_far_a = send(w_rows(1, 0), w_rows(3, 0), x_dev(1))
    w_left[1].wait_recv()
    w_far_b = send(w_rows(2, 1), w_rows(3, 1), x_dev(-1))
    swap(1, 0)
    swap(2, 1)
    for first, last in ((NEAR[1], FAR[0]), (FAR[1], ROWS)):
        count = last - first
        normed[first:last] = jnp.zeros((count, width), BF16)
        cot_all[first:last] = jnp.zeros((count, width), BF16)
        inv_all[first:last] = jnp.zeros((count, 1), F32)
        act_all[:, first:last] = jnp.zeros((LINE, count, 128), BF16)
        cots_all[:, first:last] = jnp.zeros((LINE, count, 256), BF16)
    relay(1, 2)
    relay(0, 2)
    w_right[1].wait_recv()
    swap(1, 1)
    w_left[0].wait_recv()
    swap(2, 0)

    def normalise(first, last):
        for r in range(first, last, CAP):
            head = in_all[r : r + CAP].astype(F32)
            square = jnp.sum(head * head, axis=1, keepdims=True) + tail_square
            inverse = lax.rsqrt(square / (2 * width) + EPS)
            inv_all[r : r + CAP] = inverse
            normed[r : r + CAP] = (head * inverse * gain_head).astype(BF16)
        tin_all[first:last] = jnp.zeros((last - first, 1), F32)

    def forward(first, last, low, high):
        def block(slot, carry):
            tail = tails[slot, 0:1, :]
            both = dot(normed[first:last], w_all[slot, :, 0:256]) + inv_all[first:last] * tail
            act_cot = dot(cot_all[first:last], w_all[slot, :, 256:384])
            gate, up = both[:, 0:128], both[:, 128:256]
            sigma = jax.nn.sigmoid(gate)
            swish = gate * sigma
            act_all[slot, first:last, :] = (swish * up).astype(BF16)
            gate_cot = (act_cot * up * sigma * (1.0 + gate * (1.0 - sigma))).astype(BF16)
            up_cot = (act_cot * swish).astype(BF16)
            cots_all[slot, first:last, 0:128] = gate_cot
            cots_all[slot, first:last, 128:256] = up_cot
            tin_all[first:last] += jnp.sum(
                gate_cot.astype(F32) * tail[:, 0:128] + up_cot.astype(F32) * tail[:, 128:256],
                axis=1,
                keepdims=True,
            )
            return carry

        lax.fori_loop(low, high, block, 0)

    def backward(first, last):
        def block(slot, carry):
            back[first:last] += dot_lanes(cots_all[slot, first:last], w_all[slot, :, 0:256])
            return carry

        back[first:last] = dot_lanes(cots_all[0, first:last], w_all[0, :, 0:256])
        lax.fori_loop(1, LINE, block, 0)
        for r in range(first, last, CAP):
            inverse = inv_all[r : r + CAP]
            unit = in_all[r : r + CAP].astype(F32) * inverse
            scaled = back[r : r + CAP] * gain_head
            inner = jnp.sum(scaled * unit, axis=1, keepdims=True) + tin_all[r : r + CAP] * inverse
            part_all[r : r + CAP] = (
                (scaled - unit * (inner / (2 * width))) * inverse
            ).astype(BF16)

    y_copies = []

    def y_send(step):
        row = Y_ROW[Y_ORDER.index(step)]
        there = Y_ORDER.index(4 if step == 4 else -step)
        y_copies.append(send(part_all.at[row : row + CAP], y_in.at[there], y_dev(step)))

    normalise(*NEAR)
    for copy in tail_copies + w_twin:
        copy.wait_recv()
    forward(*NEAR, 0, LINE - 1)
    relay_last(1)
    normed_t[0] = normed[0 : FAR[0]].T
    cot_t[0] = cot_all[0 : FAR[0]].T
    first_twins = len(w_twin)
    w_far_a.wait_recv()
    swap(3, 0)
    w_far_b.wait_recv()
    swap(3, 1)
    relay_last(0)
    for copy in w_twin[first_twins:]:
        copy.wait_recv()
    forward(*NEAR, LINE - 1, LINE)

    def near_product(slot, carry):
        g_acc[slot, :, 0:256] = dot(normed_t[0], cots_all[slot, 0 : FAR[0]])
        g_acc[slot, :, 256:384] = dot(cot_t[0], act_all[slot, 0 : FAR[0]])
        return carry

    lax.fori_loop(0, LINE, near_product, 0)

    for direction in (1, -1):
        ring[1, direction, 3].wait_recv()
    cot_t[1] = cot_all[FAR[0] : ROWS].T
    for direction in (1, -1):
        ring[0, direction, 3].wait_recv()
    normalise(*FAR)
    forward(*FAR, 0, LINE)
    normed_t[1] = normed[FAR[0] : ROWS].T

    def far_product(start, count, slot):
        some = pl.ds(pl.multiple_of(start, 128), count)
        wide = dot(normed_t[1, some], cots_all[slot, FAR[0] : ROWS])
        narrow = dot(cot_t[1, some], act_all[slot, FAR[0] : ROWS])
        return wide + g_acc[slot, some, 0:256], narrow + g_acc[slot, some, 256:384]

    def theirs(low, high):
        def block(slot, carry):
            wide, narrow = far_product((1 - core) * half + low, high - low, slot)
            g_out[slot, low:high, 0:256] = wide.astype(BF16)
            g_out[slot, low:high, 256:384] = narrow.astype(BF16)
            return carry

        lax.fori_loop(0, LINE, block, 0)

    def cut(part):
        return slice(PIECES[part], PIECES[part + 1])

    def halves(part):
        first, last = PIECES[part], PIECES[part + 1]
        mid = (first + last) // 2
        return slice(first, mid), slice(mid, last)

    def pair(part):
        return send(g_out.at[:, cut(part)], g_in.at[:, cut(part)], sibling)

    theirs(0, PIECES[1])
    pair_copies = [pair(0)]
    theirs(PIECES[1], half)
    pair_copies += [pair(part) for part in range(1, PARTS)]

    def ours(slot, carry):
        wide, narrow = far_product(core * half, half, slot)
        some = pl.ds(pl.multiple_of(core * half, half), half)
        g_acc[slot, some, 0:256] = wide
        g_acc[slot, some, 256:384] = narrow
        return carry

    lax.fori_loop(0, LINE, ours, 0)
    backward(*NEAR)

    x_first, x_second, z_first, z_near, z_far, last_copies = ({} for _ in range(6))

    def rows_of(which, part):
        count = PIECES[part + 1] - PIECES[part]
        return pl.ds(pl.multiple_of(which * half + PIECES[part], 128), count)

    def own_rows(part):
        return rows_of(core, part)

    def x_start(part):
        pair_copies[part].wait_recv()

        def add(slot, carry):
            total = g_acc[slot, own_rows(part)] + g_in[slot, cut(part)].astype(F32)
            g_x[slot, cut(part)] = total.astype(BF16)
            return carry

        lax.fori_loop(1, LINE, add, 0)
        low, high = halves(part)
        x_first[part] = (
            send(g_x.at[3, low], x_opp.at[low], x_dev(1)),
            send(g_x.at[3, high], x_opp.at[high], x_dev(-1)),
            send(g_x.at[2, high], x_in.at[0, high], x_dev(1)),
            send(g_x.at[1, low], x_in.at[1, low], x_dev(-1)),
        )

    def x_relay(part):
        low, high = halves(part)
        x_first[part][0].wait_recv()
        g_x[2, low] = (g_x[2, low].astype(F32) + x_opp[low].astype(F32)).astype(BF16)
        right = send(g_x.at[2, low], x_in.at[0, low], x_dev(1))
        x_first[part][1].wait_recv()
        g_x[1, high] = (g_x[1, high].astype(F32) + x_opp[high].astype(F32)).astype(BF16)
        left = send(g_x.at[1, high], x_in.at[1, high], x_dev(-1))
        x_second[part] = (right, left)

    def z_cut(part, step, base=0):
        count = (PIECES[part + 1] - PIECES[part]) // n_z
        start = base + PIECES[part] + lax.rem(z + step + n_z, n_z) * count
        return pl.ds(pl.multiple_of(start, 16), count)

    def z_slot(part):
        return slice(PIECES[part] // n_z, PIECES[part + 1] // n_z)

    def z_start(part):
        for copy in x_first[part][2:] + x_second[part]:
            copy.wait_recv()
        h_all[cut(part)] = (
            g_acc[0, own_rows(part)]
            + g_in[0, cut(part)].astype(F32)
            + x_in[0, cut(part)].astype(F32)
            + x_in[1, cut(part)].astype(F32)
        ).astype(BF16)
        z_first[part] = [
            send(h_all.at[z_cut(part, step)], z_in.at[index, z_slot(part)], z_dev(step))
            for index, step in enumerate((4, 3, -3, 2, -2, 1, -1))
        ]

    def z_final(part, step):
        return z_cut(part, step, core * half)

    def z_sum(part):
        total = h_all[z_cut(part, 0)].astype(F32)
        for index, copy in enumerate(z_first[part]):
            copy.wait_recv()
            total = total + z_in[index, z_slot(part)].astype(F32)
        final[z_final(part, 0)] = total.astype(BF16)
        mine = final.at[z_final(part, 0)]
        steps = (2, -2, 1, -1) if part < PARTS - 1 else (4, 3, -3, 2, -2, 1, -1)
        z_near[part] = [send(mine, mine, z_dev(step)) for step in steps]

    def z_spread(part):
        copies = []
        for side, step in ((0, 1), (1, -1)):
            z_near[part][side].wait_recv()
            theirs = final.at[z_final(part, -2 * step)]
            copies.append(send(theirs, theirs, z_dev(step)))
            if side == min(part, 1):
                copies.append(send(theirs, theirs, z_dev(2 * step)))
        z_far[part] = copies

    def z_end(part):
        waits = z_near[part][2:] + z_far[part] if part < PARTS - 1 else z_near[part]
        for copy in waits:
            copy.wait_recv()
        mine = final.at[own_rows(part)]
        last_copies[part] = send(mine, mine, sibling)

    x_start(0)
    x_start(1)
    for step in (2, -2):
        y_send(step)
    backward(*FAR)
    x_relay(0)
    x_start(2)
    for step in (4, 3, -3, 1, -1):
        y_send(step)
    x_relay(1)

    def tail_rows(slot, carry):
        row = jnp.sum(cots_all[slot].astype(F32) * inv_all[...], axis=0, keepdims=True)
        v_out[slot] = jnp.broadcast_to(row, (8, 256))
        return carry

    lax.fori_loop(0, LINE, tail_rows, 0)
    v_copies = [
        send(v_out.at[1], v_in.at[0], x_dev(-1)),
        send(v_out.at[2], v_in.at[1], x_dev(1)),
        send(v_out.at[3], v_in.at[2], x_dev(2)),
    ]
    x_relay(2)
    z_start(0)

    for copy in v_copies:
        copy.wait_recv()
    v_pair[...] = v_out[0] + v_in[0] + v_in[1] + v_in[2]
    v_swap = send(v_pair, v_sib, sibling)

    z_start(1)
    v_swap.wait_recv()
    v_all[z] = v_pair[...] + v_sib[...]
    v_spread = [send(v_all.at[z], v_all.at[z], z_dev(step)) for step in range(1, n_z)]
    z_sum(0)
    z_start(2)
    z_sum(1)
    z_spread(0)
    z_sum(2)
    z_spread(1)
    early = len(started)

    for copy in y_copies:
        copy.wait_recv()
    widen_cot = part_all[0:CAP].astype(F32)
    for index in range(1, n_y):
        widen_cot = widen_cot + y_in[index].astype(F32)
    spread = dot_rows(chosen, cot_all[0:CAP]) + dot_rows(chosen, widen_cot.astype(BF16))
    ecot[...] = oc_ref[...].astype(F32) + spread
    for r in range(0, rows, CHUNK):
        g_mix[r : r + CHUNK] = ecot[r : r + CHUNK] * slope[r : r + CHUNK]
    edge_copy = send(g_mix.at[0:8], edge, before)

    z_end(0)

    edge_copy.wait_recv()
    g_mix[rows : rows + 8] = edge[...] * (seq < n_seq - 1).astype(F32)
    for r in range(0, rows, CHUNK):
        grad = taps[0] * g_mix[r : r + CHUNK]
        for tap in range(1, KW):
            grad = grad + taps[tap] * g_mix[r + tap : r + tap + CHUNK]
        grad = grad * enc_gain
        value = x_ref[r : r + CHUNK].astype(F32)
        inverse = inv_x[r : r + CHUNK]
        inner = jnp.mean(grad * value, axis=1, keepdims=True) * (inverse * inverse)
        bg_ref[r : r + CHUNK] = (
            ecot[r : r + CHUNK] + (grad - value * inner) * inverse
        ).astype(BF16)
    store(bg_ref, bg_hbm)

    for copy in v_spread:
        copy.wait_recv()
    v_total = v_all[0]
    for chip in range(1, n_z):
        v_total = v_total + v_all[chip]
    v_ref[...] = v_total
    store(v_ref, v_hbm)

    z_end(1)
    for copy in started[:early]:
        copy.wait_send()
    z_end(2)
    for part in range(PARTS):
        store(final.at[own_rows(part)], final_hbm.at[own_rows(part)])
    for part in range(PARTS):
        last_copies[part].wait_recv()
        store(final.at[rows_of(1 - core, part)], final_hbm.at[rows_of(1 - core, part)])
    for copy in started[early:]:
        copy.wait_send()
    for copy in stores:
        copy.wait()


def finish(
    bg_hbm, final_hbm, tail_hbm, v_hbm, bg_out, gg_out, ug_out, dg_out, bg, final, tail_b, v_ref, gg, ug, dg, sems
):
    width = final.shape[0]
    copies = []

    def copy(source, target):
        step = pltpu.make_async_copy(source, target, sems.at[len(copies)])
        step.start()
        copies.append(step)
        return step

    load_final = copy(final_hbm, final)
    load_tail = copy(tail_hbm, tail_b)
    load_v = copy(v_hbm, v_ref)
    load_bg = copy(bg_hbm, bg)
    head, tail = slice(0, width), slice(width, 2 * width)
    load_final.wait()
    gg[head] = final[:, 0:128].astype(F32)
    copy(gg.at[head], gg_out.at[head])
    ug[head] = final[:, 128:256].astype(F32)
    copy(ug.at[head], ug_out.at[head])
    load_bg.wait()
    copy(bg, bg_out)
    load_tail.wait()
    load_v.wait()
    gg[tail] = tail_b[...] * v_ref[0:1, 0:128]
    copy(gg.at[tail], gg_out.at[tail])
    ug[tail] = tail_b[...] * v_ref[0:1, 128:256]
    copy(ug.at[tail], ug_out.at[tail])
    dg[...] = final[:, 256:384].astype(F32).T
    copy(dg, dg_out)
    for step in copies[4:]:
        step.wait()


def body(
    bytes_in,
    flags,
    enc_gain,
    conv_weight,
    widen,
    main_gain,
    gate_weight,
    up_weight,
    down_weight,
    out_cot,
):
    rows, width = bytes_in.shape[1:]
    n_y = lax.axis_size("seq") // LINE
    n_z = lax.axis_size("dp") // 2
    assert n_y == len(Y_ORDER)
    half = width // 2
    hbm = pl.BlockSpec(memory_space=pltpu.HBM)
    scratch = [
        ((rows, width), BF16),
        ((width, 384), BF16),
        ((width, 128), F32),
        ((8, 256), F32),
        ((rows, width), BF16),
        ((1, rows), jnp.int32),
        ((8, width // 8), BF16),
        ((KW, width), BF16),
        ((8, width // 8), BF16),
        ((16, width // 8), BF16),
        ((width, 128), BF16),
        ((width, 128), BF16),
        ((128, width), BF16),
        ((rows, width), BF16),
        ((LINE, width, 384), BF16),
        ((LINE, 8, 256), F32),
        ((16, width), BF16),
        ((8, width), F32),
        ((8, width), F32),
        ((rows + 16, width), F32),
        ((rows, 1), F32),
        ((rows, width), BF16),
        ((rows, width), F32),
        ((ROWS, width), BF16),
        ((ROWS, width), BF16),
        ((ROWS, width), BF16),
        ((2, width, ROWS // 2), BF16),
        ((2, width, ROWS // 2), BF16),
        ((ROWS, 1), F32),
        ((ROWS, 1), F32),
        ((LINE, ROWS, 128), BF16),
        ((LINE, ROWS, 256), BF16),
        ((ROWS, width), F32),
        ((ROWS, width), BF16),
        ((n_y, CAP, width), BF16),
        ((LINE, 8, 256), F32),
        ((LINE - 1, 8, 256), F32),
        ((8, 256), F32),
        ((8, 256), F32),
        ((n_z, 8, 256), F32),
        ((LINE, width, 384), F32),
        ((LINE, half, 384), BF16),
        ((LINE, half, 384), BF16),
        ((LINE, half, 384), BF16),
        ((half, 384), BF16),
        ((2, half, 384), BF16),
        ((half, 384), BF16),
        ((n_z - 1, half // n_z, 384), BF16),
        ((rows, width), F32),
        ((rows + 8, width), F32),
        ((8, width), F32),
    ]
    sums = pl.pallas_call(
        kernel,
        out_shape=(
            jax.ShapeDtypeStruct((rows, width), BF16),
            jax.ShapeDtypeStruct((width, 384), BF16),
            jax.ShapeDtypeStruct((width, 128), F32),
            jax.ShapeDtypeStruct((8, 256), F32),
        ),
        in_specs=[hbm] * 10,
        out_specs=[hbm] * 4,
        scratch_shapes=[pltpu.VMEM(shape, kind) for shape, kind in scratch]
        + [
            pltpu.SemaphoreType.DMA((12,)),
            pltpu.SemaphoreType.DMA((9,)),
            pltpu.SemaphoreType.DMA((120,)),
            pltpu.SemaphoreType.DMA((120,)),
        ],
        compiler_params=pltpu.CompilerParams(
            collective_id=0, has_side_effects=True, vmem_limit_bytes=60 * 1024 * 1024
        ),
    )(
        bytes_in[0],
        flags,
        enc_gain.reshape(8, width // 8),
        conv_weight,
        widen.reshape(8, width // 8),
        main_gain.reshape(16, width // 8),
        gate_weight,
        up_weight,
        down_weight,
        out_cot[0],
    )
    outs = pl.pallas_call(
        finish,
        out_shape=(
            jax.ShapeDtypeStruct((rows, width), BF16),
            jax.ShapeDtypeStruct((2 * width, 128), F32),
            jax.ShapeDtypeStruct((2 * width, 128), F32),
            jax.ShapeDtypeStruct((128, width), F32),
        ),
        in_specs=[hbm] * 4,
        out_specs=[hbm] * 4,
        scratch_shapes=[
            pltpu.VMEM((rows, width), BF16),
            pltpu.VMEM((width, 384), BF16),
            pltpu.VMEM((width, 128), F32),
            pltpu.VMEM((8, 256), F32),
            pltpu.VMEM((2 * width, 128), F32),
            pltpu.VMEM((2 * width, 128), F32),
            pltpu.VMEM((128, width), F32),
            pltpu.SemaphoreType.DMA((10,)),
        ],
        compiler_params=pltpu.CompilerParams(vmem_limit_bytes=60 * 1024 * 1024),
    )(*sums)
    return (outs[0][None], outs[1], outs[2], outs[3])


def solution(mesh):
    in_specs = (
        P("dp", "seq", None),
        P("dp", "seq"),
        P(),
        P(),
        P(),
        P(),
        P(None, "seq"),
        P(None, "seq"),
        P("seq", None),
        P("dp", "seq", None),
    )
    out_specs = (P("dp", "seq", None), P(None, "seq"), P(None, "seq"), P("seq", None))
    return jax.shard_map(body, mesh=mesh, in_specs=in_specs, out_specs=out_specs, check_vma=False)
```

```python
import jax
import jax.numpy as jnp
from jax import lax
from jax.experimental import pallas as pl
from jax.experimental.pallas import tpu as pltpu
from jax.sharding import PartitionSpec as P

MESH = pl.DeviceIdType.MESH
F32 = jnp.float32
BF16 = jnp.bfloat16

KW = 4
CAP = 48
EPS = 1e-05
LINE = 4
PIECES = (0, 256, 384, 512)
PARTS = len(PIECES) - 1
CHUNK = 32

Y_ORDER = (0, -1, 1, -2, 2, -3, 3, 4)
Y_ROW = (0, 48, 96, 144, 192, 256, 304, 352)
NEAR = (0, 240)
FAR = (256, 400)
ROWS = 512
X_ORDER = (0, -1, 1, 2)


def dot(left, right):
    return jnp.dot(left, right, preferred_element_type=F32)


def dot_rows(left, right):
    return lax.dot_general(left, right, (((0,), (0,)), ((), ())), preferred_element_type=F32)


def dot_lanes(left, right):
    return lax.dot_general(left, right, (((1,), (1,)), ((), ())), preferred_element_type=F32)


def as_row(value):
    value = value.astype(F32)
    return jnp.concatenate([value[i : i + 1] for i in range(value.shape[0])], axis=1)


def kernel(
    x_hbm,
    marks_hbm,
    enc_gain_hbm,
    conv_hbm,
    widen_hbm,
    main_gain_hbm,
    gw_hbm,
    uw_hbm,
    dw_hbm,
    oc_hbm,
    bg_hbm,
    final_hbm,
    tail_hbm,
    v_hbm,
    bg_ref,
    final,
    tail_b,
    v_ref,
    x_ref,
    marks_ref,
    enc_gain_ref,
    conv_ref,
    widen_ref,
    main_gain_ref,
    gw_tail,
    uw_tail,
    dw_ref,
    oc_ref,
    w_all,
    tails,
    halo,
    lead_out,
    lead_in,
    norm_x,
    inv_x,
    enc_out,
    slope,
    in_all,
    cot_all,
    normed,
    normed_t,
    cot_t,
    inv_all,
    tin_all,
    act_all,
    cots_all,
    back,
    part_all,
    y_in,
    y_relay,
    y_cross,
    y_mid,
    v_out,
    v_in,
    v_pair,
    v_sib,
    v_all,
    g_acc,
    g_out,
    g_in,
    g_x,
    x_opp,
    x_in,
    h_all,
    z_in,
    ecot,
    g_mix,
    edge,
    load_sems,
    store_sems,
    send_sems,
    recv_sems,
):
    n_seq = lax.axis_size("seq")
    n_y = n_seq // LINE
    n_z = lax.axis_size("dp") // 2
    dp = lax.axis_index("dp")
    seq = lax.axis_index("seq")
    z, core = dp // 2, dp % 2
    y, x = seq // LINE, seq % LINE
    rows, width = x_ref.shape
    half = width // 2

    def y_dev(step):
        return {"seq": lax.rem(y + step + n_y, n_y) * LINE + x}

    def x_dev(step):
        return {"seq": y * LINE + lax.rem(x + step + LINE, LINE)}

    def z_dev(step):
        return {"dp": lax.rem(z + step + n_z, n_z) * 2 + core}

    sibling = {"dp": z * 2 + 1 - core}
    after = {"seq": lax.rem(seq + 1, n_seq)}
    before = {"seq": lax.rem(seq + n_seq - 1, n_seq)}

    loads = []
    stores = []

    def load(source, target):
        copy = pltpu.make_async_copy(source, target, load_sems.at[len(loads)])
        copy.start()
        loads.append(copy)
        return copy

    def store(source, target):
        copy = pltpu.make_async_copy(source, target, store_sems.at[len(stores)])
        copy.start()
        stores.append(copy)

    load_marks = load(marks_hbm, marks_ref)
    load_oc = load(oc_hbm, oc_ref)

    started = []

    def send(source, target, device):
        index = len(started)
        copy = pltpu.make_async_remote_copy(
            src_ref=source,
            dst_ref=target,
            send_sem=send_sems.at[index],
            recv_sem=recv_sems.at[index],
            device_id=device,
            device_id_type=MESH,
        )
        copy.start()
        started.append(copy)
        return copy

    barrier = pltpu.get_barrier_semaphore()
    peers = [y_dev(step) for step in (1, -1, 2, -2)]
    peers += [x_dev(step) for step in (1, -1, 2)]
    peers += [z_dev(step) for step in range(1, n_z)]
    peers += [sibling, after, before]
    for peer in peers:
        pl.semaphore_signal(barrier, inc=1, device_id=peer, device_id_type=MESH)

    load_x = load(x_hbm, x_ref)
    load_gain = load(enc_gain_hbm, enc_gain_ref)
    load_conv = load(conv_hbm, conv_ref)
    load_w = [
        load(dw_hbm, dw_ref),
        load(gw_hbm.at[0:width], w_all.at[0, :, 0:128]),
        load(uw_hbm.at[0:width], w_all.at[0, :, 128:256]),
    ]
    load_tail = [
        load(widen_hbm, widen_ref),
        load(main_gain_hbm, main_gain_ref),
        load(gw_hbm.at[width : 2 * width], gw_tail),
        load(uw_hbm.at[width : 2 * width], uw_tail),
    ]

    load_marks.wait()
    marks = marks_ref[...].astype(F32)
    upper = (
        lax.broadcasted_iota(jnp.int32, (rows, rows), 0)
        <= lax.broadcasted_iota(jnp.int32, (rows, rows), 1)
    ).astype(F32).astype(BF16)
    running = dot(jnp.broadcast_to(marks, (16, rows)).astype(BF16), upper)
    lead = jnp.where(running == 0.0, 1.0, 0.0).astype(BF16)
    slot_ids = lax.broadcasted_iota(jnp.int32, (CAP, rows), 0).astype(F32)
    member = jnp.where(slot_ids == running[0:1] - 1.0, 1.0, 0.0)
    chosen = (member * marks).astype(BF16)
    last_slot = jnp.where(slot_ids[:, 0:1] == running[0:1, rows - 1 : rows] - 1.0, 1.0, 0.0)
    load_oc.wait()
    lead_out[...] = dot(lead, oc_ref[...])[0:8]

    pl.semaphore_wait(barrier, len(peers))

    halo_copy = send(x_hbm.at[rows - 16 : rows], halo, after)
    lead_copy = send(lead_out, lead_in, before)
    own_sums = dot(member.astype(BF16), oc_ref[...])

    for copy in load_w:
        copy.wait()
    w_all[0, :, 256:384] = dw_ref[...].astype(F32).T.astype(BF16)

    def w_rows(slot, part):
        start = pl.multiple_of(core * half + part * (half // 2), half // 2)
        return w_all.at[slot, pl.ds(start, half // 2)]

    w_right = [None, None]
    w_left = [None, None]

    def w_send(part):
        w_right[part] = send(w_rows(0, part), w_rows(1, part), x_dev(1))
        w_left[1 - part] = send(w_rows(0, 1 - part), w_rows(2, 1 - part), x_dev(-1))

    w_send(0)

    ring = {}

    def pass_on(which, side, direction, step):
        buffer = (in_all, cot_all)[which]
        lanes = slice(side * half, (side + 1) * half)
        here = Y_ROW[Y_ORDER.index(-direction * step)]
        there = Y_ROW[Y_ORDER.index(4 if step == 3 else -direction * (step + 1))]
        ring[which, side, direction, step] = send(
            buffer.at[here : here + CAP, lanes],
            buffer.at[there : there + CAP, lanes],
            y_dev(direction),
        )

    def first_hop(which):
        for side in (0, 1):
            for direction in (1, -1):
                pass_on(which, side, direction, 0)

    load_gain.wait()
    load_conv.wait()
    load_x.wait()
    enc_gain = as_row(enc_gain_ref[...])
    taps = [conv_ref[tap : tap + 1, :].astype(F32) for tap in range(KW)]
    for r in range(0, rows, CHUNK):
        value = x_ref[r : r + CHUNK].astype(F32)
        inverse = lax.rsqrt(jnp.mean(value * value, axis=1, keepdims=True) + EPS)
        inv_x[r : r + CHUNK] = inverse
        norm_x[16 + r : 16 + r + CHUNK] = value * inverse * enc_gain
    lead_copy.wait_recv()
    carried = lead_in[0:1] * (seq < n_seq - 1).astype(F32)
    cot_all[0:CAP] = (own_sums + last_slot * carried).astype(BF16)
    first_hop(1)

    halo_copy.wait_recv()
    value = halo[...].astype(F32) * (seq > 0).astype(F32)
    inverse = lax.rsqrt(jnp.mean(value * value, axis=1, keepdims=True) + EPS)
    norm_x[0:16] = value * inverse * enc_gain
    for r in range(0, rows, CHUNK):
        mixed = taps[0] * norm_x[16 + r : 16 + r + CHUNK]
        for tap in range(1, KW):
            mixed = mixed + taps[tap] * norm_x[16 + r - tap : 16 + r - tap + CHUNK]
        sigma = jax.nn.sigmoid(mixed)
        enc_out[r : r + CHUNK] = (x_ref[r : r + CHUNK].astype(F32) + mixed * sigma).astype(BF16)
        slope[r : r + CHUNK] = sigma * (1.0 + mixed * (1.0 - sigma))
    in_all[0:CAP] = dot(chosen, enc_out[...]).astype(BF16)
    first_hop(0)
    w_send(1)

    w_twin = []

    def swap(slot, part):
        w_twin.append(send(w_rows(slot, part), w_rows(slot, part), sibling))

    for copy in load_tail:
        copy.wait()
    widen = as_row(widen_ref[...])
    main_gain = as_row(main_gain_ref[...])
    gain_head = main_gain[:, 0:width]
    tail_vec = widen * main_gain[:, width : 2 * width]
    tail_square = jnp.sum(widen * widen, axis=1, keepdims=True)
    tail_b[...] = jnp.broadcast_to(tail_vec, (128, width)).T
    store(tail_b, tail_hbm)
    tail_gate = jnp.sum(gw_tail[...].astype(F32) * tail_b[...], axis=0, keepdims=True)
    tail_up = jnp.sum(uw_tail[...].astype(F32) * tail_b[...], axis=0, keepdims=True)
    tails[0, :, 0:128] = jnp.broadcast_to(tail_gate, (8, 128))
    tails[0, :, 128:256] = jnp.broadcast_to(tail_up, (8, 128))
    tail_copies = [
        send(tails.at[0], tails.at[1], x_dev(1)),
        send(tails.at[0], tails.at[2], x_dev(-1)),
        send(tails.at[0], tails.at[3], x_dev(2)),
    ]

    def relay(which, step):
        for side in (0, 1):
            for direction in (1, -1):
                ring[which, side, direction, step - 1].wait_recv()
                pass_on(which, side, direction, step)

    def relay_last(which):
        for side, direction in ((0, 1), (1, -1)):
            ring[which, side, direction, 2].wait_recv()
            pass_on(which, side, direction, 3)

    def wait_last(which):
        for side, direction in ((0, 1), (1, -1)):
            ring[which, 1 - side, direction, 2].wait_recv()
            ring[which, side, direction, 3].wait_recv()

    relay(1, 1)
    relay(0, 1)
    w_right[0].wait_recv()
    w_far_a = send(w_rows(1, 0), w_rows(3, 0), x_dev(1))
    w_left[1].wait_recv()
    w_far_b = send(w_rows(2, 1), w_rows(3, 1), x_dev(-1))
    swap(1, 0)
    swap(2, 1)
    for first, last in ((NEAR[1], FAR[0]), (FAR[1], ROWS)):
        count = last - first
        normed[first:last] = jnp.zeros((count, width), BF16)
        cot_all[first:last] = jnp.zeros((count, width), BF16)
        inv_all[first:last] = jnp.zeros((count, 1), F32)
        act_all[:, first:last] = jnp.zeros((LINE, count, 128), BF16)
        cots_all[:, first:last] = jnp.zeros((LINE, count, 256), BF16)
    relay(1, 2)
    relay(0, 2)
    w_right[1].wait_recv()
    swap(1, 1)
    w_left[0].wait_recv()
    swap(2, 0)

    def normalise(first, last):
        for r in range(first, last, CAP):
            head = in_all[r : r + CAP].astype(F32)
            square = jnp.sum(head * head, axis=1, keepdims=True) + tail_square
            inverse = lax.rsqrt(square / (2 * width) + EPS)
            inv_all[r : r + CAP] = inverse
            normed[r : r + CAP] = (head * inverse * gain_head).astype(BF16)
        tin_all[first:last] = jnp.zeros((last - first, 1), F32)

    def forward(first, last, low, high):
        def block(slot, carry):
            tail = tails[slot, 0:1, :]
            both = dot(normed[first:last], w_all[slot, :, 0:256]) + inv_all[first:last] * tail
            act_cot = dot(cot_all[first:last], w_all[slot, :, 256:384])
            gate, up = both[:, 0:128], both[:, 128:256]
            sigma = jax.nn.sigmoid(gate)
            swish = gate * sigma
            act_all[slot, first:last, :] = (swish * up).astype(BF16)
            gate_cot = (act_cot * up * sigma * (1.0 + gate * (1.0 - sigma))).astype(BF16)
            up_cot = (act_cot * swish).astype(BF16)
            cots_all[slot, first:last, 0:128] = gate_cot
            cots_all[slot, first:last, 128:256] = up_cot
            tin_all[first:last] += jnp.sum(
                gate_cot.astype(F32) * tail[:, 0:128] + up_cot.astype(F32) * tail[:, 128:256],
                axis=1,
                keepdims=True,
            )
            return carry

        lax.fori_loop(low, high, block, 0)

    def backward(first, last):
        def block(slot, carry):
            back[first:last] += dot_lanes(cots_all[slot, first:last], w_all[slot, :, 0:256])
            return carry

        back[first:last] = dot_lanes(cots_all[0, first:last], w_all[0, :, 0:256])
        lax.fori_loop(1, LINE, block, 0)
        for r in range(first, last, CAP):
            inverse = inv_all[r : r + CAP]
            unit = in_all[r : r + CAP].astype(F32) * inverse
            scaled = back[r : r + CAP] * gain_head
            inner = jnp.sum(scaled * unit, axis=1, keepdims=True) + tin_all[r : r + CAP] * inverse
            part_all[r : r + CAP] = (
                (scaled - unit * (inner / (2 * width))) * inverse
            ).astype(BF16)

    def part_of(step, lanes=slice(None)):
        row = Y_ROW[Y_ORDER.index(step)]
        return part_all.at[row : row + CAP, lanes]

    normalise(*NEAR)
    for copy in tail_copies + w_twin:
        copy.wait_recv()
    forward(*NEAR, 0, LINE - 1)
    relay_last(1)
    normed_t[0] = normed[0 : FAR[0]].T
    cot_t[0] = cot_all[0 : FAR[0]].T
    first_twins = len(w_twin)
    w_far_a.wait_recv()
    swap(3, 0)
    w_far_b.wait_recv()
    swap(3, 1)
    relay_last(0)
    for copy in w_twin[first_twins:]:
        copy.wait_recv()
    forward(*NEAR, LINE - 1, LINE)

    def near_product(slot, carry):
        g_acc[slot, :, 0:256] = dot(normed_t[0], cots_all[slot, 0 : FAR[0]])
        g_acc[slot, :, 256:384] = dot(cot_t[0], act_all[slot, 0 : FAR[0]])
        return carry

    lax.fori_loop(0, LINE, near_product, 0)

    wait_last(1)
    cot_t[1] = cot_all[FAR[0] : ROWS].T
    wait_last(0)
    normalise(*FAR)
    forward(*FAR, 0, LINE)
    normed_t[1] = normed[FAR[0] : ROWS].T

    def far_product(start, count, slot):
        some = pl.ds(pl.multiple_of(start, 128), count)
        wide = dot(normed_t[1, some], cots_all[slot, FAR[0] : ROWS])
        narrow = dot(cot_t[1, some], act_all[slot, FAR[0] : ROWS])
        return wide + g_acc[slot, some, 0:256], narrow + g_acc[slot, some, 256:384]

    def theirs(low, high):
        def block(slot, carry):
            wide, narrow = far_product((1 - core) * half + low, high - low, slot)
            g_out[slot, low:high, 0:256] = wide.astype(BF16)
            g_out[slot, low:high, 256:384] = narrow.astype(BF16)
            return carry

        lax.fori_loop(0, LINE, block, 0)

    def cut(part):
        return slice(PIECES[part], PIECES[part + 1])

    def halves(part):
        first, last = PIECES[part], PIECES[part + 1]
        mid = (first + last) // 2
        return slice(first, mid), slice(mid, last)

    def pair(part):
        return send(g_out.at[:, cut(part)], g_in.at[:, cut(part)], sibling)

    theirs(0, PIECES[1])
    pair_copies = [pair(0)]
    theirs(PIECES[1], half)
    pair_copies += [pair(part) for part in range(1, PARTS)]

    def ours(slot, carry):
        wide, narrow = far_product(core * half, half, slot)
        some = pl.ds(pl.multiple_of(core * half, half), half)
        g_acc[slot, some, 0:256] = wide
        g_acc[slot, some, 256:384] = narrow
        return carry

    lax.fori_loop(0, LINE, ours, 0)
    backward(*NEAR)

    x_first, x_second, z_first, z_near, z_far, last_copies = ({} for _ in range(6))

    def rows_of(which, part):
        count = PIECES[part + 1] - PIECES[part]
        return pl.ds(pl.multiple_of(which * half + PIECES[part], 128), count)

    def own_rows(part):
        return rows_of(core, part)

    def x_start(part):
        pair_copies[part].wait_recv()

        def add(slot, carry):
            total = g_acc[slot, own_rows(part)] + g_in[slot, cut(part)].astype(F32)
            g_x[slot, cut(part)] = total.astype(BF16)
            return carry

        lax.fori_loop(1, LINE, add, 0)
        low, high = halves(part)
        x_first[part] = (
            send(g_x.at[3, low], x_opp.at[low], x_dev(1)),
            send(g_x.at[3, high], x_opp.at[high], x_dev(-1)),
            send(g_x.at[2, high], x_in.at[0, high], x_dev(1)),
            send(g_x.at[1, low], x_in.at[1, low], x_dev(-1)),
        )

    def x_relay(part):
        low, high = halves(part)
        x_first[part][0].wait_recv()
        g_x[2, low] = (g_x[2, low].astype(F32) + x_opp[low].astype(F32)).astype(BF16)
        right = send(g_x.at[2, low], x_in.at[0, low], x_dev(1))
        x_first[part][1].wait_recv()
        g_x[1, high] = (g_x[1, high].astype(F32) + x_opp[high].astype(F32)).astype(BF16)
        left = send(g_x.at[1, high], x_in.at[1, high], x_dev(-1))
        x_second[part] = (right, left)

    def z_cut(part, step, base=0):
        count = (PIECES[part + 1] - PIECES[part]) // n_z
        start = base + PIECES[part] + lax.rem(z + step + n_z, n_z) * count
        return pl.ds(pl.multiple_of(start, 16), count)

    def z_slot(part):
        return slice(PIECES[part] // n_z, PIECES[part + 1] // n_z)

    def z_start(part):
        for copy in x_first[part][2:] + x_second[part]:
            copy.wait_recv()
        h_all[cut(part)] = (
            g_acc[0, own_rows(part)]
            + g_in[0, cut(part)].astype(F32)
            + x_in[0, cut(part)].astype(F32)
            + x_in[1, cut(part)].astype(F32)
        ).astype(BF16)
        z_first[part] = [
            send(h_all.at[z_cut(part, step)], z_in.at[index, z_slot(part)], z_dev(step))
            for index, step in enumerate((4, 3, -3, 2, -2, 1, -1))
        ]

    def z_final(part, step):
        return z_cut(part, step, core * half)

    def z_sum(part):
        total = h_all[z_cut(part, 0)].astype(F32)
        for index, copy in enumerate(z_first[part]):
            copy.wait_recv()
            total = total + z_in[index, z_slot(part)].astype(F32)
        final[z_final(part, 0)] = total.astype(BF16)
        mine = final.at[z_final(part, 0)]
        steps = (2, -2, 1, -1) if part < PARTS - 1 else (4, 3, -3, 2, -2, 1, -1)
        z_near[part] = [send(mine, mine, z_dev(step)) for step in steps]

    def z_spread(part):
        copies = []
        for side, step in ((0, 1), (1, -1)):
            z_near[part][side].wait_recv()
            theirs = final.at[z_final(part, -2 * step)]
            copies.append(send(theirs, theirs, z_dev(step)))
            if side == min(part, 1):
                copies.append(send(theirs, theirs, z_dev(2 * step)))
        z_far[part] = copies

    def z_end(part):
        waits = z_near[part][2:] + z_far[part] if part < PARTS - 1 else z_near[part]
        for copy in waits:
            copy.wait_recv()
        mine = final.at[own_rows(part)]
        last_copies[part] = send(mine, mine, sibling)

    x_start(0)
    x_start(1)
    y_copies = [
        send(part_of(1), y_in.at[0], y_dev(1)),
        send(part_of(-1), y_in.at[1], y_dev(-1)),
    ]
    backward(*FAR)
    x_relay(0)
    x_start(2)
    y_relays = [
        send(part_of(3), y_relay.at[0], y_dev(1)),
        send(part_of(-3), y_relay.at[1], y_dev(-1)),
        send(part_of(4, slice(0, half)), y_cross.at[0], y_dev(2)),
        send(part_of(4, slice(half, width)), y_cross.at[1], y_dev(-2)),
    ]
    x_relay(1)

    def tail_rows(slot, carry):
        row = jnp.sum(cots_all[slot].astype(F32) * inv_all[...], axis=0, keepdims=True)
        v_out[slot] = jnp.broadcast_to(row, (8, 256))
        return carry

    lax.fori_loop(0, LINE, tail_rows, 0)
    v_copies = [
        send(v_out.at[1], v_in.at[0], x_dev(-1)),
        send(v_out.at[2], v_in.at[1], x_dev(1)),
        send(v_out.at[3], v_in.at[2], x_dev(2)),
    ]
    x_relay(2)
    z_start(0)

    for copy in v_copies:
        copy.wait_recv()
    v_pair[...] = v_out[0] + v_in[0] + v_in[1] + v_in[2]
    v_swap = send(v_pair, v_sib, sibling)

    z_start(1)
    v_swap.wait_recv()
    v_all[z] = v_pair[...] + v_sib[...]
    v_spread = [send(v_all.at[z], v_all.at[z], z_dev(step)) for step in range(1, n_z)]

    for copy in y_relays:
        copy.wait_recv()
    for side, step in ((0, 2), (1, -2)):
        row = Y_ROW[Y_ORDER.index(step)]
        total = part_all[row : row + CAP].astype(F32) + y_relay[side].astype(F32)
        lanes = slice(side * half, (side + 1) * half)
        other = slice((1 - side) * half, (2 - side) * half)
        y_mid[side, :, lanes] = (total[:, lanes] + y_cross[side].astype(F32)).astype(BF16)
        y_mid[side, :, other] = total[:, other].astype(BF16)
        y_copies.append(send(y_mid.at[side], y_in.at[2 + side], y_dev(step)))

    z_sum(0)
    z_start(2)
    z_sum(1)
    z_spread(0)
    z_sum(2)
    z_spread(1)
    early = len(started)

    for copy in y_copies:
        copy.wait_recv()
    widen_cot = part_all[0:CAP].astype(F32)
    for index in range(4):
        widen_cot = widen_cot + y_in[index].astype(F32)
    spread = dot_rows(chosen, cot_all[0:CAP]) + dot_rows(chosen, widen_cot.astype(BF16))
    ecot[...] = oc_ref[...].astype(F32) + spread
    for r in range(0, rows, CHUNK):
        g_mix[r : r + CHUNK] = ecot[r : r + CHUNK] * slope[r : r + CHUNK]
    edge_copy = send(g_mix.at[0:8], edge, before)

    z_end(0)

    edge_copy.wait_recv()
    g_mix[rows : rows + 8] = edge[...] * (seq < n_seq - 1).astype(F32)
    for r in range(0, rows, CHUNK):
        grad = taps[0] * g_mix[r : r + CHUNK]
        for tap in range(1, KW):
            grad = grad + taps[tap] * g_mix[r + tap : r + tap + CHUNK]
        grad = grad * enc_gain
        value = x_ref[r : r + CHUNK].astype(F32)
        inverse = inv_x[r : r + CHUNK]
        inner = jnp.mean(grad * value, axis=1, keepdims=True) * (inverse * inverse)
        bg_ref[r : r + CHUNK] = (
            ecot[r : r + CHUNK] + (grad - value * inner) * inverse
        ).astype(BF16)
    store(bg_ref, bg_hbm)

    for copy in v_spread:
        copy.wait_recv()
    v_total = v_all[0]
    for chip in range(1, n_z):
        v_total = v_total + v_all[chip]
    v_ref[...] = v_total
    store(v_ref, v_hbm)

    z_end(1)
    for copy in started[:early]:
        copy.wait_send()
    z_end(2)
    for part in range(PARTS):
        store(final.at[own_rows(part)], final_hbm.at[own_rows(part)])
    for part in range(PARTS):
        last_copies[part].wait_recv()
        store(final.at[rows_of(1 - core, part)], final_hbm.at[rows_of(1 - core, part)])
    for copy in started[early:]:
        copy.wait_send()
    for copy in stores:
        copy.wait()


def finish(
    bg_hbm, final_hbm, tail_hbm, v_hbm, bg_out, gg_out, ug_out, dg_out, bg, final, tail_b, v_ref, gg, ug, dg, sems
):
    width = final.shape[0]
    copies = []

    def copy(source, target):
        step = pltpu.make_async_copy(source, target, sems.at[len(copies)])
        step.start()
        copies.append(step)
        return step

    load_tail = copy(tail_hbm, tail_b)
    load_v = copy(v_hbm, v_ref)
    load_final = copy(final_hbm, final)
    load_bg = copy(bg_hbm, bg)
    head, tail = slice(0, width), slice(width, 2 * width)
    load_tail.wait()
    load_v.wait()
    gg[tail] = tail_b[...] * v_ref[0:1, 0:128]
    copy(gg.at[tail], gg_out.at[tail])
    ug[tail] = tail_b[...] * v_ref[0:1, 128:256]
    copy(ug.at[tail], ug_out.at[tail])
    load_final.wait()
    gg[head] = final[:, 0:128].astype(F32)
    copy(gg.at[head], gg_out.at[head])
    ug[head] = final[:, 128:256].astype(F32)
    copy(ug.at[head], ug_out.at[head])
    load_bg.wait()
    copy(bg, bg_out)
    dg[...] = final[:, 256:384].astype(F32).T
    copy(dg, dg_out)
    for step in copies[4:]:
        step.wait()


def body(
    bytes_in,
    flags,
    enc_gain,
    conv_weight,
    widen,
    main_gain,
    gate_weight,
    up_weight,
    down_weight,
    out_cot,
):
    rows, width = bytes_in.shape[1:]
    n_y = lax.axis_size("seq") // LINE
    n_z = lax.axis_size("dp") // 2
    assert n_y == len(Y_ORDER)
    half = width // 2
    hbm = pl.BlockSpec(memory_space=pltpu.HBM)
    scratch = [
        ((rows, width), BF16),
        ((width, 384), BF16),
        ((width, 128), F32),
        ((8, 256), F32),
        ((rows, width), BF16),
        ((1, rows), jnp.int32),
        ((8, width // 8), BF16),
        ((KW, width), BF16),
        ((8, width // 8), BF16),
        ((16, width // 8), BF16),
        ((width, 128), BF16),
        ((width, 128), BF16),
        ((128, width), BF16),
        ((rows, width), BF16),
        ((LINE, width, 384), BF16),
        ((LINE, 8, 256), F32),
        ((16, width), BF16),
        ((8, width), F32),
        ((8, width), F32),
        ((rows + 16, width), F32),
        ((rows, 1), F32),
        ((rows, width), BF16),
        ((rows, width), F32),
        ((ROWS, width), BF16),
        ((ROWS, width), BF16),
        ((ROWS, width), BF16),
        ((2, width, ROWS // 2), BF16),
        ((2, width, ROWS // 2), BF16),
        ((ROWS, 1), F32),
        ((ROWS, 1), F32),
        ((LINE, ROWS, 128), BF16),
        ((LINE, ROWS, 256), BF16),
        ((ROWS, width), F32),
        ((ROWS, width), BF16),
        ((4, CAP, width), BF16),
        ((2, CAP, width), BF16),
        ((2, CAP, half), BF16),
        ((2, CAP, width), BF16),
        ((LINE, 8, 256), F32),
        ((LINE - 1, 8, 256), F32),
        ((8, 256), F32),
        ((8, 256), F32),
        ((n_z, 8, 256), F32),
        ((LINE, width, 384), F32),
        ((LINE, half, 384), BF16),
        ((LINE, half, 384), BF16),
        ((LINE, half, 384), BF16),
        ((half, 384), BF16),
        ((2, half, 384), BF16),
        ((half, 384), BF16),
        ((n_z - 1, half // n_z, 384), BF16),
        ((rows, width), F32),
        ((rows + 8, width), F32),
        ((8, width), F32),
    ]
    sums = pl.pallas_call(
        kernel,
        out_shape=(
            jax.ShapeDtypeStruct((rows, width), BF16),
            jax.ShapeDtypeStruct((width, 384), BF16),
            jax.ShapeDtypeStruct((width, 128), F32),
            jax.ShapeDtypeStruct((8, 256), F32),
        ),
        in_specs=[hbm] * 10,
        out_specs=[hbm] * 4,
        scratch_shapes=[pltpu.VMEM(shape, kind) for shape, kind in scratch]
        + [
            pltpu.SemaphoreType.DMA((12,)),
            pltpu.SemaphoreType.DMA((9,)),
            pltpu.SemaphoreType.DMA((144,)),
            pltpu.SemaphoreType.DMA((144,)),
        ],
        compiler_params=pltpu.CompilerParams(
            collective_id=0, has_side_effects=True, vmem_limit_bytes=60 * 1024 * 1024
        ),
    )(
        bytes_in[0],
        flags,
        enc_gain.reshape(8, width // 8),
        conv_weight,
        widen.reshape(8, width // 8),
        main_gain.reshape(16, width // 8),
        gate_weight,
        up_weight,
        down_weight,
        out_cot[0],
    )
    outs = pl.pallas_call(
        finish,
        out_shape=(
            jax.ShapeDtypeStruct((rows, width), BF16),
            jax.ShapeDtypeStruct((2 * width, 128), F32),
            jax.ShapeDtypeStruct((2 * width, 128), F32),
            jax.ShapeDtypeStruct((128, width), F32),
        ),
        in_specs=[hbm] * 4,
        out_specs=[hbm] * 4,
        scratch_shapes=[
            pltpu.VMEM((rows, width), BF16),
            pltpu.VMEM((width, 384), BF16),
            pltpu.VMEM((width, 128), F32),
            pltpu.VMEM((8, 256), F32),
            pltpu.VMEM((2 * width, 128), F32),
            pltpu.VMEM((2 * width, 128), F32),
            pltpu.VMEM((128, width), F32),
            pltpu.SemaphoreType.DMA((10,)),
        ],
        compiler_params=pltpu.CompilerParams(vmem_limit_bytes=60 * 1024 * 1024),
    )(*sums)
    return (outs[0][None], outs[1], outs[2], outs[3])


def solution(mesh):
    in_specs = (
        P("dp", "seq", None),
        P("dp", "seq"),
        P(),
        P(),
        P(),
        P(),
        P(None, "seq"),
        P(None, "seq"),
        P("seq", None),
        P("dp", "seq", None),
    )
    out_specs = (P("dp", "seq", None), P(None, "seq"), P(None, "seq"), P("seq", None))
    return jax.shard_map(body, mesh=mesh, in_specs=in_specs, out_specs=out_specs, check_vma=False)
```

```python
import jax
import jax.numpy as jnp
from jax import lax
from jax.experimental import pallas as pl
from jax.experimental.pallas import tpu as pltpu
from jax.sharding import PartitionSpec as P

MESH = pl.DeviceIdType.MESH
F32 = jnp.float32
BF16 = jnp.bfloat16

KW = 4
CAP = 48
EPS = 1e-05
LINE = 4
PIECES = (0, 128, 384, 512)
PARTS = len(PIECES) - 1
CHUNK = 32

Y_ORDER = (0, -1, 1, -2, 2, -3, 3, 4)
Y_ROW = (0, 48, 96, 144, 192, 256, 304, 352)
NEAR = (0, 240)
FAR = (256, 400)
ROWS = 512
X_ORDER = (0, -1, 1, 2)


def dot(left, right):
    return jnp.dot(left, right, preferred_element_type=F32)


def dot_rows(left, right):
    return lax.dot_general(left, right, (((0,), (0,)), ((), ())), preferred_element_type=F32)


def dot_lanes(left, right):
    return lax.dot_general(left, right, (((1,), (1,)), ((), ())), preferred_element_type=F32)


def as_row(value):
    value = value.astype(F32)
    return jnp.concatenate([value[i : i + 1] for i in range(value.shape[0])], axis=1)


def kernel(
    x_hbm,
    marks_hbm,
    enc_gain_hbm,
    conv_hbm,
    widen_hbm,
    main_gain_hbm,
    gw_hbm,
    uw_hbm,
    dw_hbm,
    oc_hbm,
    bg_hbm,
    final_hbm,
    tail_hbm,
    v_hbm,
    bg_ref,
    final,
    tail_b,
    v_ref,
    x_ref,
    marks_ref,
    enc_gain_ref,
    conv_ref,
    widen_ref,
    main_gain_ref,
    gw_tail,
    uw_tail,
    dw_ref,
    oc_ref,
    w_all,
    tails,
    halo,
    lead_out,
    lead_in,
    norm_x,
    inv_x,
    enc_out,
    slope,
    in_all,
    cot_all,
    normed,
    normed_t,
    cot_t,
    inv_all,
    tin_all,
    act_all,
    cots_all,
    back,
    part_all,
    y_in,
    y_relay,
    y_cross,
    y_mid,
    v_out,
    v_in,
    v_pair,
    v_sib,
    v_all,
    g_acc,
    g_out,
    g_in,
    g_x,
    x_opp,
    x_in,
    h_all,
    z_in,
    ecot,
    g_mix,
    edge,
    load_sems,
    store_sems,
    send_sems,
    recv_sems,
):
    n_seq = lax.axis_size("seq")
    n_y = n_seq // LINE
    n_z = lax.axis_size("dp") // 2
    dp = lax.axis_index("dp")
    seq = lax.axis_index("seq")
    z, core = dp // 2, dp % 2
    y, x = seq // LINE, seq % LINE
    rows, width = x_ref.shape
    half = width // 2

    def y_dev(step):
        return {"seq": lax.rem(y + step + n_y, n_y) * LINE + x}

    def x_dev(step):
        return {"seq": y * LINE + lax.rem(x + step + LINE, LINE)}

    def z_dev(step):
        return {"dp": lax.rem(z + step + n_z, n_z) * 2 + core}

    sibling = {"dp": z * 2 + 1 - core}
    after = {"seq": lax.rem(seq + 1, n_seq)}
    before = {"seq": lax.rem(seq + n_seq - 1, n_seq)}

    loads = []
    stores = []

    def load(source, target):
        copy = pltpu.make_async_copy(source, target, load_sems.at[len(loads)])
        copy.start()
        loads.append(copy)
        return copy

    def store(source, target):
        copy = pltpu.make_async_copy(source, target, store_sems.at[len(stores)])
        copy.start()
        stores.append(copy)

    load_marks = load(marks_hbm, marks_ref)
    load_oc = load(oc_hbm, oc_ref)

    started = []

    def send(source, target, device):
        index = len(started)
        copy = pltpu.make_async_remote_copy(
            src_ref=source,
            dst_ref=target,
            send_sem=send_sems.at[index],
            recv_sem=recv_sems.at[index],
            device_id=device,
            device_id_type=MESH,
        )
        copy.start()
        started.append(copy)
        return copy

    barrier = pltpu.get_barrier_semaphore()
    peers = [y_dev(step) for step in (1, -1, 2, -2)]
    peers += [x_dev(step) for step in (1, -1, 2)]
    peers += [z_dev(step) for step in range(1, n_z)]
    peers += [sibling, after, before]
    for peer in peers:
        pl.semaphore_signal(barrier, inc=1, device_id=peer, device_id_type=MESH)

    load_x = load(x_hbm, x_ref)
    load_gain = load(enc_gain_hbm, enc_gain_ref)
    load_conv = load(conv_hbm, conv_ref)
    load_w = [
        load(dw_hbm, dw_ref),
        load(gw_hbm.at[0:width], w_all.at[0, :, 0:128]),
        load(uw_hbm.at[0:width], w_all.at[0, :, 128:256]),
    ]
    load_tail = [
        load(widen_hbm, widen_ref),
        load(main_gain_hbm, main_gain_ref),
        load(gw_hbm.at[width : 2 * width], gw_tail),
        load(uw_hbm.at[width : 2 * width], uw_tail),
    ]

    load_marks.wait()
    marks = marks_ref[...].astype(F32)
    upper = (
        lax.broadcasted_iota(jnp.int32, (rows, rows), 0)
        <= lax.broadcasted_iota(jnp.int32, (rows, rows), 1)
    ).astype(F32).astype(BF16)
    running = dot(jnp.broadcast_to(marks, (16, rows)).astype(BF16), upper)
    lead = jnp.where(running == 0.0, 1.0, 0.0).astype(BF16)
    slot_ids = lax.broadcasted_iota(jnp.int32, (CAP, rows), 0).astype(F32)
    member = jnp.where(slot_ids == running[0:1] - 1.0, 1.0, 0.0)
    chosen = (member * marks).astype(BF16)
    last_slot = jnp.where(slot_ids[:, 0:1] == running[0:1, rows - 1 : rows] - 1.0, 1.0, 0.0)
    load_oc.wait()
    lead_out[...] = dot(lead, oc_ref[...])[0:8]

    pl.semaphore_wait(barrier, len(peers))

    halo_copy = send(x_hbm.at[rows - 16 : rows], halo, after)
    lead_copy = send(lead_out, lead_in, before)
    own_sums = dot(member.astype(BF16), oc_ref[...])

    for copy in load_w:
        copy.wait()
    w_all[0, :, 256:384] = dw_ref[...].astype(F32).T.astype(BF16)

    def w_rows(slot, part):
        start = pl.multiple_of(core * half + part * (half // 2), half // 2)
        return w_all.at[slot, pl.ds(start, half // 2)]

    w_right = [None, None]
    w_left = [None, None]

    def w_send(part):
        w_right[part] = send(w_rows(0, part), w_rows(1, part), x_dev(1))
        w_left[1 - part] = send(w_rows(0, 1 - part), w_rows(2, 1 - part), x_dev(-1))

    w_send(0)

    ring = {}

    def pass_on(which, side, direction, step):
        buffer = (in_all, cot_all)[which]
        lanes = slice(side * half, (side + 1) * half)
        here = Y_ROW[Y_ORDER.index(-direction * step)]
        there = Y_ROW[Y_ORDER.index(4 if step == 3 else -direction * (step + 1))]
        ring[which, side, direction, step] = send(
            buffer.at[here : here + CAP, lanes],
            buffer.at[there : there + CAP, lanes],
            y_dev(direction),
        )

    def first_hop(which):
        for side in (0, 1):
            for direction in (1, -1):
                pass_on(which, side, direction, 0)

    load_gain.wait()
    load_conv.wait()
    load_x.wait()
    enc_gain = as_row(enc_gain_ref[...])
    taps = [conv_ref[tap : tap + 1, :].astype(F32) for tap in range(KW)]
    for r in range(0, rows, CHUNK):
        value = x_ref[r : r + CHUNK].astype(F32)
        inverse = lax.rsqrt(jnp.mean(value * value, axis=1, keepdims=True) + EPS)
        inv_x[r : r + CHUNK] = inverse
        norm_x[16 + r : 16 + r + CHUNK] = value * inverse * enc_gain
    lead_copy.wait_recv()
    carried = lead_in[0:1] * (seq < n_seq - 1).astype(F32)
    cot_all[0:CAP] = (own_sums + last_slot * carried).astype(BF16)
    first_hop(1)

    halo_copy.wait_recv()
    value = halo[...].astype(F32) * (seq > 0).astype(F32)
    inverse = lax.rsqrt(jnp.mean(value * value, axis=1, keepdims=True) + EPS)
    norm_x[0:16] = value * inverse * enc_gain
    for r in range(0, rows, CHUNK):
        mixed = taps[0] * norm_x[16 + r : 16 + r + CHUNK]
        for tap in range(1, KW):
            mixed = mixed + taps[tap] * norm_x[16 + r - tap : 16 + r - tap + CHUNK]
        sigma = jax.nn.sigmoid(mixed)
        enc_out[r : r + CHUNK] = (x_ref[r : r + CHUNK].astype(F32) + mixed * sigma).astype(BF16)
        slope[r : r + CHUNK] = sigma * (1.0 + mixed * (1.0 - sigma))
    in_all[0:CAP] = dot(chosen, enc_out[...]).astype(BF16)
    first_hop(0)
    w_send(1)

    w_twin = []

    def swap(slot, part):
        w_twin.append(send(w_rows(slot, part), w_rows(slot, part), sibling))

    for copy in load_tail:
        copy.wait()
    widen = as_row(widen_ref[...])
    main_gain = as_row(main_gain_ref[...])
    gain_head = main_gain[:, 0:width]
    tail_vec = widen * main_gain[:, width : 2 * width]
    tail_square = jnp.sum(widen * widen, axis=1, keepdims=True)
    tail_b[...] = jnp.broadcast_to(tail_vec, (128, width)).T
    store(tail_b, tail_hbm)
    tail_gate = jnp.sum(gw_tail[...].astype(F32) * tail_b[...], axis=0, keepdims=True)
    tail_up = jnp.sum(uw_tail[...].astype(F32) * tail_b[...], axis=0, keepdims=True)
    tails[0, :, 0:128] = jnp.broadcast_to(tail_gate, (8, 128))
    tails[0, :, 128:256] = jnp.broadcast_to(tail_up, (8, 128))
    tail_copies = [
        send(tails.at[0], tails.at[1], x_dev(1)),
        send(tails.at[0], tails.at[2], x_dev(-1)),
        send(tails.at[0], tails.at[3], x_dev(2)),
    ]

    def relay(which, step):
        for side in (0, 1):
            for direction in (1, -1):
                ring[which, side, direction, step - 1].wait_recv()
                pass_on(which, side, direction, step)

    def relay_last(which):
        for side, direction in ((0, 1), (1, -1)):
            ring[which, side, direction, 2].wait_recv()
            pass_on(which, side, direction, 3)

    def wait_last(which):
        for side, direction in ((0, 1), (1, -1)):
            ring[which, 1 - side, direction, 2].wait_recv()
            ring[which, side, direction, 3].wait_recv()

    relay(1, 1)
    relay(0, 1)
    w_right[0].wait_recv()
    w_far_a = send(w_rows(1, 0), w_rows(3, 0), x_dev(1))
    w_left[1].wait_recv()
    w_far_b = send(w_rows(2, 1), w_rows(3, 1), x_dev(-1))
    swap(1, 0)
    swap(2, 1)
    for first, last in ((NEAR[1], FAR[0]), (FAR[1], ROWS)):
        count = last - first
        normed[first:last] = jnp.zeros((count, width), BF16)
        cot_all[first:last] = jnp.zeros((count, width), BF16)
        inv_all[first:last] = jnp.zeros((count, 1), F32)
        act_all[:, first:last] = jnp.zeros((LINE, count, 128), BF16)
        cots_all[:, first:last] = jnp.zeros((LINE, count, 256), BF16)
    relay(1, 2)
    relay(0, 2)
    w_right[1].wait_recv()
    swap(1, 1)
    w_left[0].wait_recv()
    swap(2, 0)

    def normalise(first, last):
        for r in range(first, last, CAP):
            head = in_all[r : r + CAP].astype(F32)
            square = jnp.sum(head * head, axis=1, keepdims=True) + tail_square
            inverse = lax.rsqrt(square / (2 * width) + EPS)
            inv_all[r : r + CAP] = inverse
            normed[r : r + CAP] = (head * inverse * gain_head).astype(BF16)
        tin_all[first:last] = jnp.zeros((last - first, 1), F32)

    def forward(first, last, low, high):
        def block(slot, carry):
            tail = tails[slot, 0:1, :]
            both = dot(normed[first:last], w_all[slot, :, 0:256]) + inv_all[first:last] * tail
            act_cot = dot(cot_all[first:last], w_all[slot, :, 256:384])
            gate, up = both[:, 0:128], both[:, 128:256]
            sigma = jax.nn.sigmoid(gate)
            swish = gate * sigma
            act_all[slot, first:last, :] = (swish * up).astype(BF16)
            gate_cot = (act_cot * up * sigma * (1.0 + gate * (1.0 - sigma))).astype(BF16)
            up_cot = (act_cot * swish).astype(BF16)
            cots_all[slot, first:last, 0:128] = gate_cot
            cots_all[slot, first:last, 128:256] = up_cot
            tin_all[first:last] += jnp.sum(
                gate_cot.astype(F32) * tail[:, 0:128] + up_cot.astype(F32) * tail[:, 128:256],
                axis=1,
                keepdims=True,
            )
            return carry

        lax.fori_loop(low, high, block, 0)

    def backward(first, last):
        def block(slot, carry):
            back[first:last] += dot_lanes(cots_all[slot, first:last], w_all[slot, :, 0:256])
            return carry

        back[first:last] = dot_lanes(cots_all[0, first:last], w_all[0, :, 0:256])
        lax.fori_loop(1, LINE, block, 0)
        for r in range(first, last, CAP):
            inverse = inv_all[r : r + CAP]
            unit = in_all[r : r + CAP].astype(F32) * inverse
            scaled = back[r : r + CAP] * gain_head
            inner = jnp.sum(scaled * unit, axis=1, keepdims=True) + tin_all[r : r + CAP] * inverse
            part_all[r : r + CAP] = (
                (scaled - unit * (inner / (2 * width))) * inverse
            ).astype(BF16)

    def part_of(step, lanes=slice(None)):
        row = Y_ROW[Y_ORDER.index(step)]
        return part_all.at[row : row + CAP, lanes]

    normalise(*NEAR)
    for copy in tail_copies + w_twin:
        copy.wait_recv()
    forward(*NEAR, 0, LINE - 1)
    relay_last(1)
    normed_t[0] = normed[0 : FAR[0]].T
    cot_t[0] = cot_all[0 : FAR[0]].T
    first_twins = len(w_twin)
    w_far_a.wait_recv()
    swap(3, 0)
    w_far_b.wait_recv()
    swap(3, 1)
    relay_last(0)
    for copy in w_twin[first_twins:]:
        copy.wait_recv()
    forward(*NEAR, LINE - 1, LINE)

    def near_product(slot, carry):
        g_acc[slot, :, 0:256] = dot(normed_t[0], cots_all[slot, 0 : FAR[0]])
        g_acc[slot, :, 256:384] = dot(cot_t[0], act_all[slot, 0 : FAR[0]])
        return carry

    lax.fori_loop(0, LINE, near_product, 0)

    wait_last(1)
    cot_t[1] = cot_all[FAR[0] : ROWS].T
    wait_last(0)
    normalise(*FAR)
    forward(*FAR, 0, LINE)
    normed_t[1] = normed[FAR[0] : ROWS].T

    def far_product(start, count, slot):
        some = pl.ds(pl.multiple_of(start, 128), count)
        wide = dot(normed_t[1, some], cots_all[slot, FAR[0] : ROWS])
        narrow = dot(cot_t[1, some], act_all[slot, FAR[0] : ROWS])
        return wide + g_acc[slot, some, 0:256], narrow + g_acc[slot, some, 256:384]

    def theirs(low, high):
        def block(slot, carry):
            wide, narrow = far_product((1 - core) * half + low, high - low, slot)
            g_out[slot, low:high, 0:256] = wide.astype(BF16)
            g_out[slot, low:high, 256:384] = narrow.astype(BF16)
            return carry

        lax.fori_loop(0, LINE, block, 0)

    def cut(part):
        return slice(PIECES[part], PIECES[part + 1])

    def halves(part):
        first, last = PIECES[part], PIECES[part + 1]
        mid = (first + last) // 2
        return slice(first, mid), slice(mid, last)

    def pair(part):
        return send(g_out.at[:, cut(part)], g_in.at[:, cut(part)], sibling)

    theirs(0, PIECES[1])
    pair_copies = [pair(0)]
    theirs(PIECES[1], half)
    pair_copies += [pair(part) for part in range(1, PARTS)]

    def ours(slot, carry):
        wide, narrow = far_product(core * half, half, slot)
        some = pl.ds(pl.multiple_of(core * half, half), half)
        g_acc[slot, some, 0:256] = wide
        g_acc[slot, some, 256:384] = narrow
        return carry

    lax.fori_loop(0, LINE, ours, 0)

    x_first, x_second, z_first, z_near, z_far, last_copies = ({} for _ in range(6))

    def rows_of(which, part):
        count = PIECES[part + 1] - PIECES[part]
        return pl.ds(pl.multiple_of(which * half + PIECES[part], 128), count)

    def own_rows(part):
        return rows_of(core, part)

    def x_start(part):
        pair_copies[part].wait_recv()

        def add(slot, carry):
            total = g_acc[slot, own_rows(part)] + g_in[slot, cut(part)].astype(F32)
            g_x[slot, cut(part)] = total.astype(BF16)
            return carry

        lax.fori_loop(1, LINE, add, 0)
        low, high = halves(part)
        x_first[part] = (
            send(g_x.at[3, low], x_opp.at[low], x_dev(1)),
            send(g_x.at[3, high], x_opp.at[high], x_dev(-1)),
            send(g_x.at[2, high], x_in.at[0, high], x_dev(1)),
            send(g_x.at[1, low], x_in.at[1, low], x_dev(-1)),
        )

    def x_relay(part):
        low, high = halves(part)
        x_first[part][0].wait_recv()
        g_x[2, low] = (g_x[2, low].astype(F32) + x_opp[low].astype(F32)).astype(BF16)
        right = send(g_x.at[2, low], x_in.at[0, low], x_dev(1))
        x_first[part][1].wait_recv()
        g_x[1, high] = (g_x[1, high].astype(F32) + x_opp[high].astype(F32)).astype(BF16)
        left = send(g_x.at[1, high], x_in.at[1, high], x_dev(-1))
        x_second[part] = (right, left)

    def z_cut(part, step, base=0):
        count = (PIECES[part + 1] - PIECES[part]) // n_z
        start = base + PIECES[part] + lax.rem(z + step + n_z, n_z) * count
        return pl.ds(pl.multiple_of(start, 16), count)

    def z_slot(part):
        return slice(PIECES[part] // n_z, PIECES[part + 1] // n_z)

    def z_start(part):
        for copy in x_first[part][2:] + x_second[part]:
            copy.wait_recv()
        h_all[cut(part)] = (
            g_acc[0, own_rows(part)]
            + g_in[0, cut(part)].astype(F32)
            + x_in[0, cut(part)].astype(F32)
            + x_in[1, cut(part)].astype(F32)
        ).astype(BF16)
        z_first[part] = [
            send(h_all.at[z_cut(part, step)], z_in.at[index, z_slot(part)], z_dev(step))
            for index, step in enumerate((4, 3, -3, 2, -2, 1, -1))
        ]

    def z_final(part, step):
        return z_cut(part, step, core * half)

    def z_sum(part):
        total = h_all[z_cut(part, 0)].astype(F32)
        for index, copy in enumerate(z_first[part]):
            copy.wait_recv()
            total = total + z_in[index, z_slot(part)].astype(F32)
        final[z_final(part, 0)] = total.astype(BF16)
        mine = final.at[z_final(part, 0)]
        steps = (2, -2, 1, -1) if part < PARTS - 1 else (4, 3, -3, 2, -2, 1, -1)
        z_near[part] = [send(mine, mine, z_dev(step)) for step in steps]

    def z_spread(part):
        copies = []
        for side, step in ((0, 1), (1, -1)):
            z_near[part][side].wait_recv()
            theirs = final.at[z_final(part, -2 * step)]
            copies.append(send(theirs, theirs, z_dev(step)))
            if side == (0 if part == 1 else 1):
                copies.append(send(theirs, theirs, z_dev(2 * step)))
        z_far[part] = copies

    def z_end(part):
        waits = z_near[part][2:] + z_far[part] if part < PARTS - 1 else z_near[part]
        for copy in waits:
            copy.wait_recv()
        mine = final.at[own_rows(part)]
        last_copies[part] = send(mine, mine, sibling)

    x_start(0)
    backward(*NEAR)
    x_start(1)
    y_copies = [
        send(part_of(1), y_in.at[0], y_dev(1)),
        send(part_of(-1), y_in.at[1], y_dev(-1)),
    ]
    x_relay(0)
    backward(*FAR)
    x_start(2)
    y_relays = [
        send(part_of(3), y_relay.at[0], y_dev(1)),
        send(part_of(-3), y_relay.at[1], y_dev(-1)),
        send(part_of(4, slice(0, half)), y_cross.at[0], y_dev(2)),
        send(part_of(4, slice(half, width)), y_cross.at[1], y_dev(-2)),
    ]
    x_relay(1)

    def tail_rows(slot, carry):
        row = jnp.sum(cots_all[slot].astype(F32) * inv_all[...], axis=0, keepdims=True)
        v_out[slot] = jnp.broadcast_to(row, (8, 256))
        return carry

    lax.fori_loop(0, LINE, tail_rows, 0)
    v_copies = [
        send(v_out.at[1], v_in.at[0], x_dev(-1)),
        send(v_out.at[2], v_in.at[1], x_dev(1)),
        send(v_out.at[3], v_in.at[2], x_dev(2)),
    ]
    x_relay(2)
    z_start(0)

    for copy in v_copies:
        copy.wait_recv()
    v_pair[...] = v_out[0] + v_in[0] + v_in[1] + v_in[2]
    v_swap = send(v_pair, v_sib, sibling)

    z_start(1)
    v_swap.wait_recv()
    v_all[z] = v_pair[...] + v_sib[...]
    v_spread = [send(v_all.at[z], v_all.at[z], z_dev(step)) for step in range(1, n_z)]

    for copy in y_relays:
        copy.wait_recv()
    for side, step in ((0, 2), (1, -2)):
        row = Y_ROW[Y_ORDER.index(step)]
        total = part_all[row : row + CAP].astype(F32) + y_relay[side].astype(F32)
        lanes = slice(side * half, (side + 1) * half)
        other = slice((1 - side) * half, (2 - side) * half)
        y_mid[side, :, lanes] = (total[:, lanes] + y_cross[side].astype(F32)).astype(BF16)
        y_mid[side, :, other] = total[:, other].astype(BF16)
        y_copies.append(send(y_mid.at[side], y_in.at[2 + side], y_dev(step)))

    z_sum(0)
    z_start(2)
    z_sum(1)
    z_spread(0)
    z_sum(2)
    z_spread(1)
    early = len(started)

    for copy in y_copies:
        copy.wait_recv()
    widen_cot = part_all[0:CAP].astype(F32)
    for index in range(4):
        widen_cot = widen_cot + y_in[index].astype(F32)
    spread = dot_rows(chosen, cot_all[0:CAP]) + dot_rows(chosen, widen_cot.astype(BF16))
    ecot[...] = oc_ref[...].astype(F32) + spread
    for r in range(0, rows, CHUNK):
        g_mix[r : r + CHUNK] = ecot[r : r + CHUNK] * slope[r : r + CHUNK]
    edge_copy = send(g_mix.at[0:8], edge, before)

    z_end(0)

    edge_copy.wait_recv()
    g_mix[rows : rows + 8] = edge[...] * (seq < n_seq - 1).astype(F32)
    for r in range(0, rows, CHUNK):
        grad = taps[0] * g_mix[r : r + CHUNK]
        for tap in range(1, KW):
            grad = grad + taps[tap] * g_mix[r + tap : r + tap + CHUNK]
        grad = grad * enc_gain
        value = x_ref[r : r + CHUNK].astype(F32)
        inverse = inv_x[r : r + CHUNK]
        inner = jnp.mean(grad * value, axis=1, keepdims=True) * (inverse * inverse)
        bg_ref[r : r + CHUNK] = (
            ecot[r : r + CHUNK] + (grad - value * inner) * inverse
        ).astype(BF16)
    store(bg_ref, bg_hbm)

    for copy in v_spread:
        copy.wait_recv()
    v_total = v_all[0]
    for chip in range(1, n_z):
        v_total = v_total + v_all[chip]
    v_ref[...] = v_total
    store(v_ref, v_hbm)

    def store_rows(which, part):
        store(final.at[rows_of(which, part)], final_hbm.at[rows_of(which, part)])

    def store_theirs(part):
        last_copies[part].wait_recv()
        store_rows(1 - core, part)

    store_rows(core, 0)
    z_end(1)
    store_rows(core, 1)
    store_theirs(0)
    for copy in started[:early]:
        copy.wait_send()
    z_end(2)
    store_rows(core, 2)
    store_theirs(1)
    store_theirs(2)
    for copy in started[early:]:
        copy.wait_send()
    for copy in stores:
        copy.wait()


def finish(
    bg_hbm, final_hbm, tail_hbm, v_hbm, bg_out, gg_out, ug_out, dg_out, bg, final, tail_b, v_ref, gg, ug, dg, sems
):
    width = final.shape[0]
    copies = []

    def copy(source, target):
        step = pltpu.make_async_copy(source, target, sems.at[len(copies)])
        step.start()
        copies.append(step)
        return step

    load_tail = copy(tail_hbm, tail_b)
    load_v = copy(v_hbm, v_ref)
    load_final = copy(final_hbm, final)
    load_bg = copy(bg_hbm, bg)
    head, tail = slice(0, width), slice(width, 2 * width)
    load_tail.wait()
    load_v.wait()
    gg[tail] = tail_b[...] * v_ref[0:1, 0:128]
    copy(gg.at[tail], gg_out.at[tail])
    ug[tail] = tail_b[...] * v_ref[0:1, 128:256]
    copy(ug.at[tail], ug_out.at[tail])
    load_final.wait()
    gg[head] = final[:, 0:128].astype(F32)
    copy(gg.at[head], gg_out.at[head])
    ug[head] = final[:, 128:256].astype(F32)
    copy(ug.at[head], ug_out.at[head])
    load_bg.wait()
    copy(bg, bg_out)
    dg[...] = final[:, 256:384].astype(F32).T
    copy(dg, dg_out)
    for step in copies[4:]:
        step.wait()


def body(
    bytes_in,
    flags,
    enc_gain,
    conv_weight,
    widen,
    main_gain,
    gate_weight,
    up_weight,
    down_weight,
    out_cot,
):
    rows, width = bytes_in.shape[1:]
    n_y = lax.axis_size("seq") // LINE
    n_z = lax.axis_size("dp") // 2
    assert n_y == len(Y_ORDER)
    half = width // 2
    hbm = pl.BlockSpec(memory_space=pltpu.HBM)
    scratch = [
        ((rows, width), BF16),
        ((width, 384), BF16),
        ((width, 128), F32),
        ((8, 256), F32),
        ((rows, width), BF16),
        ((1, rows), jnp.int32),
        ((8, width // 8), BF16),
        ((KW, width), BF16),
        ((8, width // 8), BF16),
        ((16, width // 8), BF16),
        ((width, 128), BF16),
        ((width, 128), BF16),
        ((128, width), BF16),
        ((rows, width), BF16),
        ((LINE, width, 384), BF16),
        ((LINE, 8, 256), F32),
        ((16, width), BF16),
        ((8, width), F32),
        ((8, width), F32),
        ((rows + 16, width), F32),
        ((rows, 1), F32),
        ((rows, width), BF16),
        ((rows, width), F32),
        ((ROWS, width), BF16),
        ((ROWS, width), BF16),
        ((ROWS, width), BF16),
        ((2, width, ROWS // 2), BF16),
        ((2, width, ROWS // 2), BF16),
        ((ROWS, 1), F32),
        ((ROWS, 1), F32),
        ((LINE, ROWS, 128), BF16),
        ((LINE, ROWS, 256), BF16),
        ((ROWS, width), F32),
        ((ROWS, width), BF16),
        ((4, CAP, width), BF16),
        ((2, CAP, width), BF16),
        ((2, CAP, half), BF16),
        ((2, CAP, width), BF16),
        ((LINE, 8, 256), F32),
        ((LINE - 1, 8, 256), F32),
        ((8, 256), F32),
        ((8, 256), F32),
        ((n_z, 8, 256), F32),
        ((LINE, width, 384), F32),
        ((LINE, half, 384), BF16),
        ((LINE, half, 384), BF16),
        ((LINE, half, 384), BF16),
        ((half, 384), BF16),
        ((2, half, 384), BF16),
        ((half, 384), BF16),
        ((n_z - 1, half // n_z, 384), BF16),
        ((rows, width), F32),
        ((rows + 8, width), F32),
        ((8, width), F32),
    ]
    sums = pl.pallas_call(
        kernel,
        out_shape=(
            jax.ShapeDtypeStruct((rows, width), BF16),
            jax.ShapeDtypeStruct((width, 384), BF16),
            jax.ShapeDtypeStruct((width, 128), F32),
            jax.ShapeDtypeStruct((8, 256), F32),
        ),
        in_specs=[hbm] * 10,
        out_specs=[hbm] * 4,
        scratch_shapes=[pltpu.VMEM(shape, kind) for shape, kind in scratch]
        + [
            pltpu.SemaphoreType.DMA((12,)),
            pltpu.SemaphoreType.DMA((9,)),
            pltpu.SemaphoreType.DMA((144,)),
            pltpu.SemaphoreType.DMA((144,)),
        ],
        compiler_params=pltpu.CompilerParams(
            collective_id=0, has_side_effects=True, vmem_limit_bytes=60 * 1024 * 1024
        ),
    )(
        bytes_in[0],
        flags,
        enc_gain.reshape(8, width // 8),
        conv_weight,
        widen.reshape(8, width // 8),
        main_gain.reshape(16, width // 8),
        gate_weight,
        up_weight,
        down_weight,
        out_cot[0],
    )
    outs = pl.pallas_call(
        finish,
        out_shape=(
            jax.ShapeDtypeStruct((rows, width), BF16),
            jax.ShapeDtypeStruct((2 * width, 128), F32),
            jax.ShapeDtypeStruct((2 * width, 128), F32),
            jax.ShapeDtypeStruct((128, width), F32),
        ),
        in_specs=[hbm] * 4,
        out_specs=[hbm] * 4,
        scratch_shapes=[
            pltpu.VMEM((rows, width), BF16),
            pltpu.VMEM((width, 384), BF16),
            pltpu.VMEM((width, 128), F32),
            pltpu.VMEM((8, 256), F32),
            pltpu.VMEM((2 * width, 128), F32),
            pltpu.VMEM((2 * width, 128), F32),
            pltpu.VMEM((128, width), F32),
            pltpu.SemaphoreType.DMA((10,)),
        ],
        compiler_params=pltpu.CompilerParams(vmem_limit_bytes=60 * 1024 * 1024),
    )(*sums)
    return (outs[0][None], outs[1], outs[2], outs[3])


def solution(mesh):
    in_specs = (
        P("dp", "seq", None),
        P("dp", "seq"),
        P(),
        P(),
        P(),
        P(),
        P(None, "seq"),
        P(None, "seq"),
        P("seq", None),
        P("dp", "seq", None),
    )
    out_specs = (P("dp", "seq", None), P(None, "seq"), P(None, "seq"), P("seq", None))
    return jax.shard_map(body, mesh=mesh, in_specs=in_specs, out_specs=out_specs, check_vma=False)
```

```python
import jax
import jax.numpy as jnp
from jax import lax
from jax.experimental import pallas as pl
from jax.experimental.pallas import tpu as pltpu
from jax.sharding import PartitionSpec as P

MESH = pl.DeviceIdType.MESH
F32 = jnp.float32
BF16 = jnp.bfloat16

KW = 4
CAP = 48
EPS = 1e-05
LINE = 4
PIECES = (0, 128, 384, 512)
PARTS = len(PIECES) - 1
CHUNK = 32

Y_ORDER = (0, -1, 1, -2, 2, -3, 3, 4)
Y_ROW = (0, 48, 96, 144, 192, 256, 304, 352)
NEAR = (0, 240)
FAR = (256, 400)
ROWS = 512
X_ORDER = (0, -1, 1, 2)


def dot(left, right):
    return jnp.dot(left, right, preferred_element_type=F32)


def dot_rows(left, right):
    return lax.dot_general(left, right, (((0,), (0,)), ((), ())), preferred_element_type=F32)


def dot_lanes(left, right):
    return lax.dot_general(left, right, (((1,), (1,)), ((), ())), preferred_element_type=F32)


def as_row(value):
    value = value.astype(F32)
    return jnp.concatenate([value[i : i + 1] for i in range(value.shape[0])], axis=1)


def kernel(
    x_hbm,
    marks_hbm,
    enc_gain_hbm,
    conv_hbm,
    widen_hbm,
    main_gain_hbm,
    gw_hbm,
    uw_hbm,
    dw_hbm,
    oc_hbm,
    bg_hbm,
    final_hbm,
    tail_hbm,
    v_hbm,
    bg_ref,
    final,
    tail_b,
    v_ref,
    x_ref,
    marks_ref,
    enc_gain_ref,
    conv_ref,
    widen_ref,
    main_gain_ref,
    gw_tail,
    uw_tail,
    dw_ref,
    oc_ref,
    w_all,
    tails,
    halo,
    lead_out,
    lead_in,
    norm_x,
    inv_x,
    enc_out,
    slope,
    in_all,
    cot_all,
    normed,
    normed_t,
    cot_t,
    inv_all,
    tin_all,
    act_all,
    cots_all,
    back,
    part_all,
    y_in,
    y_relay,
    y_cross,
    y_mid,
    v_out,
    v_in,
    v_pair,
    v_sib,
    v_all,
    g_acc,
    g_out,
    g_in,
    g_x,
    x_opp,
    x_in,
    h_all,
    z_in,
    ecot,
    g_mix,
    edge,
    load_sems,
    store_sems,
    send_sems,
    recv_sems,
):
    n_seq = lax.axis_size("seq")
    n_y = n_seq // LINE
    n_z = lax.axis_size("dp") // 2
    dp = lax.axis_index("dp")
    seq = lax.axis_index("seq")
    z, core = dp // 2, dp % 2
    y, x = seq // LINE, seq % LINE
    rows, width = x_ref.shape
    half = width // 2

    def y_dev(step):
        return {"seq": lax.rem(y + step + n_y, n_y) * LINE + x}

    def x_dev(step):
        return {"seq": y * LINE + lax.rem(x + step + LINE, LINE)}

    def z_dev(step):
        return {"dp": lax.rem(z + step + n_z, n_z) * 2 + core}

    sibling = {"dp": z * 2 + 1 - core}
    after = {"seq": lax.rem(seq + 1, n_seq)}
    before = {"seq": lax.rem(seq + n_seq - 1, n_seq)}

    loads = []
    stores = []

    def load(source, target):
        copy = pltpu.make_async_copy(source, target, load_sems.at[len(loads)])
        copy.start()
        loads.append(copy)
        return copy

    def store(source, target):
        copy = pltpu.make_async_copy(source, target, store_sems.at[len(stores)])
        copy.start()
        stores.append(copy)

    load_marks = load(marks_hbm, marks_ref)
    load_oc = load(oc_hbm, oc_ref)

    started = []

    def send(source, target, device):
        index = len(started)
        copy = pltpu.make_async_remote_copy(
            src_ref=source,
            dst_ref=target,
            send_sem=send_sems.at[index],
            recv_sem=recv_sems.at[index],
            device_id=device,
            device_id_type=MESH,
        )
        copy.start()
        started.append(copy)
        return copy

    barrier = pltpu.get_barrier_semaphore()
    peers = [y_dev(step) for step in (1, -1, 2, -2)]
    peers += [x_dev(step) for step in (1, -1, 2)]
    peers += [z_dev(step) for step in range(1, n_z)]
    peers += [sibling, after, before]
    for peer in peers:
        pl.semaphore_signal(barrier, inc=1, device_id=peer, device_id_type=MESH)

    load_x = load(x_hbm, x_ref)
    load_gain = load(enc_gain_hbm, enc_gain_ref)
    load_conv = load(conv_hbm, conv_ref)
    load_w = [
        load(dw_hbm, dw_ref),
        load(gw_hbm.at[0:width], w_all.at[0, :, 0:128]),
        load(uw_hbm.at[0:width], w_all.at[0, :, 128:256]),
    ]
    load_tail = [
        load(widen_hbm, widen_ref),
        load(main_gain_hbm, main_gain_ref),
        load(gw_hbm.at[width : 2 * width], gw_tail),
        load(uw_hbm.at[width : 2 * width], uw_tail),
    ]

    load_marks.wait()
    marks = marks_ref[...].astype(F32)
    upper = (
        lax.broadcasted_iota(jnp.int32, (rows, rows), 0)
        <= lax.broadcasted_iota(jnp.int32, (rows, rows), 1)
    ).astype(F32).astype(BF16)
    running = dot(jnp.broadcast_to(marks, (16, rows)).astype(BF16), upper)
    lead = jnp.where(running == 0.0, 1.0, 0.0).astype(BF16)
    slot_ids = lax.broadcasted_iota(jnp.int32, (CAP, rows), 0).astype(F32)
    member = jnp.where(slot_ids == running[0:1] - 1.0, 1.0, 0.0)
    chosen = (member * marks).astype(BF16)
    last_slot = jnp.where(slot_ids[:, 0:1] == running[0:1, rows - 1 : rows] - 1.0, 1.0, 0.0)
    load_oc.wait()
    lead_out[...] = dot(lead, oc_ref[...])[0:8]

    pl.semaphore_wait(barrier, len(peers))

    halo_copy = send(x_hbm.at[rows - 16 : rows], halo, after)
    lead_copy = send(lead_out, lead_in, before)
    own_sums = dot(member.astype(BF16), oc_ref[...])

    for copy in load_w:
        copy.wait()
    w_all[0, :, 256:384] = dw_ref[...].astype(F32).T.astype(BF16)

    def w_rows(slot, part):
        start = pl.multiple_of(core * half + part * (half // 2), half // 2)
        return w_all.at[slot, pl.ds(start, half // 2)]

    w_right = [None, None]
    w_left = [None, None]

    def w_send(part):
        w_right[part] = send(w_rows(0, part), w_rows(1, part), x_dev(1))
        w_left[1 - part] = send(w_rows(0, 1 - part), w_rows(2, 1 - part), x_dev(-1))

    w_send(0)

    ring = {}

    def pass_on(which, side, direction, step):
        buffer = (in_all, cot_all)[which]
        lanes = slice(side * half, (side + 1) * half)
        here = Y_ROW[Y_ORDER.index(-direction * step)]
        there = Y_ROW[Y_ORDER.index(4 if step == 3 else -direction * (step + 1))]
        ring[which, side, direction, step] = send(
            buffer.at[here : here + CAP, lanes],
            buffer.at[there : there + CAP, lanes],
            y_dev(direction),
        )

    def first_hop(which):
        for side in (0, 1):
            for direction in (1, -1):
                pass_on(which, side, direction, 0)

    load_gain.wait()
    load_conv.wait()
    load_x.wait()
    enc_gain = as_row(enc_gain_ref[...])
    taps = [conv_ref[tap : tap + 1, :].astype(F32) for tap in range(KW)]
    for r in range(0, rows, CHUNK):
        value = x_ref[r : r + CHUNK].astype(F32)
        inverse = lax.rsqrt(jnp.mean(value * value, axis=1, keepdims=True) + EPS)
        inv_x[r : r + CHUNK] = inverse
        norm_x[16 + r : 16 + r + CHUNK] = value * inverse * enc_gain
    lead_copy.wait_recv()
    carried = lead_in[0:1] * (seq < n_seq - 1).astype(F32)
    cot_all[0:CAP] = (own_sums + last_slot * carried).astype(BF16)
    first_hop(1)

    halo_copy.wait_recv()
    value = halo[...].astype(F32) * (seq > 0).astype(F32)
    inverse = lax.rsqrt(jnp.mean(value * value, axis=1, keepdims=True) + EPS)
    norm_x[0:16] = value * inverse * enc_gain
    for r in range(0, rows, CHUNK):
        mixed = taps[0] * norm_x[16 + r : 16 + r + CHUNK]
        for tap in range(1, KW):
            mixed = mixed + taps[tap] * norm_x[16 + r - tap : 16 + r - tap + CHUNK]
        sigma = jax.nn.sigmoid(mixed)
        enc_out[r : r + CHUNK] = (x_ref[r : r + CHUNK].astype(F32) + mixed * sigma).astype(BF16)
        slope[r : r + CHUNK] = sigma * (1.0 + mixed * (1.0 - sigma))
    in_all[0:CAP] = dot(chosen, enc_out[...]).astype(BF16)
    first_hop(0)
    w_send(1)

    w_twin = []

    def swap(slot, part):
        w_twin.append(send(w_rows(slot, part), w_rows(slot, part), sibling))

    for copy in load_tail:
        copy.wait()
    widen = as_row(widen_ref[...])
    main_gain = as_row(main_gain_ref[...])
    gain_head = main_gain[:, 0:width]
    tail_vec = widen * main_gain[:, width : 2 * width]
    tail_square = jnp.sum(widen * widen, axis=1, keepdims=True)
    tail_b[...] = jnp.broadcast_to(tail_vec, (128, width)).T
    store(tail_b, tail_hbm)
    tail_gate = jnp.sum(gw_tail[...].astype(F32) * tail_b[...], axis=0, keepdims=True)
    tail_up = jnp.sum(uw_tail[...].astype(F32) * tail_b[...], axis=0, keepdims=True)
    tails[0, :, 0:128] = jnp.broadcast_to(tail_gate, (8, 128))
    tails[0, :, 128:256] = jnp.broadcast_to(tail_up, (8, 128))
    tail_copies = [
        send(tails.at[0], tails.at[1], x_dev(1)),
        send(tails.at[0], tails.at[2], x_dev(-1)),
        send(tails.at[0], tails.at[3], x_dev(2)),
    ]

    def relay(which, step):
        for side in (0, 1):
            for direction in (1, -1):
                ring[which, side, direction, step - 1].wait_recv()
                pass_on(which, side, direction, step)

    def relay_last(which):
        for side, direction in ((0, 1), (1, -1)):
            ring[which, side, direction, 2].wait_recv()
            pass_on(which, side, direction, 3)

    def wait_last(which):
        for side, direction in ((0, 1), (1, -1)):
            ring[which, 1 - side, direction, 2].wait_recv()
            ring[which, side, direction, 3].wait_recv()

    relay(1, 1)
    relay(0, 1)
    w_right[0].wait_recv()
    w_far_a = send(w_rows(1, 0), w_rows(3, 0), x_dev(1))
    w_left[1].wait_recv()
    w_far_b = send(w_rows(2, 1), w_rows(3, 1), x_dev(-1))
    swap(1, 0)
    swap(2, 1)
    for first, last in ((NEAR[1], FAR[0]), (FAR[1], ROWS)):
        count = last - first
        normed[first:last] = jnp.zeros((count, width), BF16)
        cot_all[first:last] = jnp.zeros((count, width), BF16)
        inv_all[first:last] = jnp.zeros((count, 1), F32)
        act_all[:, first:last] = jnp.zeros((LINE, count, 128), BF16)
        cots_all[:, first:last] = jnp.zeros((LINE, count, 256), BF16)
    relay(1, 2)
    relay(0, 2)
    w_right[1].wait_recv()
    swap(1, 1)
    w_left[0].wait_recv()
    swap(2, 0)

    def normalise(first, last):
        for r in range(first, last, CAP):
            head = in_all[r : r + CAP].astype(F32)
            square = jnp.sum(head * head, axis=1, keepdims=True) + tail_square
            inverse = lax.rsqrt(square / (2 * width) + EPS)
            inv_all[r : r + CAP] = inverse
            normed[r : r + CAP] = (head * inverse * gain_head).astype(BF16)
        tin_all[first:last] = jnp.zeros((last - first, 1), F32)

    def forward(first, last, low, high):
        def block(slot, carry):
            tail = tails[slot, 0:1, :]
            both = dot(normed[first:last], w_all[slot, :, 0:256]) + inv_all[first:last] * tail
            act_cot = dot(cot_all[first:last], w_all[slot, :, 256:384])
            gate, up = both[:, 0:128], both[:, 128:256]
            sigma = jax.nn.sigmoid(gate)
            swish = gate * sigma
            act_all[slot, first:last, :] = (swish * up).astype(BF16)
            gate_cot = (act_cot * up * sigma * (1.0 + gate * (1.0 - sigma))).astype(BF16)
            up_cot = (act_cot * swish).astype(BF16)
            cots_all[slot, first:last, 0:128] = gate_cot
            cots_all[slot, first:last, 128:256] = up_cot
            tin_all[first:last] += jnp.sum(
                gate_cot.astype(F32) * tail[:, 0:128] + up_cot.astype(F32) * tail[:, 128:256],
                axis=1,
                keepdims=True,
            )
            return carry

        lax.fori_loop(low, high, block, 0)

    def backward(first, last):
        def block(slot, carry):
            back[first:last] += dot_lanes(cots_all[slot, first:last], w_all[slot, :, 0:256])
            return carry

        back[first:last] = dot_lanes(cots_all[0, first:last], w_all[0, :, 0:256])
        lax.fori_loop(1, LINE, block, 0)
        for r in range(first, last, CAP):
            inverse = inv_all[r : r + CAP]
            unit = in_all[r : r + CAP].astype(F32) * inverse
            scaled = back[r : r + CAP] * gain_head
            inner = jnp.sum(scaled * unit, axis=1, keepdims=True) + tin_all[r : r + CAP] * inverse
            part_all[r : r + CAP] = (
                (scaled - unit * (inner / (2 * width))) * inverse
            ).astype(BF16)

    def part_of(step, lanes=slice(None)):
        row = Y_ROW[Y_ORDER.index(step)]
        return part_all.at[row : row + CAP, lanes]

    normalise(*NEAR)
    for copy in tail_copies + w_twin:
        copy.wait_recv()
    forward(*NEAR, 0, LINE - 1)
    relay_last(1)
    normed_t[0] = normed[0 : FAR[0]].T
    cot_t[0] = cot_all[0 : FAR[0]].T
    first_twins = len(w_twin)
    w_far_a.wait_recv()
    swap(3, 0)
    w_far_b.wait_recv()
    swap(3, 1)
    relay_last(0)
    for copy in w_twin[first_twins:]:
        copy.wait_recv()
    forward(*NEAR, LINE - 1, LINE)

    def near_product(slot, carry):
        g_acc[slot, :, 0:256] = dot(normed_t[0], cots_all[slot, 0 : FAR[0]])
        g_acc[slot, :, 256:384] = dot(cot_t[0], act_all[slot, 0 : FAR[0]])
        return carry

    lax.fori_loop(0, LINE, near_product, 0)

    wait_last(1)
    cot_t[1] = cot_all[FAR[0] : ROWS].T
    wait_last(0)
    normalise(*FAR)
    forward(*FAR, 0, LINE)
    normed_t[1] = normed[FAR[0] : ROWS].T

    def far_product(start, count, slot):
        some = pl.ds(pl.multiple_of(start, 128), count)
        wide = dot(normed_t[1, some], cots_all[slot, FAR[0] : ROWS])
        narrow = dot(cot_t[1, some], act_all[slot, FAR[0] : ROWS])
        return wide + g_acc[slot, some, 0:256], narrow + g_acc[slot, some, 256:384]

    def theirs(low, high):
        def block(slot, carry):
            wide, narrow = far_product((1 - core) * half + low, high - low, slot)
            g_out[slot, low:high, 0:256] = wide.astype(BF16)
            g_out[slot, low:high, 256:384] = narrow.astype(BF16)
            return carry

        lax.fori_loop(0, LINE, block, 0)

    def cut(part):
        return slice(PIECES[part], PIECES[part + 1])

    def halves(part):
        first, last = PIECES[part], PIECES[part + 1]
        mid = (first + last) // 2
        return slice(first, mid), slice(mid, last)

    def pair(part):
        return send(g_out.at[:, cut(part)], g_in.at[:, cut(part)], sibling)

    theirs(0, PIECES[1])
    pair_copies = [pair(0)]
    theirs(PIECES[1], half)
    pair_copies += [pair(part) for part in range(1, PARTS)]

    def ours(slot, carry):
        wide, narrow = far_product(core * half, half, slot)
        some = pl.ds(pl.multiple_of(core * half, half), half)
        g_acc[slot, some, 0:256] = wide
        g_acc[slot, some, 256:384] = narrow
        return carry

    lax.fori_loop(0, LINE, ours, 0)

    x_first, x_second, z_first, z_near, z_far, last_copies = ({} for _ in range(6))

    def rows_of(which, part):
        count = PIECES[part + 1] - PIECES[part]
        return pl.ds(pl.multiple_of(which * half + PIECES[part], 128), count)

    def own_rows(part):
        return rows_of(core, part)

    def x_start(part):
        pair_copies[part].wait_recv()

        def add(slot, carry):
            total = g_acc[slot, own_rows(part)] + g_in[slot, cut(part)].astype(F32)
            g_x[slot, cut(part)] = total.astype(BF16)
            return carry

        lax.fori_loop(1, LINE, add, 0)
        low, high = halves(part)
        x_first[part] = (
            send(g_x.at[3, low], x_opp.at[low], x_dev(1)),
            send(g_x.at[3, high], x_opp.at[high], x_dev(-1)),
            send(g_x.at[2, high], x_in.at[0, high], x_dev(1)),
            send(g_x.at[1, low], x_in.at[1, low], x_dev(-1)),
        )

    def x_relay(part):
        low, high = halves(part)
        x_first[part][0].wait_recv()
        g_x[2, low] = (g_x[2, low].astype(F32) + x_opp[low].astype(F32)).astype(BF16)
        right = send(g_x.at[2, low], x_in.at[0, low], x_dev(1))
        x_first[part][1].wait_recv()
        g_x[1, high] = (g_x[1, high].astype(F32) + x_opp[high].astype(F32)).astype(BF16)
        left = send(g_x.at[1, high], x_in.at[1, high], x_dev(-1))
        x_second[part] = (right, left)

    def z_cut(part, step, base=0):
        count = (PIECES[part + 1] - PIECES[part]) // n_z
        start = base + PIECES[part] + lax.rem(z + step + n_z, n_z) * count
        return pl.ds(pl.multiple_of(start, 16), count)

    def z_slot(part):
        return slice(PIECES[part] // n_z, PIECES[part + 1] // n_z)

    def z_start(part):
        for copy in x_first[part][2:] + x_second[part]:
            copy.wait_recv()
        h_all[cut(part)] = (
            g_acc[0, own_rows(part)]
            + g_in[0, cut(part)].astype(F32)
            + x_in[0, cut(part)].astype(F32)
            + x_in[1, cut(part)].astype(F32)
        ).astype(BF16)
        z_first[part] = [
            send(h_all.at[z_cut(part, step)], z_in.at[index, z_slot(part)], z_dev(step))
            for index, step in enumerate((4, 3, -3, 2, -2, 1, -1))
        ]

    def z_final(part, step):
        return z_cut(part, step, core * half)

    def z_sum(part):
        total = h_all[z_cut(part, 0)].astype(F32)
        for index, copy in enumerate(z_first[part]):
            copy.wait_recv()
            total = total + z_in[index, z_slot(part)].astype(F32)
        final[z_final(part, 0)] = total.astype(BF16)
        mine = final.at[z_final(part, 0)]
        steps = (2, -2, 1, -1) if part < PARTS - 1 else (4, 3, -3, 2, -2, 1, -1)
        z_near[part] = [send(mine, mine, z_dev(step)) for step in steps]

    def z_spread(part):
        copies = []
        for side, step in ((0, 1), (1, -1)):
            z_near[part][side].wait_recv()
            theirs = final.at[z_final(part, -2 * step)]
            copies.append(send(theirs, theirs, z_dev(step)))
            if side == (0 if part == 1 else 1):
                copies.append(send(theirs, theirs, z_dev(2 * step)))
        z_far[part] = copies

    def z_end(part):
        waits = z_near[part][2:] + z_far[part] if part < PARTS - 1 else z_near[part]
        for copy in waits:
            copy.wait_recv()
        mine = final.at[own_rows(part)]
        last_copies[part] = send(mine, mine, sibling)

    x_start(0)
    backward(*NEAR)
    x_start(1)
    y_copies = [
        send(part_of(1), y_in.at[0], y_dev(1)),
        send(part_of(-1), y_in.at[1], y_dev(-1)),
    ]
    x_relay(0)
    backward(*FAR)
    x_start(2)
    y_relays = [
        send(part_of(3), y_relay.at[0], y_dev(1)),
        send(part_of(-3), y_relay.at[1], y_dev(-1)),
        send(part_of(4, slice(0, half)), y_cross.at[0], y_dev(2)),
        send(part_of(4, slice(half, width)), y_cross.at[1], y_dev(-2)),
    ]
    x_relay(1)

    def tail_rows(slot, carry):
        row = jnp.sum(cots_all[slot].astype(F32) * inv_all[...], axis=0, keepdims=True)
        v_out[slot] = jnp.broadcast_to(row, (8, 256))
        return carry

    lax.fori_loop(0, LINE, tail_rows, 0)
    v_copies = [
        send(v_out.at[1], v_in.at[0], x_dev(-1)),
        send(v_out.at[2], v_in.at[1], x_dev(1)),
        send(v_out.at[3], v_in.at[2], x_dev(2)),
    ]
    z_start(0)
    x_relay(2)

    for copy in v_copies:
        copy.wait_recv()
    v_pair[...] = v_out[0] + v_in[0] + v_in[1] + v_in[2]
    v_swap = send(v_pair, v_sib, sibling)

    z_sum(0)
    z_start(1)
    v_swap.wait_recv()
    v_all[z] = v_pair[...] + v_sib[...]
    v_spread = [send(v_all.at[z], v_all.at[z], z_dev(step)) for step in range(1, n_z)]

    for copy in y_relays:
        copy.wait_recv()
    for side, step in ((0, 2), (1, -2)):
        row = Y_ROW[Y_ORDER.index(step)]
        total = part_all[row : row + CAP].astype(F32) + y_relay[side].astype(F32)
        lanes = slice(side * half, (side + 1) * half)
        other = slice((1 - side) * half, (2 - side) * half)
        y_mid[side, :, lanes] = (total[:, lanes] + y_cross[side].astype(F32)).astype(BF16)
        y_mid[side, :, other] = total[:, other].astype(BF16)
        y_copies.append(send(y_mid.at[side], y_in.at[2 + side], y_dev(step)))

    z_spread(0)
    z_start(2)
    z_sum(1)
    z_sum(2)
    z_spread(1)
    early = len(started)

    for copy in y_copies:
        copy.wait_recv()
    widen_cot = part_all[0:CAP].astype(F32)
    for index in range(4):
        widen_cot = widen_cot + y_in[index].astype(F32)
    spread = dot_rows(chosen, cot_all[0:CAP]) + dot_rows(chosen, widen_cot.astype(BF16))
    ecot[...] = oc_ref[...].astype(F32) + spread
    for r in range(0, rows, CHUNK):
        g_mix[r : r + CHUNK] = ecot[r : r + CHUNK] * slope[r : r + CHUNK]
    edge_copy = send(g_mix.at[0:8], edge, before)

    z_end(0)

    edge_copy.wait_recv()
    g_mix[rows : rows + 8] = edge[...] * (seq < n_seq - 1).astype(F32)
    for r in range(0, rows, CHUNK):
        grad = taps[0] * g_mix[r : r + CHUNK]
        for tap in range(1, KW):
            grad = grad + taps[tap] * g_mix[r + tap : r + tap + CHUNK]
        grad = grad * enc_gain
        value = x_ref[r : r + CHUNK].astype(F32)
        inverse = inv_x[r : r + CHUNK]
        inner = jnp.mean(grad * value, axis=1, keepdims=True) * (inverse * inverse)
        bg_ref[r : r + CHUNK] = (
            ecot[r : r + CHUNK] + (grad - value * inner) * inverse
        ).astype(BF16)
    store(bg_ref, bg_hbm)

    for copy in v_spread:
        copy.wait_recv()
    v_total = v_all[0]
    for chip in range(1, n_z):
        v_total = v_total + v_all[chip]
    v_ref[...] = v_total
    store(v_ref, v_hbm)

    def store_rows(which, part):
        store(final.at[rows_of(which, part)], final_hbm.at[rows_of(which, part)])

    def store_theirs(part):
        last_copies[part].wait_recv()
        store_rows(1 - core, part)

    store_rows(core, 0)
    z_end(1)
    store_rows(core, 1)
    store_theirs(0)
    for copy in started[:early]:
        copy.wait_send()
    z_end(2)
    store_rows(core, 2)
    store_theirs(1)
    store_theirs(2)
    for copy in started[early:]:
        copy.wait_send()
    for copy in stores:
        copy.wait()


def finish(
    bg_hbm, final_hbm, tail_hbm, v_hbm, bg_out, gg_out, ug_out, dg_out, bg, final, tail_b, v_ref, gg, ug, dg, sems
):
    width = final.shape[0]
    copies = []

    def copy(source, target):
        step = pltpu.make_async_copy(source, target, sems.at[len(copies)])
        step.start()
        copies.append(step)
        return step

    load_tail = copy(tail_hbm, tail_b)
    load_v = copy(v_hbm, v_ref)
    load_final = copy(final_hbm, final)
    load_bg = copy(bg_hbm, bg)
    head, tail = slice(0, width), slice(width, 2 * width)
    load_tail.wait()
    load_v.wait()
    gg[tail] = tail_b[...] * v_ref[0:1, 0:128]
    copy(gg.at[tail], gg_out.at[tail])
    ug[tail] = tail_b[...] * v_ref[0:1, 128:256]
    copy(ug.at[tail], ug_out.at[tail])
    load_final.wait()
    gg[head] = final[:, 0:128].astype(F32)
    copy(gg.at[head], gg_out.at[head])
    ug[head] = final[:, 128:256].astype(F32)
    copy(ug.at[head], ug_out.at[head])
    load_bg.wait()
    copy(bg, bg_out)
    dg[...] = final[:, 256:384].astype(F32).T
    copy(dg, dg_out)
    for step in copies[4:]:
        step.wait()


def body(
    bytes_in,
    flags,
    enc_gain,
    conv_weight,
    widen,
    main_gain,
    gate_weight,
    up_weight,
    down_weight,
    out_cot,
):
    rows, width = bytes_in.shape[1:]
    n_y = lax.axis_size("seq") // LINE
    n_z = lax.axis_size("dp") // 2
    assert n_y == len(Y_ORDER)
    half = width // 2
    hbm = pl.BlockSpec(memory_space=pltpu.HBM)
    scratch = [
        ((rows, width), BF16),
        ((width, 384), BF16),
        ((width, 128), F32),
        ((8, 256), F32),
        ((rows, width), BF16),
        ((1, rows), jnp.int32),
        ((8, width // 8), BF16),
        ((KW, width), BF16),
        ((8, width // 8), BF16),
        ((16, width // 8), BF16),
        ((width, 128), BF16),
        ((width, 128), BF16),
        ((128, width), BF16),
        ((rows, width), BF16),
        ((LINE, width, 384), BF16),
        ((LINE, 8, 256), F32),
        ((16, width), BF16),
        ((8, width), F32),
        ((8, width), F32),
        ((rows + 16, width), F32),
        ((rows, 1), F32),
        ((rows, width), BF16),
        ((rows, width), F32),
        ((ROWS, width), BF16),
        ((ROWS, width), BF16),
        ((ROWS, width), BF16),
        ((2, width, ROWS // 2), BF16),
        ((2, width, ROWS // 2), BF16),
        ((ROWS, 1), F32),
        ((ROWS, 1), F32),
        ((LINE, ROWS, 128), BF16),
        ((LINE, ROWS, 256), BF16),
        ((ROWS, width), F32),
        ((ROWS, width), BF16),
        ((4, CAP, width), BF16),
        ((2, CAP, width), BF16),
        ((2, CAP, half), BF16),
        ((2, CAP, width), BF16),
        ((LINE, 8, 256), F32),
        ((LINE - 1, 8, 256), F32),
        ((8, 256), F32),
        ((8, 256), F32),
        ((n_z, 8, 256), F32),
        ((LINE, width, 384), F32),
        ((LINE, half, 384), BF16),
        ((LINE, half, 384), BF16),
        ((LINE, half, 384), BF16),
        ((half, 384), BF16),
        ((2, half, 384), BF16),
        ((half, 384), BF16),
        ((n_z - 1, half // n_z, 384), BF16),
        ((rows, width), F32),
        ((rows + 8, width), F32),
        ((8, width), F32),
    ]
    sums = pl.pallas_call(
        kernel,
        out_shape=(
            jax.ShapeDtypeStruct((rows, width), BF16),
            jax.ShapeDtypeStruct((width, 384), BF16),
            jax.ShapeDtypeStruct((width, 128), F32),
            jax.ShapeDtypeStruct((8, 256), F32),
        ),
        in_specs=[hbm] * 10,
        out_specs=[hbm] * 4,
        scratch_shapes=[pltpu.VMEM(shape, kind) for shape, kind in scratch]
        + [
            pltpu.SemaphoreType.DMA((12,)),
            pltpu.SemaphoreType.DMA((9,)),
            pltpu.SemaphoreType.DMA((144,)),
            pltpu.SemaphoreType.DMA((144,)),
        ],
        compiler_params=pltpu.CompilerParams(
            collective_id=0, has_side_effects=True, vmem_limit_bytes=60 * 1024 * 1024
        ),
    )(
        bytes_in[0],
        flags,
        enc_gain.reshape(8, width // 8),
        conv_weight,
        widen.reshape(8, width // 8),
        main_gain.reshape(16, width // 8),
        gate_weight,
        up_weight,
        down_weight,
        out_cot[0],
    )
    outs = pl.pallas_call(
        finish,
        out_shape=(
            jax.ShapeDtypeStruct((rows, width), BF16),
            jax.ShapeDtypeStruct((2 * width, 128), F32),
            jax.ShapeDtypeStruct((2 * width, 128), F32),
            jax.ShapeDtypeStruct((128, width), F32),
        ),
        in_specs=[hbm] * 4,
        out_specs=[hbm] * 4,
        scratch_shapes=[
            pltpu.VMEM((rows, width), BF16),
            pltpu.VMEM((width, 384), BF16),
            pltpu.VMEM((width, 128), F32),
            pltpu.VMEM((8, 256), F32),
            pltpu.VMEM((2 * width, 128), F32),
            pltpu.VMEM((2 * width, 128), F32),
            pltpu.VMEM((128, width), F32),
            pltpu.SemaphoreType.DMA((10,)),
        ],
        compiler_params=pltpu.CompilerParams(vmem_limit_bytes=60 * 1024 * 1024),
    )(*sums)
    return (outs[0][None], outs[1], outs[2], outs[3])


def solution(mesh):
    in_specs = (
        P("dp", "seq", None),
        P("dp", "seq"),
        P(),
        P(),
        P(),
        P(),
        P(None, "seq"),
        P(None, "seq"),
        P("seq", None),
        P("dp", "seq", None),
    )
    out_specs = (P("dp", "seq", None), P(None, "seq"), P(None, "seq"), P("seq", None))
    return jax.shard_map(body, mesh=mesh, in_specs=in_specs, out_specs=out_specs, check_vma=False)
```

```python
import jax
import jax.numpy as jnp
from jax import lax
from jax.experimental import pallas as pl
from jax.experimental.pallas import tpu as pltpu
from jax.sharding import PartitionSpec as P

MESH = pl.DeviceIdType.MESH
F32 = jnp.float32
BF16 = jnp.bfloat16

KW = 4
CAP = 48
EPS = 1e-05
LINE = 4
PIECES = (0, 128, 384, 512)
PARTS = len(PIECES) - 1
CHUNK = 32

Y_ORDER = (0, -1, 1, -2, 2, -3, 3, 4)
Y_ROW = (0, 48, 96, 144, 192, 256, 304, 352)
NEAR = (0, 240)
FAR = (256, 400)
THIRD = (256, 352)
OPPOSITE = (352, 400)
ROWS = 512
X_ORDER = (0, -1, 1, 2)


def dot(left, right):
    return jnp.dot(left, right, preferred_element_type=F32)


def dot_rows(left, right):
    return lax.dot_general(left, right, (((0,), (0,)), ((), ())), preferred_element_type=F32)


def dot_lanes(left, right):
    return lax.dot_general(left, right, (((1,), (1,)), ((), ())), preferred_element_type=F32)


def as_row(value):
    value = value.astype(F32)
    return jnp.concatenate([value[i : i + 1] for i in range(value.shape[0])], axis=1)


def kernel(
    x_hbm,
    marks_hbm,
    enc_gain_hbm,
    conv_hbm,
    widen_hbm,
    main_gain_hbm,
    gw_hbm,
    uw_hbm,
    dw_hbm,
    oc_hbm,
    bg_hbm,
    final_hbm,
    tail_hbm,
    v_hbm,
    bg_ref,
    final,
    tail_b,
    v_ref,
    x_ref,
    marks_ref,
    enc_gain_ref,
    conv_ref,
    widen_ref,
    main_gain_ref,
    gw_tail,
    uw_tail,
    dw_ref,
    oc_ref,
    w_all,
    tails,
    halo,
    lead_out,
    lead_in,
    norm_x,
    inv_x,
    enc_out,
    slope,
    in_all,
    cot_all,
    normed,
    normed_t,
    cot_t,
    inv_all,
    tin_all,
    act_all,
    cots_all,
    back,
    part_all,
    y_in,
    y_relay,
    y_cross,
    y_mid,
    v_out,
    v_in,
    v_pair,
    v_sib,
    v_all,
    g_acc,
    g_out,
    g_in,
    g_x,
    x_opp,
    x_in,
    h_all,
    z_in,
    ecot,
    g_mix,
    edge,
    load_sems,
    store_sems,
    send_sems,
    recv_sems,
):
    n_seq = lax.axis_size("seq")
    n_y = n_seq // LINE
    n_z = lax.axis_size("dp") // 2
    dp = lax.axis_index("dp")
    seq = lax.axis_index("seq")
    z, core = dp // 2, dp % 2
    y, x = seq // LINE, seq % LINE
    rows, width = x_ref.shape
    half = width // 2

    def y_dev(step):
        return {"seq": lax.rem(y + step + n_y, n_y) * LINE + x}

    def x_dev(step):
        return {"seq": y * LINE + lax.rem(x + step + LINE, LINE)}

    def z_dev(step):
        return {"dp": lax.rem(z + step + n_z, n_z) * 2 + core}

    sibling = {"dp": z * 2 + 1 - core}
    after = {"seq": lax.rem(seq + 1, n_seq)}
    before = {"seq": lax.rem(seq + n_seq - 1, n_seq)}

    loads = []
    stores = []

    def load(source, target):
        copy = pltpu.make_async_copy(source, target, load_sems.at[len(loads)])
        copy.start()
        loads.append(copy)
        return copy

    def store(source, target):
        copy = pltpu.make_async_copy(source, target, store_sems.at[len(stores)])
        copy.start()
        stores.append(copy)

    load_marks = load(marks_hbm, marks_ref)
    load_oc = load(oc_hbm, oc_ref)

    started = []

    def send(source, target, device):
        index = len(started)
        copy = pltpu.make_async_remote_copy(
            src_ref=source,
            dst_ref=target,
            send_sem=send_sems.at[index],
            recv_sem=recv_sems.at[index],
            device_id=device,
            device_id_type=MESH,
        )
        copy.start()
        started.append(copy)
        return copy

    barrier = pltpu.get_barrier_semaphore()
    peers = [y_dev(step) for step in (1, -1, 2, -2)]
    peers += [x_dev(step) for step in (1, -1, 2)]
    peers += [z_dev(step) for step in range(1, n_z)]
    peers += [sibling, after, before]
    for peer in peers:
        pl.semaphore_signal(barrier, inc=1, device_id=peer, device_id_type=MESH)

    load_x = load(x_hbm, x_ref)
    load_gain = load(enc_gain_hbm, enc_gain_ref)
    load_conv = load(conv_hbm, conv_ref)
    load_w = [
        load(dw_hbm, dw_ref),
        load(gw_hbm.at[0:width], w_all.at[0, :, 0:128]),
        load(uw_hbm.at[0:width], w_all.at[0, :, 128:256]),
    ]
    load_tail = [
        load(widen_hbm, widen_ref),
        load(main_gain_hbm, main_gain_ref),
        load(gw_hbm.at[width : 2 * width], gw_tail),
        load(uw_hbm.at[width : 2 * width], uw_tail),
    ]

    load_marks.wait()
    marks = marks_ref[...].astype(F32)
    upper = (
        lax.broadcasted_iota(jnp.int32, (rows, rows), 0)
        <= lax.broadcasted_iota(jnp.int32, (rows, rows), 1)
    ).astype(F32).astype(BF16)
    running = dot(jnp.broadcast_to(marks, (16, rows)).astype(BF16), upper)
    lead = jnp.where(running == 0.0, 1.0, 0.0).astype(BF16)
    slot_ids = lax.broadcasted_iota(jnp.int32, (CAP, rows), 0).astype(F32)
    member = jnp.where(slot_ids == running[0:1] - 1.0, 1.0, 0.0)
    chosen = (member * marks).astype(BF16)
    last_slot = jnp.where(slot_ids[:, 0:1] == running[0:1, rows - 1 : rows] - 1.0, 1.0, 0.0)
    load_oc.wait()
    lead_out[...] = dot(lead, oc_ref[...])[0:8]

    pl.semaphore_wait(barrier, len(peers))

    halo_copy = send(x_hbm.at[rows - 16 : rows], halo, after)
    lead_copy = send(lead_out, lead_in, before)
    own_sums = dot(member.astype(BF16), oc_ref[...])

    for copy in load_w:
        copy.wait()
    w_all[0, :, 256:384] = dw_ref[...].astype(F32).T.astype(BF16)

    def w_rows(slot, part):
        start = pl.multiple_of(core * half + part * (half // 2), half // 2)
        return w_all.at[slot, pl.ds(start, half // 2)]

    w_right = [None, None]
    w_left = [None, None]

    def w_send(part):
        w_right[part] = send(w_rows(0, part), w_rows(1, part), x_dev(1))
        w_left[1 - part] = send(w_rows(0, 1 - part), w_rows(2, 1 - part), x_dev(-1))

    w_send(0)

    ring = {}

    def pass_on(which, side, direction, step):
        buffer = (in_all, cot_all)[which]
        lanes = slice(side * half, (side + 1) * half)
        here = Y_ROW[Y_ORDER.index(-direction * step)]
        there = Y_ROW[Y_ORDER.index(4 if step == 3 else -direction * (step + 1))]
        ring[which, side, direction, step] = send(
            buffer.at[here : here + CAP, lanes],
            buffer.at[there : there + CAP, lanes],
            y_dev(direction),
        )

    def first_hop(which):
        for side in (0, 1):
            for direction in (1, -1):
                pass_on(which, side, direction, 0)

    load_gain.wait()
    load_conv.wait()
    load_x.wait()
    enc_gain = as_row(enc_gain_ref[...])
    taps = [conv_ref[tap : tap + 1, :].astype(F32) for tap in range(KW)]
    for r in range(0, rows, CHUNK):
        value = x_ref[r : r + CHUNK].astype(F32)
        inverse = lax.rsqrt(jnp.mean(value * value, axis=1, keepdims=True) + EPS)
        inv_x[r : r + CHUNK] = inverse
        norm_x[16 + r : 16 + r + CHUNK] = value * inverse * enc_gain
    lead_copy.wait_recv()
    carried = lead_in[0:1] * (seq < n_seq - 1).astype(F32)
    cot_all[0:CAP] = (own_sums + last_slot * carried).astype(BF16)
    first_hop(1)

    halo_copy.wait_recv()
    value = halo[...].astype(F32) * (seq > 0).astype(F32)
    inverse = lax.rsqrt(jnp.mean(value * value, axis=1, keepdims=True) + EPS)
    norm_x[0:16] = value * inverse * enc_gain
    for r in range(0, rows, CHUNK):
        mixed = taps[0] * norm_x[16 + r : 16 + r + CHUNK]
        for tap in range(1, KW):
            mixed = mixed + taps[tap] * norm_x[16 + r - tap : 16 + r - tap + CHUNK]
        sigma = jax.nn.sigmoid(mixed)
        enc_out[r : r + CHUNK] = (x_ref[r : r + CHUNK].astype(F32) + mixed * sigma).astype(BF16)
        slope[r : r + CHUNK] = sigma * (1.0 + mixed * (1.0 - sigma))
    in_all[0:CAP] = dot(chosen, enc_out[...]).astype(BF16)
    first_hop(0)
    w_send(1)

    w_twin = []

    def swap(slot, part):
        w_twin.append(send(w_rows(slot, part), w_rows(slot, part), sibling))

    for copy in load_tail:
        copy.wait()
    widen = as_row(widen_ref[...])
    main_gain = as_row(main_gain_ref[...])
    gain_head = main_gain[:, 0:width]
    tail_vec = widen * main_gain[:, width : 2 * width]
    tail_square = jnp.sum(widen * widen, axis=1, keepdims=True)
    tail_b[...] = jnp.broadcast_to(tail_vec, (128, width)).T
    store(tail_b, tail_hbm)
    tail_gate = jnp.sum(gw_tail[...].astype(F32) * tail_b[...], axis=0, keepdims=True)
    tail_up = jnp.sum(uw_tail[...].astype(F32) * tail_b[...], axis=0, keepdims=True)
    tails[0, :, 0:128] = jnp.broadcast_to(tail_gate, (8, 128))
    tails[0, :, 128:256] = jnp.broadcast_to(tail_up, (8, 128))
    tail_copies = [
        send(tails.at[0], tails.at[1], x_dev(1)),
        send(tails.at[0], tails.at[2], x_dev(-1)),
        send(tails.at[0], tails.at[3], x_dev(2)),
    ]

    def relay(which, step):
        for side in (0, 1):
            for direction in (1, -1):
                ring[which, side, direction, step - 1].wait_recv()
                pass_on(which, side, direction, step)

    def relay_last(which):
        for side, direction in ((0, 1), (1, -1)):
            ring[which, side, direction, 2].wait_recv()
            pass_on(which, side, direction, 3)

    def wait_third(which):
        for side, direction in ((0, 1), (1, -1)):
            ring[which, 1 - side, direction, 2].wait_recv()

    def wait_last(which):
        for side, direction in ((0, 1), (1, -1)):
            ring[which, side, direction, 3].wait_recv()

    relay(1, 1)
    relay(0, 1)
    w_right[0].wait_recv()
    w_far_a = send(w_rows(1, 0), w_rows(3, 0), x_dev(1))
    w_left[1].wait_recv()
    w_far_b = send(w_rows(2, 1), w_rows(3, 1), x_dev(-1))
    swap(1, 0)
    swap(2, 1)
    for first, last in ((NEAR[1], FAR[0]), (FAR[1], ROWS)):
        count = last - first
        normed[first:last] = jnp.zeros((count, width), BF16)
        cot_all[first:last] = jnp.zeros((count, width), BF16)
        inv_all[first:last] = jnp.zeros((count, 1), F32)
        act_all[:, first:last] = jnp.zeros((LINE, count, 128), BF16)
        cots_all[:, first:last] = jnp.zeros((LINE, count, 256), BF16)
    relay(1, 2)
    relay(0, 2)
    w_right[1].wait_recv()
    swap(1, 1)
    w_left[0].wait_recv()
    swap(2, 0)

    def normalise(first, last):
        for r in range(first, last, CAP):
            head = in_all[r : r + CAP].astype(F32)
            square = jnp.sum(head * head, axis=1, keepdims=True) + tail_square
            inverse = lax.rsqrt(square / (2 * width) + EPS)
            inv_all[r : r + CAP] = inverse
            normed[r : r + CAP] = (head * inverse * gain_head).astype(BF16)
        tin_all[first:last] = jnp.zeros((last - first, 1), F32)

    def forward(first, last, low, high):
        def block(slot, carry):
            tail = tails[slot, 0:1, :]
            both = dot(normed[first:last], w_all[slot, :, 0:256]) + inv_all[first:last] * tail
            act_cot = dot(cot_all[first:last], w_all[slot, :, 256:384])
            gate, up = both[:, 0:128], both[:, 128:256]
            sigma = jax.nn.sigmoid(gate)
            swish = gate * sigma
            act_all[slot, first:last, :] = (swish * up).astype(BF16)
            gate_cot = (act_cot * up * sigma * (1.0 + gate * (1.0 - sigma))).astype(BF16)
            up_cot = (act_cot * swish).astype(BF16)
            cots_all[slot, first:last, 0:128] = gate_cot
            cots_all[slot, first:last, 128:256] = up_cot
            tin_all[first:last] += jnp.sum(
                gate_cot.astype(F32) * tail[:, 0:128] + up_cot.astype(F32) * tail[:, 128:256],
                axis=1,
                keepdims=True,
            )
            return carry

        lax.fori_loop(low, high, block, 0)

    def backward(first, last):
        def block(slot, carry):
            back[first:last] += dot_lanes(cots_all[slot, first:last], w_all[slot, :, 0:256])
            return carry

        back[first:last] = dot_lanes(cots_all[0, first:last], w_all[0, :, 0:256])
        lax.fori_loop(1, LINE, block, 0)
        for r in range(first, last, CAP):
            inverse = inv_all[r : r + CAP]
            unit = in_all[r : r + CAP].astype(F32) * inverse
            scaled = back[r : r + CAP] * gain_head
            inner = jnp.sum(scaled * unit, axis=1, keepdims=True) + tin_all[r : r + CAP] * inverse
            part_all[r : r + CAP] = (
                (scaled - unit * (inner / (2 * width))) * inverse
            ).astype(BF16)

    def part_of(step, lanes=slice(None)):
        row = Y_ROW[Y_ORDER.index(step)]
        return part_all.at[row : row + CAP, lanes]

    normalise(*NEAR)
    for copy in tail_copies + w_twin:
        copy.wait_recv()
    forward(*NEAR, 0, LINE - 1)
    relay_last(1)
    normed_t[0] = normed[0 : FAR[0]].T
    cot_t[0] = cot_all[0 : FAR[0]].T
    first_twins = len(w_twin)
    w_far_a.wait_recv()
    swap(3, 0)
    w_far_b.wait_recv()
    swap(3, 1)
    relay_last(0)
    for copy in w_twin[first_twins:]:
        copy.wait_recv()
    forward(*NEAR, LINE - 1, LINE)

    def near_product(slot, carry):
        g_acc[slot, :, 0:256] = dot(normed_t[0], cots_all[slot, 0 : FAR[0]])
        g_acc[slot, :, 256:384] = dot(cot_t[0], act_all[slot, 0 : FAR[0]])
        return carry

    lax.fori_loop(0, LINE, near_product, 0)

    wait_third(1)
    wait_third(0)
    normalise(*THIRD)
    forward(*THIRD, 0, LINE)
    wait_last(1)
    cot_t[1] = cot_all[FAR[0] : ROWS].T
    wait_last(0)
    normalise(*OPPOSITE)
    forward(*OPPOSITE, 0, LINE)
    normed_t[1] = normed[FAR[0] : ROWS].T

    def far_product(start, count, slot):
        some = pl.ds(pl.multiple_of(start, 128), count)
        wide = dot(normed_t[1, some], cots_all[slot, FAR[0] : ROWS])
        narrow = dot(cot_t[1, some], act_all[slot, FAR[0] : ROWS])
        return wide + g_acc[slot, some, 0:256], narrow + g_acc[slot, some, 256:384]

    def theirs(low, high):
        def block(slot, carry):
            wide, narrow = far_product((1 - core) * half + low, high - low, slot)
            g_out[slot, low:high, 0:256] = wide.astype(BF16)
            g_out[slot, low:high, 256:384] = narrow.astype(BF16)
            return carry

        lax.fori_loop(0, LINE, block, 0)

    def cut(part):
        return slice(PIECES[part], PIECES[part + 1])

    def halves(part):
        first, last = PIECES[part], PIECES[part + 1]
        mid = (first + last) // 2
        return slice(first, mid), slice(mid, last)

    def pair(part):
        return send(g_out.at[:, cut(part)], g_in.at[:, cut(part)], sibling)

    theirs(0, PIECES[1])
    pair_copies = [pair(0)]
    theirs(PIECES[1], half)
    pair_copies += [pair(part) for part in range(1, PARTS)]

    def ours(slot, carry):
        wide, narrow = far_product(core * half, half, slot)
        some = pl.ds(pl.multiple_of(core * half, half), half)
        g_acc[slot, some, 0:256] = wide
        g_acc[slot, some, 256:384] = narrow
        return carry

    lax.fori_loop(0, LINE, ours, 0)

    x_first, x_second, z_first, z_near, z_far, last_copies = ({} for _ in range(6))

    def rows_of(which, part):
        count = PIECES[part + 1] - PIECES[part]
        return pl.ds(pl.multiple_of(which * half + PIECES[part], 128), count)

    def own_rows(part):
        return rows_of(core, part)

    def x_start(part):
        pair_copies[part].wait_recv()

        def add(slot, carry):
            total = g_acc[slot, own_rows(part)] + g_in[slot, cut(part)].astype(F32)
            g_x[slot, cut(part)] = total.astype(BF16)
            return carry

        lax.fori_loop(1, LINE, add, 0)
        low, high = halves(part)
        x_first[part] = (
            send(g_x.at[3, low], x_opp.at[low], x_dev(1)),
            send(g_x.at[3, high], x_opp.at[high], x_dev(-1)),
            send(g_x.at[2, high], x_in.at[0, high], x_dev(1)),
            send(g_x.at[1, low], x_in.at[1, low], x_dev(-1)),
        )

    def x_relay(part):
        low, high = halves(part)
        x_first[part][0].wait_recv()
        g_x[2, low] = (g_x[2, low].astype(F32) + x_opp[low].astype(F32)).astype(BF16)
        right = send(g_x.at[2, low], x_in.at[0, low], x_dev(1))
        x_first[part][1].wait_recv()
        g_x[1, high] = (g_x[1, high].astype(F32) + x_opp[high].astype(F32)).astype(BF16)
        left = send(g_x.at[1, high], x_in.at[1, high], x_dev(-1))
        x_second[part] = (right, left)

    def z_cut(part, step, base=0):
        count = (PIECES[part + 1] - PIECES[part]) // n_z
        start = base + PIECES[part] + lax.rem(z + step + n_z, n_z) * count
        return pl.ds(pl.multiple_of(start, 16), count)

    def z_slot(part):
        return slice(PIECES[part] // n_z, PIECES[part + 1] // n_z)

    def z_start(part):
        for copy in x_first[part][2:] + x_second[part]:
            copy.wait_recv()
        h_all[cut(part)] = (
            g_acc[0, own_rows(part)]
            + g_in[0, cut(part)].astype(F32)
            + x_in[0, cut(part)].astype(F32)
            + x_in[1, cut(part)].astype(F32)
        ).astype(BF16)
        z_first[part] = [
            send(h_all.at[z_cut(part, step)], z_in.at[index, z_slot(part)], z_dev(step))
            for index, step in enumerate((4, 3, -3, 2, -2, 1, -1))
        ]

    def z_final(part, step):
        return z_cut(part, step, core * half)

    def z_sum(part):
        total = h_all[z_cut(part, 0)].astype(F32)
        for index, copy in enumerate(z_first[part]):
            copy.wait_recv()
            total = total + z_in[index, z_slot(part)].astype(F32)
        final[z_final(part, 0)] = total.astype(BF16)
        mine = final.at[z_final(part, 0)]
        steps = (2, -2, 1, -1) if part < PARTS - 1 else (4, 3, -3, 2, -2, 1, -1)
        z_near[part] = [send(mine, mine, z_dev(step)) for step in steps]

    def z_spread(part):
        copies = []
        for side, step in ((0, 1), (1, -1)):
            z_near[part][side].wait_recv()
            theirs = final.at[z_final(part, -2 * step)]
            copies.append(send(theirs, theirs, z_dev(step)))
            if side == (0 if part == 1 else 1):
                copies.append(send(theirs, theirs, z_dev(2 * step)))
        z_far[part] = copies

    def z_end(part):
        waits = z_near[part][2:] + z_far[part] if part < PARTS - 1 else z_near[part]
        for copy in waits:
            copy.wait_recv()
        mine = final.at[own_rows(part)]
        last_copies[part] = send(mine, mine, sibling)

    x_start(0)
    backward(*NEAR)
    x_start(1)
    y_copies = [
        send(part_of(1), y_in.at[0], y_dev(1)),
        send(part_of(-1), y_in.at[1], y_dev(-1)),
    ]
    x_relay(0)
    backward(*FAR)
    x_start(2)
    y_relays = [
        send(part_of(3), y_relay.at[0], y_dev(1)),
        send(part_of(-3), y_relay.at[1], y_dev(-1)),
        send(part_of(4, slice(0, half)), y_cross.at[0], y_dev(2)),
        send(part_of(4, slice(half, width)), y_cross.at[1], y_dev(-2)),
    ]
    x_relay(1)

    def tail_rows(slot, carry):
        row = jnp.sum(cots_all[slot].astype(F32) * inv_all[...], axis=0, keepdims=True)
        v_out[slot] = jnp.broadcast_to(row, (8, 256))
        return carry

    lax.fori_loop(0, LINE, tail_rows, 0)
    v_copies = [
        send(v_out.at[1], v_in.at[0], x_dev(-1)),
        send(v_out.at[2], v_in.at[1], x_dev(1)),
        send(v_out.at[3], v_in.at[2], x_dev(2)),
    ]
    x_relay(2)
    z_start(0)

    for copy in v_copies:
        copy.wait_recv()
    v_pair[...] = v_out[0] + v_in[0] + v_in[1] + v_in[2]
    v_swap = send(v_pair, v_sib, sibling)

    z_start(1)
    v_swap.wait_recv()
    v_all[z] = v_pair[...] + v_sib[...]
    v_spread = [send(v_all.at[z], v_all.at[z], z_dev(step)) for step in range(1, n_z)]

    for copy in y_relays:
        copy.wait_recv()
    for side, step in ((0, 2), (1, -2)):
        row = Y_ROW[Y_ORDER.index(step)]
        total = part_all[row : row + CAP].astype(F32) + y_relay[side].astype(F32)
        lanes = slice(side * half, (side + 1) * half)
        other = slice((1 - side) * half, (2 - side) * half)
        y_mid[side, :, lanes] = (total[:, lanes] + y_cross[side].astype(F32)).astype(BF16)
        y_mid[side, :, other] = total[:, other].astype(BF16)
        y_copies.append(send(y_mid.at[side], y_in.at[2 + side], y_dev(step)))

    z_sum(0)
    z_start(2)
    z_spread(0)
    z_sum(1)
    z_sum(2)
    z_spread(1)
    early = len(started)

    for copy in y_copies:
        copy.wait_recv()
    widen_cot = part_all[0:CAP].astype(F32)
    for index in range(4):
        widen_cot = widen_cot + y_in[index].astype(F32)
    spread = dot_rows(chosen, cot_all[0:CAP]) + dot_rows(chosen, widen_cot.astype(BF16))
    ecot[...] = oc_ref[...].astype(F32) + spread
    for r in range(0, rows, CHUNK):
        g_mix[r : r + CHUNK] = ecot[r : r + CHUNK] * slope[r : r + CHUNK]
    edge_copy = send(g_mix.at[0:8], edge, before)

    z_end(0)

    edge_copy.wait_recv()
    g_mix[rows : rows + 8] = edge[...] * (seq < n_seq - 1).astype(F32)
    for r in range(0, rows, CHUNK):
        grad = taps[0] * g_mix[r : r + CHUNK]
        for tap in range(1, KW):
            grad = grad + taps[tap] * g_mix[r + tap : r + tap + CHUNK]
        grad = grad * enc_gain
        value = x_ref[r : r + CHUNK].astype(F32)
        inverse = inv_x[r : r + CHUNK]
        inner = jnp.mean(grad * value, axis=1, keepdims=True) * (inverse * inverse)
        bg_ref[r : r + CHUNK] = (
            ecot[r : r + CHUNK] + (grad - value * inner) * inverse
        ).astype(BF16)
    store(bg_ref, bg_hbm)

    for copy in v_spread:
        copy.wait_recv()
    v_total = v_all[0]
    for chip in range(1, n_z):
        v_total = v_total + v_all[chip]
    v_ref[...] = v_total
    store(v_ref, v_hbm)

    def store_rows(which, part):
        store(final.at[rows_of(which, part)], final_hbm.at[rows_of(which, part)])

    def store_theirs(part):
        last_copies[part].wait_recv()
        store_rows(1 - core, part)

    store_rows(core, 0)
    z_end(1)
    store_rows(core, 1)
    store_theirs(0)
    for copy in started[:early]:
        copy.wait_send()
    z_end(2)
    store_rows(core, 2)
    store_theirs(1)
    store_theirs(2)
    for copy in started[early:]:
        copy.wait_send()
    for copy in stores:
        copy.wait()


def finish(
    bg_hbm, final_hbm, tail_hbm, v_hbm, bg_out, gg_out, ug_out, dg_out, bg, final, tail_b, v_ref, gg, ug, dg, sems
):
    width = final.shape[0]
    copies = []

    def copy(source, target):
        step = pltpu.make_async_copy(source, target, sems.at[len(copies)])
        step.start()
        copies.append(step)
        return step

    load_tail = copy(tail_hbm, tail_b)
    load_v = copy(v_hbm, v_ref)
    load_final = copy(final_hbm, final)
    load_bg = copy(bg_hbm, bg)
    head, tail = slice(0, width), slice(width, 2 * width)
    load_tail.wait()
    load_v.wait()
    gg[tail] = tail_b[...] * v_ref[0:1, 0:128]
    copy(gg.at[tail], gg_out.at[tail])
    ug[tail] = tail_b[...] * v_ref[0:1, 128:256]
    copy(ug.at[tail], ug_out.at[tail])
    load_final.wait()
    gg[head] = final[:, 0:128].astype(F32)
    copy(gg.at[head], gg_out.at[head])
    ug[head] = final[:, 128:256].astype(F32)
    copy(ug.at[head], ug_out.at[head])
    load_bg.wait()
    copy(bg, bg_out)
    dg[...] = final[:, 256:384].astype(F32).T
    copy(dg, dg_out)
    for step in copies[4:]:
        step.wait()


def body(
    bytes_in,
    flags,
    enc_gain,
    conv_weight,
    widen,
    main_gain,
    gate_weight,
    up_weight,
    down_weight,
    out_cot,
):
    rows, width = bytes_in.shape[1:]
    n_y = lax.axis_size("seq") // LINE
    n_z = lax.axis_size("dp") // 2
    assert n_y == len(Y_ORDER)
    half = width // 2
    hbm = pl.BlockSpec(memory_space=pltpu.HBM)
    scratch = [
        ((rows, width), BF16),
        ((width, 384), BF16),
        ((width, 128), F32),
        ((8, 256), F32),
        ((rows, width), BF16),
        ((1, rows), jnp.int32),
        ((8, width // 8), BF16),
        ((KW, width), BF16),
        ((8, width // 8), BF16),
        ((16, width // 8), BF16),
        ((width, 128), BF16),
        ((width, 128), BF16),
        ((128, width), BF16),
        ((rows, width), BF16),
        ((LINE, width, 384), BF16),
        ((LINE, 8, 256), F32),
        ((16, width), BF16),
        ((8, width), F32),
        ((8, width), F32),
        ((rows + 16, width), F32),
        ((rows, 1), F32),
        ((rows, width), BF16),
        ((rows, width), F32),
        ((ROWS, width), BF16),
        ((ROWS, width), BF16),
        ((ROWS, width), BF16),
        ((2, width, ROWS // 2), BF16),
        ((2, width, ROWS // 2), BF16),
        ((ROWS, 1), F32),
        ((ROWS, 1), F32),
        ((LINE, ROWS, 128), BF16),
        ((LINE, ROWS, 256), BF16),
        ((ROWS, width), F32),
        ((ROWS, width), BF16),
        ((4, CAP, width), BF16),
        ((2, CAP, width), BF16),
        ((2, CAP, half), BF16),
        ((2, CAP, width), BF16),
        ((LINE, 8, 256), F32),
        ((LINE - 1, 8, 256), F32),
        ((8, 256), F32),
        ((8, 256), F32),
        ((n_z, 8, 256), F32),
        ((LINE, width, 384), F32),
        ((LINE, half, 384), BF16),
        ((LINE, half, 384), BF16),
        ((LINE, half, 384), BF16),
        ((half, 384), BF16),
        ((2, half, 384), BF16),
        ((half, 384), BF16),
        ((n_z - 1, half // n_z, 384), BF16),
        ((rows, width), F32),
        ((rows + 8, width), F32),
        ((8, width), F32),
    ]
    sums = pl.pallas_call(
        kernel,
        out_shape=(
            jax.ShapeDtypeStruct((rows, width), BF16),
            jax.ShapeDtypeStruct((width, 384), BF16),
            jax.ShapeDtypeStruct((width, 128), F32),
            jax.ShapeDtypeStruct((8, 256), F32),
        ),
        in_specs=[hbm] * 10,
        out_specs=[hbm] * 4,
        scratch_shapes=[pltpu.VMEM(shape, kind) for shape, kind in scratch]
        + [
            pltpu.SemaphoreType.DMA((12,)),
            pltpu.SemaphoreType.DMA((9,)),
            pltpu.SemaphoreType.DMA((144,)),
            pltpu.SemaphoreType.DMA((144,)),
        ],
        compiler_params=pltpu.CompilerParams(
            collective_id=0, has_side_effects=True, vmem_limit_bytes=60 * 1024 * 1024
        ),
    )(
        bytes_in[0],
        flags,
        enc_gain.reshape(8, width // 8),
        conv_weight,
        widen.reshape(8, width // 8),
        main_gain.reshape(16, width // 8),
        gate_weight,
        up_weight,
        down_weight,
        out_cot[0],
    )
    outs = pl.pallas_call(
        finish,
        out_shape=(
            jax.ShapeDtypeStruct((rows, width), BF16),
            jax.ShapeDtypeStruct((2 * width, 128), F32),
            jax.ShapeDtypeStruct((2 * width, 128), F32),
            jax.ShapeDtypeStruct((128, width), F32),
        ),
        in_specs=[hbm] * 4,
        out_specs=[hbm] * 4,
        scratch_shapes=[
            pltpu.VMEM((rows, width), BF16),
            pltpu.VMEM((width, 384), BF16),
            pltpu.VMEM((width, 128), F32),
            pltpu.VMEM((8, 256), F32),
            pltpu.VMEM((2 * width, 128), F32),
            pltpu.VMEM((2 * width, 128), F32),
            pltpu.VMEM((128, width), F32),
            pltpu.SemaphoreType.DMA((10,)),
        ],
        compiler_params=pltpu.CompilerParams(vmem_limit_bytes=60 * 1024 * 1024),
    )(*sums)
    return (outs[0][None], outs[1], outs[2], outs[3])


def solution(mesh):
    in_specs = (
        P("dp", "seq", None),
        P("dp", "seq"),
        P(),
        P(),
        P(),
        P(),
        P(None, "seq"),
        P(None, "seq"),
        P("seq", None),
        P("dp", "seq", None),
    )
    out_specs = (P("dp", "seq", None), P(None, "seq"), P(None, "seq"), P("seq", None))
    return jax.shard_map(body, mesh=mesh, in_specs=in_specs, out_specs=out_specs, check_vma=False)
```
